32 devices in a mesh: seq: 8 (over y, x, core), tp: 4 (over z).
Axes of the slice: x: 2, y: 2, z: 4, core: 2. Of those that a mesh axis runs over, the one named last changes fastest.
Arguments:
- layer_input: bfloat16 [16384, 768], P(('seq', 'tp')), may hold values from -6 to 6
- clusters: int32 [16384, 12], P('seq', 'tp'), may hold values from 0 to 15, as said below
- document_lengths: int32 [8, 4], P('seq'), may hold values from 0 to 2048, as said below
- query_weight: bfloat16 [768, 768], P(None, 'tp'), may hold values from -0.3125 to 0.3125
- key_weight: bfloat16 [768, 768], P(None, 'tp'), may hold values from -0.3125 to 0.3125
- value_weight: bfloat16 [768, 768], P(None, 'tp'), may hold values from -0.21875 to 0.21875
- query_bias: float32 [768], P('tp'), may hold values from -1.2 to 1.2
- value_bias: float32 [768], P('tp'), may hold values from -1.2 to 1.2
- output_weight: bfloat16 [768, 768], P('tp'), may hold values from -0.875 to 0.875
- output_bias: float32 [768], replicated, may hold values from -1.2 to 1.2
- first_gain: float32 [768], replicated, may hold values from 0.5 to 1.5
- first_shift: float32 [768], replicated, may hold values from -1.2 to 1.2
- inner_weight: bfloat16 [768, 3072], P(None, 'tp'), may hold values from -0.21875 to 0.21875
- inner_bias: float32 [3072], P('tp'), may hold values from -1.2 to 1.2
- outer_weight: bfloat16 [3072, 768], P('tp'), may hold values from -0.15625 to 0.15625
- outer_bias: float32 [768], replicated, may hold values from -1.2 to 1.2
- second_gain: float32 [768], replicated, may hold values from 0.5 to 1.5
- second_shift: float32 [768], replicated, may hold values from -1.2 to 1.2
- cotangent: bfloat16 [16384, 768], P(('seq', 'tp')), may hold values from -6 to 6
Outputs:
- layer_output: bfloat16 [16384, 768], P(('seq', 'tp'))
- input_grad: float32 [16384, 768], P(('seq', 'tp'))
- grad_query_weight: float32 [768, 768], P(None, 'tp')
- grad_key_weight: float32 [768, 768], P(None, 'tp')
- grad_value_weight: float32 [768, 768], P(None, 'tp')
- grad_query_bias: float32 [768], P('tp')
- grad_value_bias: float32 [768], P('tp')
- grad_output_weight: float32 [768, 768], P('tp')
- grad_output_bias: float32 [768], replicated
- grad_first_gain: float32 [768], replicated
- grad_first_shift: float32 [768], replicated
- grad_inner_weight: float32 [768, 3072], P(None, 'tp')
- grad_inner_bias: float32 [3072], P('tp')
- grad_outer_weight: float32 [3072, 768], P('tp')
- grad_outer_bias: float32 [768], replicated
- grad_second_gain: float32 [768], replicated
- grad_second_shift: float32 [768], replicated
The draws below stay inside these ranges and needn't reach their ends.
Inputs may be any that keep to these rules, and one draw needn't show every extreme that they name: `document_lengths`: within each shard, the document spans of 128 * ceil(length / 128) slots, laid end to end from place 0, fill between half of the shard and all of it; a zero is an empty slot. One shard of every draw holds a single document of 2048 tokens. `clusters`: for each shard and head, every cluster number is held by exactly 128 tokens of the shard, and one cluster's tokens lie all within one document's padded span or all within the shard's unused tail.
All inputs are finite; a program needn't handle non-finite values.
Results may differ from the reference program's by a relative error of at most 0.015.
The reference program's roundings to bfloat16 on the way count: a program that leaves them out, or rounds other values in their place, can miss the bound.
Values may be sent and summed in bfloat16 or wider, within the bound.
A program may use at most 128 MiB of HBM per device.

```python
import jax
import jax.numpy as jnp
from jax import lax

D = 768
HEADS = 12
HEAD_DIM = 64
FF = 3072
TOK_DEV = 2048
CLUSTER = 128
DOCS = 4
SHARDS = 8
TOKENS = 16384


def layout(key):
    units = TOK_DEV // CLUSTER
    key_total, key_full, key_cuts, key_trim = jax.random.split(key, 4)
    total = jax.random.randint(key_total, (SHARDS,), (units + 1) // 2, units + 1)
    full = jax.random.randint(key_full, (), 0, SHARDS)
    cuts = jax.random.randint(key_cuts, (SHARDS, DOCS - 1), 0, units + 1)
    cuts = jnp.sort(jnp.minimum(cuts, total[:, None]), axis=1)
    bounds = jnp.concatenate([jnp.zeros((SHARDS, 1), jnp.int32), cuts, total[:, None]], axis=1)
    pieces = bounds[:, 1:] - bounds[:, :-1]
    single = (jnp.arange(DOCS, dtype=jnp.int32) == 0).astype(jnp.int32) * units
    chosen = jnp.arange(SHARDS, dtype=jnp.int32)[:, None] == full
    pieces = jnp.where(chosen, single[None, :], pieces)
    padded = pieces * CLUSTER
    trim = jax.random.randint(key_trim, (SHARDS, DOCS), 0, CLUSTER)
    trim = jnp.where(chosen, 0, trim)
    lengths = jnp.where(padded > 0, padded - trim, 0)
    return (padded.astype(jnp.int32), lengths.astype(jnp.int32))


def draw_document_lengths(key, part):
    padded, lengths = layout(key)
    return lengths


def draw_clusters(key, part):
    padded, lengths = layout(key)
    key = jax.random.fold_in(key, 7)
    ends = jnp.cumsum(padded, axis=1)
    place = jnp.arange(TOK_DEV, dtype=jnp.int32)
    span = jnp.sum((place[None, :, None] >= ends[:, None, :]).astype(jnp.int32), axis=2)
    noise = jax.random.randint(key, (SHARDS, HEADS, TOK_DEV), 0, 1024)
    score = (span[:, None, :] * 1024 + noise) * TOK_DEV + place[None, None, :]
    order = jnp.argsort(score, axis=2, stable=True)
    ranks = jnp.argsort(order, axis=2, stable=True)
    groups = (ranks // CLUSTER).astype(jnp.int32)
    return jnp.transpose(groups, (0, 2, 1)).reshape(SHARDS * TOK_DEV, HEADS)


def block_scale(key, dims, cuts, low, top_value):
    loudness = 1.0
    for dim, shards_of in cuts:
        heights = jax.random.uniform(jax.random.fold_in(jax.random.fold_in(key, 6), dim), (shards_of,), jnp.float32, low / len(cuts), top_value / len(cuts))
        loudness = loudness * jnp.repeat(jnp.exp(heights), dims[dim] // shards_of).reshape((-1,) + (1,) * (len(dims) - 1 - dim))
    return loudness


def normal_values(key, dims, scale, bound, shards=(), kind=jnp.bfloat16):
    level = block_scale(key, dims, shards, -0.22, 0.18) if shards else 1.0
    drawn = jax.random.normal(key, dims, jnp.float32) * scale * level
    return jnp.minimum(jnp.maximum(drawn, -bound), bound).astype(kind)


def setup_inputs(seed: int = 0) -> dict:
    arg_keys = jax.random.split(jax.random.key(seed), 20)
    return {
        "layer_input": normal_values(arg_keys[0], (TOKENS, D), 1.0, 6.0, ((0, 32),)),
        "clusters": draw_clusters(jax.random.fold_in(arg_keys[19], 71), 0),
        "document_lengths": draw_document_lengths(jax.random.fold_in(arg_keys[19], 71), 0),
        "query_weight": normal_values(arg_keys[3], (D, D), (D // 2) ** -0.5, 0.3125, ((1, 4),)),
        "key_weight": normal_values(arg_keys[4], (D, D), (D // 2) ** -0.5, 0.3125, ((1, 4),)),
        "value_weight": normal_values(arg_keys[5], (D, D), D ** -0.5, 0.21875, ((1, 4),)),
        "query_bias": normal_values(arg_keys[6], (D,), 0.3, 1.2, ((0, 4),), jnp.float32),
        "value_bias": normal_values(arg_keys[7], (D,), 0.3, 1.2, ((0, 4),), jnp.float32),
        "output_weight": normal_values(arg_keys[8], (D, D), (D // 16) ** -0.5, 0.875, ((0, 4),)),
        "output_bias": normal_values(arg_keys[9], (D,), 0.3, 1.2, (), jnp.float32),
        "first_gain": jnp.clip(1.0 + 0.1 * jax.random.normal(arg_keys[10], (D,), jnp.float32), 0.5, 1.5),
        "first_shift": normal_values(arg_keys[11], (D,), 0.3, 1.2, (), jnp.float32),
        "inner_weight": normal_values(arg_keys[12], (D, FF), D ** -0.5, 0.21875, ((1, 4),)),
        "inner_bias": normal_values(arg_keys[13], (FF,), 0.3, 1.2, ((0, 4),), jnp.float32),
        "outer_weight": normal_values(arg_keys[14], (FF, D), (FF // 2) ** -0.5, 0.15625, ((0, 4),)),
        "outer_bias": normal_values(arg_keys[15], (D,), 0.3, 1.2, (), jnp.float32),
        "second_gain": jnp.clip(1.0 + 0.1 * jax.random.normal(arg_keys[16], (D,), jnp.float32), 0.5, 1.5),
        "second_shift": normal_values(arg_keys[17], (D,), 0.3, 1.2, (), jnp.float32),
        "cotangent": normal_values(arg_keys[18], (TOKENS, D), 1.0, 6.0, ((0, 32),)),
    }


@jax.custom_vjp
def low(v):
    return lax.optimization_barrier(v.astype(jnp.bfloat16)).astype(jnp.float32)

@jax.custom_vjp
def low_back(v):
    return v

def low_keep(v):
    return (low(v), None)

def low_pass(kept, grad):
    return (grad,)

def back_keep(v):
    return (v, None)

def back_low(kept, grad):
    return (low(grad),)
low.defvjp(low_keep, low_pass)
low_back.defvjp(back_keep, back_low)
EPSILON = 1e-06
HIGH = lax.Precision.HIGHEST

def matmul(left, right):
    return jnp.dot(left, right, precision=HIGH, preferred_element_type=jnp.float32)

def layer_norm(rows, gain, shift):
    mean = lax.optimization_barrier(jnp.mean(rows, axis=-1, keepdims=True))
    centred = rows - mean
    spread = lax.optimization_barrier(jnp.mean(centred * centred, axis=-1, keepdims=True))
    return centred * lax.rsqrt(spread + EPSILON) * gain + shift

def real_tokens(lengths):
    padded = (lengths + CLUSTER - 1) // CLUSTER * CLUSTER
    ends = jnp.cumsum(padded)
    starts = ends - padded
    place = jnp.arange(TOK_DEV, dtype=jnp.int32)
    inside = (place[:, None] >= starts[None, :]) & (place[:, None] < starts[None, :] + lengths[None, :])
    return jnp.any(inside, axis=1).astype(jnp.float32)

def head_attention(query, keys, values, groups, valid):
    blocks = TOK_DEV // CLUSTER
    place = jnp.arange(TOK_DEV, dtype=jnp.int32)
    order = jnp.argsort(groups.astype(jnp.int32) * TOK_DEV + place).astype(jnp.int32)
    inverse = jnp.argsort(order).astype(jnp.int32)
    sorted_query = jnp.take(query, order, axis=0).reshape(blocks, CLUSTER, HEAD_DIM)
    sorted_keys = jnp.take(keys, order, axis=0).reshape(blocks, CLUSTER, HEAD_DIM)
    sorted_values = jnp.take(values, order, axis=0).reshape(blocks, CLUSTER, HEAD_DIM)
    keep = jnp.take(valid, order, axis=0).reshape(blocks, 1, CLUSTER)
    raw = jnp.einsum('cqd,ckd->cqk', sorted_query, sorted_keys, precision=HIGH)
    scores = low_back(raw) * HEAD_DIM ** (-0.5)
    masked = jnp.where(keep > 0.5, scores, -1e+30)
    top = lax.optimization_barrier(jnp.max(masked, axis=-1, keepdims=True))
    weights = jnp.exp(masked - top) * keep
    total = lax.optimization_barrier(jnp.sum(weights, axis=-1, keepdims=True))
    probs = low(weights / jnp.where(total > 0.5, total, 1.0))
    result = jnp.einsum('cqk,ckd->cqd', probs, sorted_values, precision=HIGH)
    return jnp.take(result.reshape(TOK_DEV, HEAD_DIM), inverse, axis=0)

def shard_layer(params, rows, groups, lengths):
    query_weight, key_weight, value_weight, query_bias, value_bias, output_weight, output_bias, first_gain, first_shift, inner_weight, inner_bias, outer_weight, outer_bias, second_gain, second_shift = params
    valid = real_tokens(lengths)
    query = low_back(low(matmul(rows, query_weight) + query_bias))
    keys = low_back(low(matmul(rows, key_weight)))
    values = low_back(low(matmul(rows, value_weight) + value_bias))
    split = lambda arr: arr.reshape(TOK_DEV, HEADS, HEAD_DIM)
    heads = jax.vmap(head_attention, in_axes=(1, 1, 1, 1, None), out_axes=1)(split(query), split(keys), split(values), groups, valid)
    mixed = low_back(low(heads.reshape(TOK_DEV, D)))
    attended = low_back(matmul(mixed, output_weight) + output_bias)
    first = layer_norm(rows + attended, first_gain, first_shift)
    inner = low_back(matmul(low(first), inner_weight) + inner_bias)
    activated = low(jax.nn.gelu(inner, approximate=False))
    branch = low_back(matmul(activated, outer_weight) + outer_bias)
    return layer_norm(first + branch, second_gain, second_shift)

def reference(layer_input, clusters, document_lengths, query_weight, key_weight, value_weight, query_bias, value_bias, output_weight, output_bias, first_gain, first_shift, inner_weight, inner_bias, outer_weight, outer_bias, second_gain, second_shift, cotangent):
    params = tuple((arr.astype(jnp.float32) for arr in (query_weight, key_weight, value_weight, query_bias, value_bias, output_weight, output_bias, first_gain, first_shift, inner_weight, inner_bias, outer_weight, outer_bias, second_gain, second_shift)))
    rows = layer_input.astype(jnp.float32).reshape(SHARDS, TOK_DEV, D)
    groups = clusters.reshape(SHARDS, TOK_DEV, HEADS)

    def forward(weights, inputs):
        step = jax.checkpoint(shard_layer)
        return lax.map(lambda item: step(weights, item[0], item[1], item[2]), (inputs, groups, document_lengths))
    outputs, pullback = jax.vjp(forward, params, rows)
    grads, grad_rows = pullback(cotangent.astype(jnp.float32).reshape(SHARDS, TOK_DEV, D))
    return (outputs.reshape(TOKENS, D).astype(jnp.bfloat16), grad_rows.reshape(TOKENS, D), grads[0], grads[1], grads[2], grads[3], grads[4], grads[5], grads[6], grads[7], grads[8], grads[9], grads[10], grads[11], grads[12], grads[13], grads[14])
```

```python
import functools
import jax
import jax.numpy as jnp
from jax import lax
from jax.experimental import pallas as pl
from jax.experimental.pallas import tpu as pltpu
from jax.sharding import PartitionSpec as P

MESH = pl.DeviceIdType.MESH
HEAD_DIM = 64
CLUSTER = 128
TOK = 2048
QUARTER = 512
D = 768
BLOCKS = TOK // CLUSTER
GROUP = 192
CHUNK = 256
CHUNKS = QUARTER // CHUNK
K_ROWS, Q_ROWS, V_ROWS, AUG = 0, 80, 160, 224
bf16, f32 = jnp.bfloat16, jnp.float32


def nn(a, b):
    return lax.dot_general(a, b, (((1,), (0,)), ((), ())), preferred_element_type=f32)


def nt(a, b):
    return lax.dot_general(a, b, (((1,), (1,)), ((), ())), preferred_element_type=f32)


def tn(a, b):
    return lax.dot_general(a, b, (((0,), (0,)), ((), ())), preferred_element_type=f32)


def remote(src, dst, send, recv, seq, tp):
    return pltpu.make_async_remote_copy(
        src_ref=src, dst_ref=dst, send_sem=send, recv_sem=recv, device_id=(seq, tp), device_id_type=MESH
    )


def place():
    s, z = lax.axis_index("seq"), lax.axis_index("tp")
    return s, z, s // 2, s % 2


def greet(columns):
    s, z, c, k = place()
    barrier = pltpu.get_barrier_semaphore()
    for step in range(1, 8):
        other = (k * 4 + z + step) % 8
        pl.semaphore_signal(barrier, inc=1, device_id=(2 * c + other // 4, other % 4), device_id_type=MESH)

    @pl.loop(1, columns)
    def _(step):
        pl.semaphore_signal(barrier, inc=1, device_id=(2 * ((c + step) % columns) + k, z), device_id_type=MESH)

    pl.semaphore_wait(barrier, 7 + columns - 1)


def rows_at(start, size, multiple):
    return pl.ds(pl.multiple_of(start, multiple), size)


def attend_forward(
    columns, x_ref, cl_ref, wt_ref, bias_ref, wpack_ref, cot_in, ib_in,
    xg_out, wf_ref, srt_out, share_out, mixed_ref, slot_ref, wg_ref, cot_ref, ib_ref,
    xg, cl, bias, qt, srt, share, table, onehot, rt, mx,
    x_send, x_recv, fwd_send, core_send, cl_sem, q_send, q_recv, b_sem, w1_send, w1_recv, w2_send, w2_recv, w3_send, w3_recv,
    m_send, m_recv, out_sem, loc_sem, cot_sem, ib_send, ib_recv,
):
    s, z, c, k = place()
    half = z // 2
    mate = s + 1 - 2 * k
    group = (z + 2 * k) % 4
    across = (z + 2) % 4
    inner, outer = 1 + k, 3 * k
    primary = k == half
    is_inner = z == inner
    prow = wpack_ref.shape[0] // 8
    crow = 4 * prow
    greet(columns)

    target = jnp.where(is_inner, outer, inner)

    def x_rows(q, j):
        return xg.at[rows_at(QUARTER * q + CHUNK * j, CHUNK, CHUNK)]

    def x_copy(j):
        return remote(x_ref.at[pl.ds(CHUNK * j, CHUNK)], x_rows(z, j), x_send.at[j], x_recv.at[z, j], s, target)

    x_copy(0).start()

    @pl.when(primary)
    def _():
        x_copy(1).start()

    cl_z = 2 * k + z % 2
    cl_k = ((z - cl_z + 4) % 4) // 2
    cl_self = (cl_z == z) & (cl_k == k)
    cl_copy = remote(cl_ref, cl, cl_sem.at[0], cl_sem.at[1], 2 * c + cl_k, cl_z)
    cl_local = pltpu.make_async_copy(cl_ref, cl, cl_sem.at[1])

    @pl.when(cl_self)
    def _():
        cl_local.start()

    @pl.when(jnp.logical_not(cl_self))
    def _():
        cl_copy.start()

    wrow = wt_ref.shape[0] // 4
    active = c < 4

    def wq_rows(piece):
        return wg_ref.at[rows_at(wrow * piece, wrow, 16)]

    w_copy = remote(wt_ref.at[rows_at(wrow * c, wrow, 16)], wq_rows(c), q_send.at[0], q_recv.at[c], s, across)

    def wq_copy(step):
        return remote(wq_rows(c), wq_rows(c), q_send.at[step], q_recv.at[c], 2 * ((c + step) % columns) + k, z)

    b_copy = remote(bias_ref, bias, b_sem.at[0], b_sem.at[1], s, across)
    b_local = pltpu.make_async_copy(bias_ref, bias, b_sem.at[1])
    w_local = pltpu.make_async_copy(wt_ref, wg_ref, q_send.at[0])

    @pl.when((k == 1) & active)
    def _():
        w_copy.start()

    @pl.when(k == 1)
    def _():
        b_copy.start()

    @pl.when(k == 0)
    def _():
        w_local.start()
        b_local.start()

    @pl.when(primary)
    def _():
        xg[rows_at(QUARTER * z, QUARTER, QUARTER), :] = x_ref[...]

    piece = 4 * k + c

    def wf_rows(plane, start, size):
        return wf_ref.at[plane, rows_at(start, size, 16)]

    w_own = pltpu.make_async_copy(wpack_ref, wf_ref.at[z], loc_sem.at[0])
    w_own.start()

    def plane_of(step):
        return [z + 1 - 2 * (z % 2), across, 3 - z][step - 1]

    def w1(step):
        return remote(
            wpack_ref.at[rows_at(prow * piece, prow, 16)], wf_rows(z, prow * piece, prow),
            w1_send.at[step - 1], w1_recv.at[step - 1], s, plane_of(step),
        )

    def w2(step, turn):
        rows = wf_rows(plane_of(step), prow * piece, prow)
        return remote(rows, rows, w2_send.at[step - 1, turn - 1], w2_recv.at[step - 1, c], 2 * ((c + turn) % columns) + k, z)

    def w3(step, core):
        rows = wf_rows(plane_of(step), crow * core, crow)
        return remote(rows, rows, w3_send.at[step - 1], w3_recv.at[step - 1], mate, z)

    cot_k, cot_z = z % 2, 2 * k + z // 2
    cot_self = (cot_k == k) & (cot_z == z)
    cot_copy = remote(cot_in, cot_ref, cot_sem.at[0], cot_sem.at[1], 2 * c + cot_k, cot_z)
    cot_local = pltpu.make_async_copy(cot_in, cot_ref, cot_sem.at[1])

    def ib_copy(step):
        return remote(ib_in, ib_ref.at[z], ib_send.at[step - 1], ib_recv.at[step - 1], s, plane_of(step))

    @pl.when(cl_self)
    def _():
        cl_local.wait()

    @pl.when(jnp.logical_not(cl_self))
    def _():
        cl_copy.wait()

    low_iota = lax.broadcasted_iota(jnp.int32, (CLUSTER, CLUSTER), 0)
    high_iota = lax.broadcasted_iota(jnp.int32, (CLUSTER, CLUSTER), 1)
    upper = jnp.concatenate([(low_iota < high_iota).astype(f32), jnp.ones((CLUSTER, CLUSTER), f32)], axis=1).astype(bf16)
    names = lax.broadcasted_iota(jnp.int32, (BLOCKS, CLUSTER), 0).astype(f32)
    base = jnp.zeros((3 * BLOCKS, CLUSTER), f32)
    slot_ref[...] = jnp.zeros_like(slot_ref)
    for b in range(BLOCKS):
        lanes = slice(CLUSTER * b, CLUSTER * (b + 1))
        block = cl[:, lanes].astype(f32)
        member = jnp.concatenate([(block[h : h + 1] == names).astype(f32) for h in range(3)], axis=0)
        counts = nn(member.astype(bf16), upper)
        seen = (counts[:, :CLUSTER] + base) * member
        base = base + counts[:, CLUSTER:]
        for h in range(3):
            rank = jnp.sum(seen[BLOCKS * h : BLOCKS * (h + 1)], axis=0, keepdims=True)
            slot_ref[h : h + 1, lanes] = rank
            slot_ref[h + 3 : h + 4, lanes] = block[h : h + 1]
    valid = cl[3:4, :].astype(f32)
    fill = lax.broadcasted_iota(jnp.int32, (16, TOK), 0) == 0
    mask_rows = jnp.where(fill, jnp.where(valid > 0.5, 0.0, -1e30), 0.0).astype(bf16)
    ones_rows = jnp.where(fill, 1.0, 0.0).astype(bf16)
    for h in range(3):
        qt[h, 64:80, :] = mask_rows
        qt[h, 144:160, :] = ones_rows

    @pl.when(jnp.logical_not(primary))
    def _():
        x_copy(0).wait_send()
        x_copy(1).start()

    @pl.when(k == 0)
    def _():
        w_local.wait()
        b_local.wait()

    @pl.when((k == 1) & active)
    def _():
        w_copy.wait()

        @pl.loop(1, columns)
        def _(step):
            wq_copy(step).start()

    @pl.when(k == 1)
    def _():
        b_copy.wait()
        for peer in range(4):
            @pl.when(c != peer)
            def _():
                remote(wq_rows(peer), wq_rows(peer), q_send.at[0], q_recv.at[peer], s, z).wait_recv()

    @pl.when((k == 1) & active)
    def _():
        @pl.loop(1, columns)
        def _(step):
            wq_copy(step).wait_send()

    bias_col = jnp.transpose(bias[...], (1, 0))[:, 0:1]

    zc = jnp.where(half == 1, 3 - z, z)
    for i in range(4):
        qc = [zc, 1 - zc, 2, 3][i]
        q = jnp.where(half == 1, 3 - qc, qc)
        for j in range(CHUNKS):
            arrived = remote(x_rows(q, j), x_rows(q, j), x_send.at[j], x_recv.at[q, j], s, z)
            if i == 0:
                @pl.when(jnp.logical_not(primary))
                def _():
                    arrived.wait_recv()
            else:
                arrived.wait_recv()
            if i >= 2:
                @pl.when(is_inner)
                def _():
                    remote(x_rows(q, j), x_rows(q, j), fwd_send.at[i - 2, j], x_recv.at[q, j], s, outer).start()

            @pl.when(primary)
            def _():
                remote(x_rows(q, j), x_rows(q, j), core_send.at[i, j], x_recv.at[q, j], mate, z).start()
        tokens = xg[rows_at(QUARTER * q, QUARTER, QUARTER), :]
        lanes = rows_at(QUARTER * q, QUARTER, QUARTER)
        for h in range(3):
            found = (nt(wg_ref[GROUP * h : GROUP * (h + 1), :], tokens) + bias_col[GROUP * h : GROUP * (h + 1)]).astype(bf16)
            qt[h, K_ROWS : K_ROWS + 64, lanes] = found[0:64]
            qt[h, Q_ROWS : Q_ROWS + 64, lanes] = found[64:128]
            qt[h, V_ROWS : V_ROWS + 64, lanes] = found[128:192]
    x_flush = pltpu.make_async_copy(xg, xg_out, out_sem.at[0])
    x_flush.start()

    @pl.when(active)
    def _():
        w1(1).start()
        w1(2).start()

    @pl.when(cot_self)
    def _():
        cot_local.start()

    @pl.when(jnp.logical_not(cot_self))
    def _():
        cot_copy.start()

    ib_ref[pl.ds(z, 1)] = ib_in[...][None]
    for step in range(1, 4):
        ib_copy(step).start()

    def spread(step):
        @pl.when(active)
        def _():
            rows = wf_rows(plane_of(step), prow * piece, prow)
            remote(rows, rows, w1_send.at[step - 1], w1_recv.at[step - 1], s, z).wait_recv()

            @pl.loop(1, columns)
            def _(turn):
                w2(step, turn).start()

    member_of = 2 * (z % 2) + k

    def mixed_at(h, grp):
        return mixed_ref.at[rows_at(GROUP * grp + HEAD_DIM * h, HEAD_DIM, HEAD_DIM)]

    rank_iota = lax.broadcasted_iota(jnp.int32, (CLUSTER, TOK), 0).astype(f32)

    def head(h, carry):
        rank_row = slot_ref[pl.ds(h, 1), :]
        name_row = slot_ref[pl.ds(h + 3, 1), :]
        onehot[...] = (rank_row == rank_iota).astype(f32).astype(bf16)

        def sort(b, carry):
            for e in range(2):
                name = (2 * b + e).astype(f32)
                table[rows_at(2 * CLUSTER * b + CLUSTER * e, CLUSTER, CLUSTER), :] = onehot[...] * (name_row == name).astype(f32).astype(bf16)
            rows = rows_at(2 * CLUSTER * b, 2 * CLUSTER, 2 * CLUSTER)
            srt[h, :, rows] = nt(qt[h], table[rows, :]).astype(bf16)
            return carry

        lax.fori_loop(0, BLOCKS // 2, sort, 0)

        def cluster(b, carry):
            for e in range(4):
                lanes = rows_at(CLUSTER * (4 * b + e), CLUSTER, CLUSTER)
                scores = tn(srt[h, K_ROWS : K_ROWS + 80, lanes], srt[h, Q_ROWS : Q_ROWS + 80, lanes]) * (HEAD_DIM ** (-0.5))
                top = jnp.maximum(jnp.max(scores, axis=0, keepdims=True), -1e20)
                weights = jnp.exp(scores - top)
                total = jnp.sum(weights, axis=0, keepdims=True)
                part = weights / jnp.where(total > 0.5, total, 1.0)
                share[h, 4 * b + e] = part
                rt[:, lanes] = nn(srt[h, V_ROWS : V_ROWS + 64, lanes], part.astype(bf16)).astype(bf16)
            return carry

        lax.fori_loop(0, BLOCKS // 4, cluster, 0)

        def back(d, carry):
            rows = rows_at(QUARTER * d, QUARTER, QUARTER)
            mx[h, d] = nn(rt[...], table[:, rows]).astype(bf16)

            @pl.when(d == member_of)
            def _():
                pltpu.make_async_copy(mx.at[h, d], mixed_at(h, group), m_recv.at[h, d]).start()

            @pl.when(d != member_of)
            def _():
                remote(
                    mx.at[h, d], mixed_at(h, group), m_send.at[h, d], m_recv.at[h, member_of],
                    2 * c + d % 2, 2 * half + d // 2,
                ).start()

            return carry

        lax.fori_loop(0, 4, back, 0)

        @pl.when(h == 0)
        def _():
            @pl.when(active)
            def _():
                w1(3).start()

            spread(1)

        @pl.when(h == 1)
        def _():
            spread(2)

        return carry

    lax.fori_loop(0, 3, head, 0)
    srt_flush = pltpu.make_async_copy(srt, srt_out, out_sem.at[1])
    share_flush = pltpu.make_async_copy(share, share_out, out_sem.at[2])
    srt_flush.start()
    share_flush.start()

    spread(3)

    def await_mixed(h, carry):
        def one(d, carry):
            grp = (2 * half + d // 2 + 2 * (d % 2)) % 4
            remote(mx.at[h, d], mixed_at(h, grp), m_send.at[h, d], m_recv.at[h, d], s, z).wait_recv()

            @pl.when(d != member_of)
            def _():
                remote(mx.at[h, d], mixed_at(h, grp), m_send.at[h, d], m_recv.at[h, d], s, z).wait_send()

            return carry

        return lax.fori_loop(0, 4, one, carry)

    lax.fori_loop(0, 3, await_mixed, 0)

    for j in range(CHUNKS):
        if j == 0:
            @pl.when(primary)
            def _():
                x_copy(0).wait_send()
        else:
            x_copy(j).wait_send()
        for i in range(4):
            @pl.when(primary)
            def _():
                remote(x_rows(0, j), x_rows(0, j), core_send.at[i, j], x_recv.at[0, j], mate, z).wait_send()
        for i in range(2):
            @pl.when(is_inner)
            def _():
                remote(x_rows(0, j), x_rows(0, j), fwd_send.at[i, j], x_recv.at[0, j], s, outer).wait_send()
    @pl.when(active)
    def _():
        for step in range(1, 4):
            w1(step).wait_send()

            @pl.loop(1, columns)
            def _(turn):
                w2(step, turn).wait_send()

    w_own.wait()
    for step in range(1, 4):
        for peer in range(4):
            rows = wf_rows(plane_of(step), prow * (4 * k + peer), prow)

            @pl.when(c != peer)
            def _():
                remote(rows, rows, w1_send.at[0], w2_recv.at[step - 1, peer], s, z).wait_recv()
        w3(step, k).start()
        ib_copy(step).wait_send()
        remote(ib_in, ib_ref.at[plane_of(step)], ib_send.at[step - 1], ib_recv.at[step - 1], s, z).wait_recv()

    @pl.when(cot_self)
    def _():
        cot_local.wait()

    @pl.when(jnp.logical_not(cot_self))
    def _():
        cot_copy.wait()

    for step in range(1, 4):
        w3(step, k).wait_send()
        w3(step, 1 - k).wait_recv()
    x_flush.wait()
    srt_flush.wait()
    share_flush.wait()


def forward_call(columns, x, cl, wt, bias, wpack, cot, ib):
    vmem = pl.BlockSpec(memory_space=pltpu.VMEM)
    anyspec = pl.BlockSpec(memory_space=pl.ANY)
    dma = pltpu.SemaphoreType.DMA
    return pl.pallas_call(
        functools.partial(attend_forward, columns),
        out_shape=[
            jax.ShapeDtypeStruct((TOK, D), bf16),
            jax.ShapeDtypeStruct((4,) + wpack.shape, bf16),
            jax.ShapeDtypeStruct((3, AUG, TOK), bf16),
            jax.ShapeDtypeStruct((3, BLOCKS, CLUSTER, CLUSTER), f32),
            jax.ShapeDtypeStruct((D, QUARTER), bf16),
            jax.ShapeDtypeStruct((8, TOK), f32),
            jax.ShapeDtypeStruct(wt.shape, bf16),
            jax.ShapeDtypeStruct(cot.shape, bf16),
            jax.ShapeDtypeStruct((4,) + ib.shape, f32),
        ],
        in_specs=[vmem, vmem, vmem, vmem, anyspec, vmem, vmem],
        out_specs=[anyspec, anyspec, anyspec, anyspec, vmem, vmem, vmem, vmem, vmem],
        scratch_shapes=[
            pltpu.VMEM((TOK, D), bf16),
            pltpu.VMEM(cl.shape, bf16),
            pltpu.VMEM(bias.shape, f32),
            pltpu.VMEM((3, AUG, TOK), bf16),
            pltpu.VMEM((3, AUG, TOK), bf16),
            pltpu.VMEM((3, BLOCKS, CLUSTER, CLUSTER), f32),
            pltpu.VMEM((TOK, TOK), bf16),
            pltpu.VMEM((CLUSTER, TOK), bf16),
            pltpu.VMEM((HEAD_DIM, TOK), bf16),
            pltpu.VMEM((3, 4, HEAD_DIM, QUARTER), bf16),
            dma((CHUNKS,)), dma((4, CHUNKS)), dma((2, CHUNKS)), dma((4, CHUNKS)),
            dma((2,)), dma((columns,)), dma((4,)), dma((2,)),
            dma((3,)), dma((3,)), dma((3, columns - 1)), dma((3, 4)), dma((3,)), dma((3,)),
            dma((3, 4)), dma((3, 4)), dma((3,)), dma((1,)), dma((2,)), dma((3,)), dma((3,)),
        ],
        compiler_params=pltpu.CompilerParams(collective_id=0, has_side_effects=True, vmem_limit_bytes=56 * 2**20),
    )(x, cl, wt, bias, wpack, cot, ib)


ROWS = 64


def backward(
    columns, reducers, tail, far,
    mixed, xg_in, wf_in, srt_in, share_in, slot_ref, wg_ref, cot, ib_ref, vec,
    lo_ref, dx_ref, fin, dw_ref, *rest,
):
    got2, stage = (rest[0], rest[1]) if far else (rest[0], None)
    (
    g, two, gb, gf, gsend, gm, dt,
    lo_src, dx_src, got1, got1s, got2s, got3, got3s, rd1, rd2, e1_got, e2_got,
    load_sem, gm_send, gm_recv, lo_sem, c1_send, c1_recv, c2_send, c2_recv, c3_send, c3_recv, c4_send, c4_recv, c5_send, c5_recv,
    d1_send, d1_recv, d2_send, d2_recv, d3_send, d3_recv, e1_send, e1_recv, e2_send, e2_recv, e3_send, e3_recv, e4_send, e4_recv,
    ) = rest[2 if far else 1 :]
    s, z, c, k = place()
    half, zb = z // 2, z % 2
    mate = s + 1 - 2 * k
    pair = z + 1 - 2 * zb
    across = (z + 2) % 4
    group = (z + 2 * k) % 4
    member = 2 * zb + k
    owner_seq, owner_tp = 2 * c + half, member
    own_home = (owner_seq == s) & (owner_tp == z)
    reduces = c < reducers
    scale = HEAD_DIM ** (-0.5)
    piece = D // reducers
    small = tail // 2
    spiece = small // reducers
    wide = [slice(256 * n, 256 * (n + 1)) for n in range(3)]

    loads = [pltpu.make_async_copy(wf_in.at[j], g.at[j], load_sem.at[j]) for j in range(4)]
    for one in loads:
        one.start()
    greet(columns)

    def plane_of(step):
        return [pair, across, 3 - z][step - 1]

    def bump(dst, src, rows, start=0):
        def body(t, carry):
            at = pl.ds(pl.multiple_of(start + 16 * t, 16), 16)
            from_ = pl.ds(pl.multiple_of(16 * t, 16), 16)
            dst[at, :] = (dst[at, :].astype(f32) + src[from_, :].astype(f32)).astype(bf16)
            return carry

        lax.fori_loop(0, rows // 16, body, 0)

    def core_copy(j):
        rows = rows_at(D * (1 - k), D, 16)
        return remote(g.at[j, rows], got1.at[j], c1_send.at[j], c1_recv.at[j], mate, z)

    def core_copy_small():
        rows = rows_at(2 * D + small * (1 - k), small, 16)
        return remote(g.at[:, rows], got1s, c1_send.at[4], c1_recv.at[4], mate, z)

    def column_copy(j, turn):
        dest = (c + turn) % columns
        if j < 4:
            rows = rows_at(D * k + piece * dest, piece, 16)
            return remote(g.at[j, rows], got2.at[j, turn - 1], c2_send.at[j, turn - 1], c2_recv.at[j, turn - 1], 2 * dest + k, z)
        rows = rows_at(2 * D + small * k + spiece * dest, spiece, 16)
        return remote(g.at[:, rows], got2s.at[turn - 1], c2_send.at[j, turn - 1], c2_recv.at[j, turn - 1], 2 * dest + k, z)

    def start_columns(j):
        @pl.loop(1, columns)
        def _(turn):
            @pl.when((c + turn) % columns < reducers)
            def _():
                column_copy(j, turn).start()

    def core_add(j):
        core_copy(j).wait()
        bump(g.at[j], got1.at[j], D, D * k)
        start_columns(j)

    def core_add_small():
        core_copy_small().wait()

        def one(j, carry):
            bump(g.at[j], got1s.at[j], small, 2 * D + small * k)
            return carry

        lax.fori_loop(0, 4, one, 0)
        start_columns(4)

    mine = D * k + piece * c
    smine = 2 * D + small * k + spiece * c

    def column_add(j):
        @pl.when(reduces)
        def _():
            @pl.loop(1, columns)
            def _(turn):
                if j < 4:
                    column_copy(j, turn).wait_recv()
                    term = got2.at[j, turn - 1]
                    if far:
                        fetch = pltpu.make_async_copy(term, stage, load_sem.at[0])
                        fetch.start()
                        fetch.wait()
                        term = stage
                    bump(g.at[j], term, piece, mine)
                else:
                    column_copy(j, turn).wait_recv()

                    def one(i, carry):
                        bump(g.at[i], got2s.at[turn - 1, i], spiece, smine)
                        return carry

                    lax.fori_loop(0, 4, one, 0)

    def plane_copy(part, step):
        rows = rows_at(mine if part == 0 else smine, piece if part == 0 else spiece, 16)
        got = got3 if part == 0 else got3s
        return remote(g.at[plane_of(step), rows], got.at[step - 1], c3_send.at[part, step - 1], c3_recv.at[part, step - 1], s, plane_of(step))

    def start_planes(part):
        @pl.when(reduces)
        def _():
            for step in range(1, 4):
                plane_copy(part, step).start()

    def final_rows(part, column, core):
        base, size = (D * core + piece * column, piece) if part == 0 else (2 * D + small * core + spiece * column, spiece)
        return fin.at[rows_at(base, size, 16)]

    def final_copy(part, turn):
        rows = final_rows(part, c, k)
        return remote(rows, rows, c4_send.at[part, turn - 1], c4_recv.at[part, c], 2 * ((c + turn) % columns) + k, z)

    def finish_planes(part):
        start, size = (mine, piece) if part == 0 else (smine, spiece)
        got = got3 if part == 0 else got3s

        @pl.when(reduces)
        def _():
            for step in range(1, 4):
                plane_copy(part, step).wait_recv()

            def body(t, carry):
                at = pl.ds(pl.multiple_of(start + 16 * t, 16), 16)
                from_ = pl.ds(pl.multiple_of(16 * t, 16), 16)
                total = g[z, at, :].astype(f32)
                for step in range(3):
                    total += got[step, from_, :].astype(f32)
                fin[at, :] = total.astype(bf16)
                return carry

            lax.fori_loop(0, size // 16, body, 0)

            @pl.loop(1, columns)
            def _(turn):
                final_copy(part, turn).start()

    def mate_copy(part, core):
        base, size = (D * core, D) if part == 0 else (2 * D + small * core, small)
        rows = fin.at[rows_at(base, size, 16)]
        return remote(rows, rows, c5_send.at[part], c5_recv.at[part], mate, z)

    def spread_final(part):
        for peer in range(reducers):
            @pl.when(c != peer)
            def _():
                rows = final_rows(part, peer, k)
                remote(rows, rows, c4_send.at[part, 0], c4_recv.at[part, peer], s, z).wait_recv()
        mate_copy(part, k).start()

    lo_copy = remote(lo_src, lo_ref, lo_sem.at[0], lo_sem.at[1], owner_seq, owner_tp)
    lo_local = pltpu.make_async_copy(lo_src, lo_ref, lo_sem.at[1])

    def gm_copy(q):
        home_z = 2 * half + q % 2
        home_k = ((q - home_z + 4) % 4) // 2
        return remote(gsend.at[q], gm.at[:, rows_at(QUARTER * member, QUARTER, QUARTER)], gm_send.at[q], gm_recv.at[member], 2 * c + home_k, home_z)

    dwb = got1.at[3, 0 : dw_ref.shape[0]]
    dxp = [got1.at[i, 0:QUARTER] for i in range(3)]
    wrow = dwb.shape[0] // reducers

    def dw_rows(ref, part):
        return ref.at[rows_at(wrow * part, wrow, 16)]

    def e1(turn):
        dest = (c + turn) % columns
        return remote(dw_rows(dwb, dest), e1_got.at[turn - 1], e1_send.at[turn - 1], e1_recv.at[turn - 1], 2 * dest + k, z)

    def feed_forward(x_own, mixt, norm, rstd, low, turned, act, slope):
        x_load = pltpu.make_async_copy(xg_in.at[rows_at(QUARTER * member, QUARTER, QUARTER)], x_own, load_sem.at[4])
        x_load.start()
        for one in loads:
            one.wait()
        x_load.wait()
        for q in range(4):
            mixt[q] = jnp.transpose(mixed[GROUP * q : GROUP * (q + 1), :], (1, 0))
        for n in wide:
            total = nn(mixt[0], g[0, 2 * D : 2 * D + GROUP, n])
            for q in range(1, 4):
                total += nn(mixt[q], g[q, 2 * D : 2 * D + GROUP, n])
            two[:, n] = total

        def mean_of(rows):
            return jnp.mean(rows, axis=-1, keepdims=True)

        def first_norm(t, carry):
            at = rows_at(ROWS * t, ROWS, ROWS)
            rows = two[at, :] + x_own[at, :].astype(f32) + vec[0:1, :]
            centred = rows - mean_of(rows)
            scaled = lax.rsqrt(mean_of(centred * centred) + 1e-6)
            normed = centred * scaled
            norm[at, :] = normed
            rstd[at, :] = jnp.broadcast_to(scaled, (ROWS, 128))
            low[at, :] = (normed * vec[1:2, :] + vec[2:3, :]).astype(bf16)
            return carry

        lax.fori_loop(0, QUARTER // ROWS, first_norm, 0)

        def forward_slice(j, carry):
            for n in wide:
                slope[j, :, n] = nn(low[...], g[j, 0:D, n]) + ib_ref[j, 0:1, n]

            def bend(t, carry):
                at = rows_at(ROWS * t, ROWS, ROWS)
                v = slope[j, at, :]
                phi = 0.5 + 0.5 * lax.erf(v * (0.5 ** 0.5))
                act[j, at, :] = (v * phi).astype(bf16)
                slope[j, at, :] = phi + v * (jnp.exp(v * v * -0.5) * 0.3989422804014327)
                return carry

            lax.fori_loop(0, QUARTER // ROWS, bend, 0)
            for n in wide:
                part = nn(act[j], g[j, D : 2 * D, n])

                @pl.when(j == 0)
                def _():
                    two[:, n] = part

                @pl.when(j > 0)
                def _():
                    two[:, n] += part

            return carry

        lax.fori_loop(0, 4, forward_slice, 0)

        zero_row = jnp.zeros((1, D), f32)

        def second_norm(t, carry):
            gain_sum, shift_sum, bias_sum = carry
            at = rows_at(ROWS * t, ROWS, ROWS)
            rows = norm[at, :] * vec[1:2, :] + vec[2:3, :] + two[at, :] + vec[3:4, :]
            centred = rows - mean_of(rows)
            scaled = lax.rsqrt(mean_of(centred * centred) + 1e-6)
            normed = centred * scaled
            lo_src[at, :] = (normed * vec[4:5, :] + vec[5:6, :]).astype(bf16)
            up = cot[at, :].astype(f32)
            e = up * vec[4:5, :]
            grad = (e - mean_of(e) - normed * mean_of(e * normed)) * scaled
            two[at, :] = grad
            grad_low = grad.astype(bf16)
            gb[at, :] = grad_low
            return (
                gain_sum + jnp.sum(up * normed, axis=0, keepdims=True),
                shift_sum + jnp.sum(up, axis=0, keepdims=True),
                bias_sum + jnp.sum(grad_low.astype(f32), axis=0, keepdims=True),
            )

        gain2, shift2, outer_bias = lax.fori_loop(0, QUARTER // ROWS, second_norm, (zero_row, zero_row, zero_row))

        @pl.when(own_home)
        def _():
            lo_local.start()

        @pl.when(jnp.logical_not(own_home))
        def _():
            lo_copy.start()

        turned[...] = jnp.transpose(low[...], (1, 0))
        gi = x_own
        inner_bias = []
        for j in range(4):
            sums = []
            for n in wide:
                found = (nt(gb[...], g[j, D + n.start : D + n.stop, :]) * slope[j, :, n]).astype(bf16)
                gi[:, n] = found
                sums.append(jnp.sum(found.astype(f32), axis=0, keepdims=True))
            inner_bias.append(jnp.concatenate(sums, axis=1))
            act_turned = jnp.transpose(act[j], (1, 0))
            for n in wide:
                g[j, D : 2 * D, n] = nn(act_turned, gb[:, n]).astype(bf16)
            for n in wide:
                part = nt(gi[...], g[j, n.start : n.stop, :])
                gf[:, n] = part if j == 0 else gf[:, n] + part
            for n in wide:
                g[j, 0:D, n] = nn(turned[...], gi[:, n]).astype(bf16)
            core_copy(j).start()
            if j > 0:
                core_add(j - 1)

        def first_back(t, carry):
            gain_sum, shift_sum, bias_sum = carry
            at = rows_at(ROWS * t, ROWS, ROWS)
            up = two[at, :] + gf[at, :]
            e = up * vec[1:2, :]
            normed = norm[at, :]
            grad = (e - mean_of(e) - normed * mean_of(e * normed)) * rstd[at, 0:1]
            two[at, :] = grad
            grad_low = grad.astype(bf16)
            gb[at, :] = grad_low
            return (
                gain_sum + jnp.sum(up * normed, axis=0, keepdims=True),
                shift_sum + jnp.sum(up, axis=0, keepdims=True),
                bias_sum + jnp.sum(grad_low.astype(f32), axis=0, keepdims=True),
            )

        gain1, shift1, output_bias = lax.fori_loop(0, QUARTER // ROWS, first_back, (zero_row, zero_row, zero_row))

        for q in range(4):
            gsend[q] = nt(g[q, 2 * D : 2 * D + GROUP, :], gb[...]).astype(bf16)

            @pl.when(group == q)
            def _():
                gm[:, rows_at(QUARTER * member, QUARTER, QUARTER)] = gsend[q]

            @pl.when(group != q)
            def _():
                gm_copy(q).start()

        head_rows = jnp.concatenate([gain2, shift2, outer_bias, gain1, shift1, output_bias], axis=0)
        for q in range(4):
            g[q, 2 * D : 2 * D + GROUP, :] = nn(mixed[GROUP * q : GROUP * (q + 1), :], gb[...]).astype(bf16)
            g[q, 2 * D + GROUP : 2 * D + GROUP + 16, :] = jnp.concatenate(
                [head_rows, inner_bias[q], jnp.zeros((9, D), f32)], axis=0
            ).astype(bf16)
        core_copy_small().start()
        core_add(3)

    pl.run_scoped(
        feed_forward,
        pltpu.VMEM((QUARTER, D), bf16), pltpu.VMEM((4, QUARTER, GROUP), bf16), pltpu.VMEM((QUARTER, D), f32), pltpu.VMEM((QUARTER, 128), f32),
        pltpu.VMEM((QUARTER, D), bf16), pltpu.VMEM((D, QUARTER), bf16), pltpu.VMEM((4, QUARTER, D), bf16), pltpu.VMEM((4, QUARTER, D), f32),
    )

    def attention_back(xg, srt, share, table, onehot, gs, ds):
        x_load = pltpu.make_async_copy(xg_in, xg, load_sem.at[4])
        srt_load = pltpu.make_async_copy(srt_in, srt, load_sem.at[5])
        share_load = pltpu.make_async_copy(share_in, share, load_sem.at[6])
        x_load.start()
        srt_load.start()
        share_load.start()
        for m in range(4):
            @pl.when(m != member)
            def _():
                rows = gm.at[:, QUARTER * m : QUARTER * (m + 1)]
                remote(rows, rows, gm_send.at[0], gm_recv.at[m], s, z).wait_recv()

        rank_iota = lax.broadcasted_iota(jnp.int32, (CLUSTER, TOK), 0).astype(f32)

        def head(h, carry):
            rank_row = slot_ref[pl.ds(h, 1), :]
            name_row = slot_ref[pl.ds(h + 3, 1), :]
            onehot[...] = (rank_row == rank_iota).astype(f32).astype(bf16)
            upper = gm[rows_at(HEAD_DIM * h, HEAD_DIM, HEAD_DIM), :]

            def sort(b, carry):
                for e in range(2):
                    name = (2 * b + e).astype(f32)
                    table[rows_at(2 * CLUSTER * b + CLUSTER * e, CLUSTER, CLUSTER), :] = onehot[...] * (name_row == name).astype(f32).astype(bf16)
                rows = rows_at(2 * CLUSTER * b, 2 * CLUSTER, 2 * CLUSTER)
                gs[:, rows] = nt(gm[rows_at(HEAD_DIM * h, HEAD_DIM, HEAD_DIM), :], table[rows, :]).astype(bf16)
                return carry

            lax.fori_loop(0, BLOCKS // 2, sort, 0)

            def cluster(b, carry):
                for e in range(4):
                    lanes = rows_at(CLUSTER * (4 * b + e), CLUSTER, CLUSTER)
                    part = share[h, 4 * b + e]
                    grad = gs[:, lanes]
                    grad_part = tn(srt[h, V_ROWS : V_ROWS + 64, lanes], grad)
                    inside = jnp.sum(grad_part * part, axis=0, keepdims=True)
                    grad_score = (part * (grad_part - inside)).astype(bf16)
                    ds[0:64, lanes] = (nt(srt[h, Q_ROWS : Q_ROWS + 64, lanes], grad_score) * scale).astype(bf16)
                    ds[64:128, lanes] = (nn(srt[h, K_ROWS : K_ROWS + 64, lanes], grad_score) * scale).astype(bf16)
                    ds[128:192, lanes] = nt(grad, part.astype(bf16)).astype(bf16)
                return carry

            lax.fori_loop(0, BLOCKS // 4, cluster, 0)

            def back(d, carry):
                rows = rows_at(QUARTER * d, QUARTER, QUARTER)
                dt[rows_at(GROUP * h, GROUP, GROUP), rows] = nn(ds[...], table[:, rows]).astype(bf16)
                return carry

            lax.fori_loop(0, 4, back, 0)

            @pl.when(h == 0)
            def _():
                core_add_small()

            return carry

        srt_load.wait()
        share_load.wait()
        lax.fori_loop(0, 3, head, 0)
        x_load.wait()

        for n in wide:
            dwb[0 : 3 * GROUP, n] = nn(dt[...], xg[:, n]).astype(bf16)
        ones = jnp.ones((16, TOK), bf16)
        dwb[3 * GROUP : 3 * GROUP + 16, 0 : 3 * GROUP] = nt(ones, dt[...]).astype(bf16)
        dwb[3 * GROUP : 3 * GROUP + 16, 3 * GROUP :] = jnp.zeros((16, D - 3 * GROUP), bf16)
        dwb[3 * GROUP + 16 :, :] = jnp.zeros((dwb.shape[0] - 3 * GROUP - 16, D), bf16)

        @pl.loop(1, columns)
        def _(turn):
            @pl.when((c + turn) % columns < reducers)
            def _():
                e1(turn).start()

    pl.run_scoped(
        attention_back,
        pltpu.VMEM((TOK, D), bf16), pltpu.VMEM((3, AUG, TOK), bf16), pltpu.VMEM((3, BLOCKS, CLUSTER, CLUSTER), f32),
        pltpu.VMEM((TOK, TOK), bf16), pltpu.VMEM((CLUSTER, TOK), bf16), pltpu.VMEM((HEAD_DIM, TOK), bf16), pltpu.VMEM((GROUP, TOK), bf16),
    )

    here = 2 * zb
    there = 2 * (1 - zb)

    def partial_rows(quarter, n):
        return tn(dt[:, rows_at(QUARTER * quarter, QUARTER, QUARTER)], wg_ref[:, n])

    def d1(i):
        return remote(dxp[i], rd1.at[i], d1_send.at[i], d1_recv.at[i], mate, z)

    def d2(i):
        rows = slice(256 * i, 256 * (i + 1))
        return remote(dxp[2].at[rows], rd2.at[rows], d2_send.at[i], d2_recv.at[i], s, pair)

    def d3(i):
        rows = slice(256 * i, 256 * (i + 1))
        return remote(dx_src.at[rows], dx_ref.at[rows], d3_send.at[i], d3_recv.at[i], owner_seq, owner_tp)

    def d3_local(i):
        rows = slice(256 * i, 256 * (i + 1))
        return pltpu.make_async_copy(dx_src.at[rows], dx_ref.at[rows], d3_recv.at[i])

    for n in wide:
        dxp[0][:, n] = partial_rows(there + 1 - k, n).astype(bf16)
    d1(0).start()
    for n in wide:
        gf[:, n] = partial_rows(there + k, n)
    d1(0).wait_recv()
    for i in range(2):
        def add_there(t, carry):
            at = rows_at(256 * i + 16 * t, 16, 16)
            dxp[2][at, :] = (gf[at, :] + rd1[0, at, :].astype(f32)).astype(bf16)
            return carry

        lax.fori_loop(0, 16, add_there, 0)
        d2(i).start()
    for n in wide:
        dxp[1][:, n] = partial_rows(here + 1 - k, n).astype(bf16)
    d1(1).start()
    for n in wide:
        two[:, n] += partial_rows(here + k, n)
    d1(1).wait_recv()

    for j in range(4):
        column_add(j)
    start_planes(0)
    column_add(4)
    start_planes(1)

    for i in range(2):
        d2(i).wait_recv()

        def add_here(t, carry):
            at = rows_at(256 * i + 16 * t, 16, 16)
            dx_src[at, :] = (two[at, :] + rd1[1, at, :].astype(f32) + rd2[at, :].astype(f32)).astype(bf16)
            return carry

        lax.fori_loop(0, 16, add_here, 0)

        @pl.when(own_home)
        def _():
            d3_local(i).start()

        @pl.when(jnp.logical_not(own_home))
        def _():
            d3(i).start()

    @pl.when(reduces)
    def _():
        @pl.loop(1, columns)
        def _(turn):
            e1(turn).wait_recv()
            bump(dwb, e1_got.at[turn - 1], wrow, wrow * c)

    e2 = remote(dw_rows(dwb, c), e2_got, e2_send.at[0], e2_recv.at[0], s - 1, across)

    def e3(turn):
        return remote(dw_rows(dw_ref, c), dw_rows(dw_ref, c), e3_send.at[turn - 1], e3_recv.at[c], 2 * ((c + turn) % columns) + k, z)

    e4 = remote(dw_ref, dw_ref, e4_send.at[0], e4_recv.at[0], mate, z)

    @pl.when(reduces & (k == 1))
    def _():
        e2.start()

    finish_planes(0)
    finish_planes(1)

    @pl.when(reduces & (k == 0))
    def _():
        remote(e2_got, e2_got, e2_send.at[0], e2_recv.at[0], s, z).wait_recv()

        def add_dw(t, carry):
            at = rows_at(wrow * c + 16 * t, 16, 16)
            from_ = rows_at(16 * t, 16, 16)
            dw_ref[at, :] = (dwb[at, :].astype(f32) + e2_got[from_, :].astype(f32)).astype(bf16)
            return carry

        lax.fori_loop(0, wrow // 16, add_dw, 0)

        @pl.loop(1, columns)
        def _(turn):
            e3(turn).start()

    spread_final(0)
    spread_final(1)

    @pl.when(k == 0)
    def _():
        for peer in range(reducers):
            @pl.when(c != peer)
            def _():
                remote(dw_rows(dw_ref, peer), dw_rows(dw_ref, peer), e3_send.at[0], e3_recv.at[peer], s, z).wait_recv()
        e4.start()
        e4.wait_send()

    @pl.when(k == 1)
    def _():
        e4.wait_recv()

    @pl.when(reduces & (k == 1))
    def _():
        e2.wait_send()

    @pl.when(reduces & (k == 0))
    def _():
        @pl.loop(1, columns)
        def _(turn):
            e3(turn).wait_send()

    @pl.loop(1, columns)
    def _(turn):
        @pl.when((c + turn) % columns < reducers)
        def _():
            e1(turn).wait_send()

        @pl.when((c + turn) % columns < reducers)
        def _():
            for j in range(5):
                column_copy(j, turn).wait_send()

    for part in range(2):
        @pl.when(reduces)
        def _():
            for step in range(1, 4):
                plane_copy(part, step).wait_send()

            @pl.loop(1, columns)
            def _(turn):
                final_copy(part, turn).wait_send()

        mate_copy(part, k).wait_send()
        mate_copy(part, 1 - k).wait_recv()

    @pl.when(own_home)
    def _():
        lo_local.wait()
        for i in range(2):
            d3_local(i).wait()

    @pl.when(jnp.logical_not(own_home))
    def _():
        lo_copy.wait()
        for i in range(2):
            d3(i).wait()

    for q in range(4):
        @pl.when(group != q)
        def _():
            gm_copy(q).wait_send()
    for i in range(2):
        d1(i).wait_send()
        d2(i).wait_send()


def backward_call(columns, reducers, tail, mixed, xg, wf, srt, share, slot, wg, cot, ib, vec):
    vmem = pl.BlockSpec(memory_space=pltpu.VMEM)
    anyspec = pl.BlockSpec(memory_space=pl.ANY)
    dma = pltpu.SemaphoreType.DMA
    rows = 2 * D + tail
    piece, spiece = D // reducers, tail // 2 // reducers
    turns = columns - 1
    wide = 16 * reducers * -(-(3 * GROUP + 16) // (16 * reducers))
    far = columns > 4
    low = lambda *shape: pltpu.VMEM(shape, bf16)
    full = lambda *shape: pltpu.VMEM(shape, f32)
    out = lambda *shape: jax.ShapeDtypeStruct(shape, bf16)
    terms = (4, turns, piece, D)
    return pl.pallas_call(
        functools.partial(backward, columns, reducers, tail, far),
        out_shape=[out(QUARTER, D), out(QUARTER, D), out(rows, D), out(wide, D)] + ([out(*terms)] if far else []),
        in_specs=[vmem, anyspec, anyspec, anyspec, anyspec, vmem, vmem, vmem, vmem, vmem],
        out_specs=[vmem, vmem, vmem, vmem] + ([anyspec] if far else []),
        scratch_shapes=[
            low(piece, D) if far else low(*terms),
            low(4, rows, D), full(QUARTER, D), low(QUARTER, D), full(QUARTER, D), low(4, GROUP, QUARTER), low(GROUP, TOK), low(3 * GROUP, TOK),
            low(QUARTER, D), low(QUARTER, D),
            low(4, D, D), low(4, tail // 2, D), low(turns, 4, spiece, D), low(3, piece, D), low(3, spiece, D),
            low(2, QUARTER, D), low(QUARTER, D), low(turns, wide // reducers, D), low(wide // reducers, D),
            dma((7,)), dma((4,)), dma((4,)), dma((2,)), dma((5,)), dma((5,)), dma((5, turns)), dma((5, turns)),
            dma((2, 3)), dma((2, 3)), dma((2, turns)), dma((2, reducers)), dma((2,)), dma((2,)),
            dma((2,)), dma((2,)), dma((2,)), dma((2,)), dma((2,)), dma((2,)),
            dma((turns,)), dma((turns,)), dma((1,)), dma((1,)), dma((turns,)), dma((reducers,)), dma((1,)), dma((1,)),
        ],
        compiler_params=pltpu.CompilerParams(collective_id=1, has_side_effects=True, vmem_limit_bytes=62 * 2**20),
    )(mixed, xg, wf, srt, share, slot, wg, cot, ib, vec)


def real_tokens(lengths):
    padded = (lengths + CLUSTER - 1) // CLUSTER * CLUSTER
    ends = jnp.cumsum(padded)
    starts = ends - padded
    spot = jnp.arange(TOK, dtype=jnp.int32)
    inside = (spot[:, None] >= starts[None, :]) & (spot[:, None] < starts[None, :] + lengths[None, :])
    return jnp.any(inside, axis=1).astype(bf16)


def shards(
    layer_input, clusters, document_lengths, query_weight, key_weight, value_weight, query_bias, value_bias, output_weight,
    output_bias, first_gain, first_shift, inner_weight, inner_bias, outer_weight, outer_bias, second_gain, second_shift, cotangent,
):
    columns = lax.axis_size("seq") // 2
    reducers = min(columns, 16)
    tail = 32 * reducers * -(-(GROUP + 16) // (32 * reducers))
    heads = lambda w: w.T.reshape(3, HEAD_DIM, D)
    valid = real_tokens(document_lengths[0])
    cl = jnp.concatenate([clusters.T.astype(bf16), valid[None], jnp.zeros((12, TOK), bf16)], axis=0)
    wt = jnp.stack([heads(key_weight), heads(query_weight), heads(value_weight)], axis=1).reshape(3 * GROUP, D)
    by_head = lambda b: b.reshape(3, HEAD_DIM)
    bias = jnp.stack([jnp.zeros((3, HEAD_DIM), f32), by_head(query_bias), by_head(value_bias)], axis=1).reshape(1, 3 * GROUP)
    bias = jnp.pad(bias, ((0, 7), (0, 64)))
    wpack = jnp.concatenate([inner_weight, outer_weight, output_weight, jnp.zeros((tail - GROUP, D), bf16)], axis=0)
    ib = jnp.pad(inner_bias[None], ((0, 7), (0, 0)))
    vec = jnp.stack([output_bias, first_gain, first_shift, outer_bias, second_gain, second_shift, output_bias, output_bias])
    xg, wf, srt, share, mixed, slot, wg, cot, ibg = forward_call(columns, layer_input, cl, wt, bias, wpack, cotangent, ib)
    lo, dx, fin, dw, *_ = backward_call(columns, reducers, tail, mixed, xg, wf, srt, share, slot, wg, cot, ibg, vec)
    fin = fin.astype(f32)
    dw = dw.astype(f32)
    kqv = dw[: 3 * GROUP].reshape(3, 3, HEAD_DIM, D)
    columns_of = lambda i: kqv[:, i].reshape(GROUP, D).T
    bias_rows = dw[3 * GROUP, : 3 * GROUP].reshape(3, 3, HEAD_DIM)
    row = 2 * D + GROUP
    return (
        lo,
        dx.astype(f32),
        columns_of(1),
        columns_of(0),
        columns_of(2),
        bias_rows[:, 1].reshape(GROUP),
        bias_rows[:, 2].reshape(GROUP),
        fin[2 * D : 2 * D + GROUP],
        fin[row + 5],
        fin[row + 3],
        fin[row + 4],
        fin[:D],
        fin[row + 6],
        fin[D : 2 * D],
        fin[row + 2],
        fin[row],
        fin[row + 1],
    )


def solution(mesh):
    rows, cols = P(("seq", "tp"), None), P(None, "tp")
    return jax.shard_map(
        shards,
        mesh=mesh,
        in_specs=(
            rows, P("seq", "tp"), P("seq", None), cols, cols, cols, P("tp"), P("tp"), P("tp", None), P(), P(), P(),
            cols, P("tp"), P("tp", None), P(), P(), P(), rows,
        ),
        out_specs=(
            rows, rows, cols, cols, cols, P("tp"), P("tp"), P("tp", None), P(), P(), P(), cols, P("tp"), P("tp", None), P(), P(), P(),
        ),
        check_vma=False,
    )
```

```python
import functools
import jax
import jax.numpy as jnp
from jax import lax
from jax.experimental import pallas as pl
from jax.experimental.pallas import tpu as pltpu
from jax.sharding import PartitionSpec as P

MESH = pl.DeviceIdType.MESH
HEAD_DIM = 64
CLUSTER = 128
TOK = 2048
QUARTER = 512
D = 768
BLOCKS = TOK // CLUSTER
GROUP = 192
CHUNK = 128
CHUNKS = QUARTER // CHUNK
ROWS = 64
K_ROWS, Q_ROWS, V_ROWS, AUG = 0, 80, 160, 224
bf16, f32 = jnp.bfloat16, jnp.float32


def nn(a, b):
    return lax.dot_general(a, b, (((1,), (0,)), ((), ())), preferred_element_type=f32)


def nt(a, b):
    return lax.dot_general(a, b, (((1,), (1,)), ((), ())), preferred_element_type=f32)


def tn(a, b):
    return lax.dot_general(a, b, (((0,), (0,)), ((), ())), preferred_element_type=f32)


def diagonal(a, b):
    blank = jnp.zeros_like(a)
    return jnp.concatenate([jnp.concatenate([a, blank], axis=1), jnp.concatenate([blank, b], axis=1)], axis=0)


def remote(src, dst, send, recv, seq, tp):
    return pltpu.make_async_remote_copy(
        src_ref=src, dst_ref=dst, send_sem=send, recv_sem=recv, device_id=(seq, tp), device_id_type=MESH
    )


def place():
    s, z = lax.axis_index("seq"), lax.axis_index("tp")
    return s, z, s // 2, s % 2


def greet(columns):
    s, z, c, k = place()
    barrier = pltpu.get_barrier_semaphore()
    for step in range(1, 8):
        other = (k * 4 + z + step) % 8
        pl.semaphore_signal(barrier, inc=1, device_id=(2 * c + other // 4, other % 4), device_id_type=MESH)

    @pl.loop(1, columns)
    def _(step):
        pl.semaphore_signal(barrier, inc=1, device_id=(2 * ((c + step) % columns) + k, z), device_id_type=MESH)

    pl.semaphore_wait(barrier, 7 + columns - 1)


def rows_at(start, size, multiple):
    return pl.ds(pl.multiple_of(start, multiple), size)


def layer(
    columns, reducers, tail, far,
    x_in, groups_in, lengths, query_in, key_in, value_in, inner_in, outer_in, output_in, cot_in, vectors,
    lo_ref, dx_ref, fin_inner, fin_outer, fin_tail, dw_ref, *rest,
):
    got2, got2s, stage, stages = rest[:4] if far else (rest[0], rest[1], None, None)
    (
        g, xg, srt, share, wg, cl, slot_ref, bias, mixed, cot, ib_ref, two, gf, gb, gsend, gm, lo_src, dx_src,
        got1, got1s, got3, got3s, rd1, rd2, e1_got, e2_got, done, dones, cl_in, wt_ref, bias_in, ib_in,
        load_sem, x_send, x_recv, fwd_send, core_send, cl_sem, q_send, q_recv, b_sem, cot_sem, ib_send, ib_recv,
        w1_send, w1_recv, w2_send, w2_recv, w3_send, w3_recv, m_send, m_recv, gm_send, gm_recv, lo_sem,
        c1_send, c1_recv, c2_send, c2_recv, c3_send, c3_recv, c4_send, c4_recv, c5_send, c5_recv,
        d1_send, d1_recv, d2_send, d2_recv, d3_send, d3_recv, e1_send, e1_recv, e2_send, e2_recv, e3_send, e3_recv, e4_send, e4_recv,
    ) = rest[4 if far else 2 :]
    s, z, c, k = place()
    half, zb = z // 2, z % 2
    mate = s + 1 - 2 * k
    pair = z + 1 - 2 * zb
    across = (z + 2) % 4
    group = (z + 2 * k) % 4
    member = 2 * zb + k
    owner_seq, owner_tp = 2 * c + half, member
    own_home = (owner_seq == s) & (owner_tp == z)
    gathers = c < 4
    reduces = c < reducers
    inner, outer = 1 + k, 3 * k
    primary = k == half
    is_inner = z == inner
    scale = HEAD_DIM ** (-0.5)
    small = tail // 2
    piece, spiece = D // reducers, small // reducers
    wide = [slice(256 * n, 256 * (n + 1)) for n in range(3)]
    planes = [z, pair, across, 3 - z]

    vec = [vectors[:, D * i : D * (i + 1)] for i in range(6)]

    def start(local, here, there):
        @pl.when(local)
        def _():
            here.start()

        @pl.when(jnp.logical_not(local))
        def _():
            there.start()

    def finish(local, here, there):
        @pl.when(local)
        def _():
            here.wait()

        @pl.when(jnp.logical_not(local))
        def _():
            there.wait()

    own_rows = rows_at(QUARTER * z, QUARTER, QUARTER)
    x_local = pltpu.make_async_copy(x_in, xg.at[own_rows], load_sem.at[0])
    g_loads = [
        pltpu.make_async_copy(inner_in, g.at[z, 0:D], load_sem.at[1]),
        pltpu.make_async_copy(outer_in, g.at[z, D : 2 * D], load_sem.at[2]),
        pltpu.make_async_copy(output_in, g.at[z, 2 * D : 2 * D + GROUP], load_sem.at[3]),
    ]

    @pl.when(primary)
    def _():
        x_local.start()

    for one in g_loads:
        one.start()
    g[z, 2 * D + GROUP :, :] = jnp.zeros((tail - GROUP, D), bf16)
    greet(columns)
    target = jnp.where(is_inner, outer, inner)

    def x_rows(q, j):
        return xg.at[rows_at(QUARTER * q + CHUNK * j, CHUNK, CHUNK)]

    def x_copy(j):
        return remote(x_in.at[pl.ds(CHUNK * j, CHUNK)], x_rows(z, j), x_send.at[j], x_recv.at[z, j], s, target)

    def x_forward(q, i, j):
        return remote(x_rows(q, j), x_rows(q, j), fwd_send.at[i, j], x_recv.at[q, j], s, outer)

    def x_mate(q, i, j):
        return remote(x_rows(q, j), x_rows(q, j), core_send.at[i, j], x_recv.at[q, j], mate, z)

    for j in range(CHUNKS):
        x_copy(j).start()

    spot = lax.broadcasted_iota(jnp.int32, (1, TOK), 1)
    valid = jnp.zeros((1, TOK), f32)
    first_spot = 0
    for i in range(lengths.shape[1]):
        real = lengths[0, i]
        valid += jnp.where((spot >= first_spot) & (spot < first_spot + real), 1.0, 0.0)
        first_spot += (real + CLUSTER - 1) // CLUSTER * CLUSTER
    cl_in[...] = jnp.concatenate([groups_in[...].astype(f32), valid, jnp.zeros((12, TOK), f32)], axis=0).astype(bf16)

    cl_z = 2 * k + zb
    cl_k = ((z - cl_z + 4) % 4) // 2
    cl_self = (cl_z == z) & (cl_k == k)
    cl_copy = remote(cl_in, cl, cl_sem.at[0], cl_sem.at[1], 2 * c + cl_k, cl_z)
    cl_local = pltpu.make_async_copy(cl_in, cl, cl_sem.at[1])
    start(cl_self, cl_local, cl_copy)

    for i, one in enumerate((key_in, query_in, value_in)):
        wt_ref[GROUP * i : GROUP * (i + 1), :] = one[...]
    bias_in[...] = jnp.broadcast_to(vectors[:, 7 * D :], bias_in.shape)
    ib_in[...] = jnp.broadcast_to(vectors[:, 6 * D : 7 * D], ib_in.shape)
    qrow = wt_ref.shape[0] // 4

    def wq_rows(part):
        return wg.at[rows_at(qrow * part, qrow, 16)]

    w_copy = remote(wt_ref.at[rows_at(qrow * c, qrow, 16)], wq_rows(c), q_send.at[0], q_recv.at[c], s, across)
    w_local = pltpu.make_async_copy(wt_ref, wg, q_send.at[0])
    b_copy = remote(bias_in, bias, b_sem.at[0], b_sem.at[1], s, across)
    b_local = pltpu.make_async_copy(bias_in, bias, b_sem.at[1])

    def wq_copy(turn):
        return remote(wq_rows(c), wq_rows(c), q_send.at[turn], q_recv.at[c], 2 * ((c + turn) % columns) + k, z)

    @pl.when((k == 1) & gathers)
    def _():
        w_copy.start()

    @pl.when(k == 1)
    def _():
        b_copy.start()

    @pl.when(k == 0)
    def _():
        w_local.start()
        b_local.start()

    bases, pieces = [0, 2 * D], [2 * D // 8, tail // 8]

    def w_rows(r, part, which):
        return g.at[planes[r], rows_at(bases[part] + pieces[part] * which, pieces[part], 16)]

    def w1(r, part):
        rows = w_rows(0, part, 4 * k + c)
        return remote(rows, rows, w1_send.at[part, r - 1], w1_recv.at[part, r - 1], s, planes[r])

    def w2(r, part, turn):
        rows = w_rows(r, part, 4 * k + c)
        return remote(rows, rows, w2_send.at[part, r - 1, turn - 1], w2_recv.at[part, r - 1, c], 2 * ((c + turn) % columns) + k, z)

    def w3(r, part, core):
        rows = g.at[planes[r], rows_at(bases[part] + 4 * pieces[part] * core, 4 * pieces[part], 16)]
        return remote(rows, rows, w3_send.at[part, r - 1], w3_recv.at[part, r - 1], mate, z)

    at_end = (z == 0) | (z == 3)

    def arrived_piece(r, part):
        rows = w_rows(r, part, 4 * k + c)
        return remote(rows, rows, w1_send.at[part, r - 1], w1_recv.at[part, r - 1], s, z)

    def relay_piece(r, part, index):
        rows = w_rows(r, part, 4 * k + c)
        return remote(rows, rows, w1_send.at[part, index - 1], w1_recv.at[part, index - 1], s, pair)

    def send_middle(part):
        @pl.when(gathers & at_end)
        def _():
            w1(1, part).start()
            w1(2, part).start()

        @pl.when(gathers & jnp.logical_not(at_end))
        def _():
            w1(3, part).start()

    def send_end(part):
        @pl.when(gathers & jnp.logical_not(at_end))
        def _():
            w1(1, part).start()

    def relay_ends(part):
        @pl.when(gathers & jnp.logical_not(at_end))
        def _():
            arrived_piece(3, part).wait_recv()
            w1(3, part).wait_send()
            relay_piece(3, part, 2).start()
            arrived_piece(2, part).wait_recv()
            relay_piece(2, part, 3).start()

    def spread(r, part):
        @pl.when(gathers)
        def _():
            if r == 1:
                arrived_piece(r, part).wait_recv()
            else:
                @pl.when(at_end)
                def _():
                    arrived_piece(r, part).wait_recv()

            @pl.loop(1, columns)
            def _(turn):
                w2(r, part, turn).start()

    def share_core(r, part):
        for peer in range(4):
            @pl.when(c != peer)
            def _():
                rows = w_rows(r, part, 4 * k + peer)
                remote(rows, rows, w1_send.at[part, 0], w2_recv.at[part, r - 1, peer], s, z).wait_recv()
        w3(r, part, k).start()

    def have(r, part):
        w3(r, part, 1 - k).wait_recv()

    for one in g_loads:
        one.wait()
    send_middle(1)
    send_middle(0)

    cot_k, cot_z = zb, 2 * k + half
    cot_self = (cot_k == k) & (cot_z == z)
    cot_copy = remote(cot_in, cot, cot_sem.at[0], cot_sem.at[1], 2 * c + cot_k, cot_z)
    cot_local = pltpu.make_async_copy(cot_in, cot, cot_sem.at[1])

    def ib_copy(r):
        return remote(ib_in, ib_ref.at[z], ib_send.at[r - 1], ib_recv.at[r - 1], s, planes[r])

    def bump(dst, src, rows, first=0):
        def body(t, carry):
            at = pl.ds(pl.multiple_of(first + 16 * t, 16), 16)
            from_ = pl.ds(pl.multiple_of(16 * t, 16), 16)
            dst[at, :] = (dst[at, :].astype(f32) + src[from_, :].astype(f32)).astype(bf16)
            return carry

        lax.fori_loop(0, rows // 16, body, 0)

    def core_copy(j):
        rows = rows_at(D * (1 - k), D, 16)
        return remote(g.at[j, rows], got1.at[j], c1_send.at[j], c1_recv.at[j], mate, z)

    def core_copy_small():
        rows = rows_at(2 * D + small * (1 - k), small, 16)
        return remote(g.at[:, rows], got1s, c1_send.at[4], c1_recv.at[4], mate, z)

    def column_copy(j, turn):
        dest = (c + turn) % columns
        if j < 4:
            rows = rows_at(D * k + piece * dest, piece, 16)
            return remote(g.at[j, rows], got2.at[j, turn - 1], c2_send.at[j, turn - 1], c2_recv.at[j, turn - 1], 2 * dest + k, z)
        rows = rows_at(2 * D + small * k + spiece * dest, spiece, 16)
        return remote(g.at[:, rows], got2s.at[turn - 1], c2_send.at[j, turn - 1], c2_recv.at[j, turn - 1], 2 * dest + k, z)

    def start_columns(j):
        @pl.loop(1, columns)
        def _(turn):
            @pl.when((c + turn) % columns < reducers)
            def _():
                column_copy(j, turn).start()

    def core_add(j):
        core_copy(j).wait()
        bump(g.at[j], got1.at[j], D, D * k)
        start_columns(j)

    def core_add_small():
        core_copy_small().wait()

        def one(j, carry):
            bump(g.at[j], got1s.at[j], small, 2 * D + small * k)
            return carry

        lax.fori_loop(0, 4, one, 0)
        start_columns(4)

    mine = D * k + piece * c
    smine = 2 * D + small * k + spiece * c

    def column_add(j):
        @pl.when(reduces)
        def _():
            @pl.loop(1, columns)
            def _(turn):
                if j < 4:
                    column_copy(j, turn).wait_recv()
                    term = got2.at[j, turn - 1]
                    if far:
                        fetch = pltpu.make_async_copy(term, stage, load_sem.at[4])
                        fetch.start()
                        fetch.wait()
                        term = stage
                    bump(g.at[j], term, piece, mine)
                else:
                    column_copy(j, turn).wait_recv()

                    def one(i, carry):
                        term = got2s.at[turn - 1, i]
                        if far:
                            fetch = pltpu.make_async_copy(term, stages, load_sem.at[4])
                            fetch.start()
                            fetch.wait()
                            term = stages
                        bump(g.at[i], term, spiece, smine)
                        return carry

                    lax.fori_loop(0, 4, one, 0)

    def plane_rows(part):
        return rows_at(mine if part == 0 else smine, piece if part == 0 else spiece, 16)

    def plane_copy(part, r):
        got = got3 if part == 0 else got3s
        return remote(g.at[planes[r], plane_rows(part)], got.at[r - 1], c3_send.at[part, r - 1], c3_recv.at[part, r - 1], s, planes[r])

    def start_plane(part, j):
        got = got3 if part == 0 else got3s
        r = planes[j]

        @pl.when(reduces & (z != j))
        def _():
            remote(g.at[j, plane_rows(part)], got.at[r - 1], c3_send.at[part, r - 1], c3_recv.at[part, r - 1], s, j).start()

    def by_core(action):
        for core, half_of in ((0, fin_inner), (1, fin_outer)):
            @pl.when(k == core)
            def _():
                action(half_of)

    def final_rows(part, column, core, half_of=fin_inner):
        if part == 0:
            return half_of.at[rows_at(piece * column, piece, 16)]
        return fin_tail.at[rows_at(small * core + spiece * column, spiece, 16)]

    def final_copy(part, turn, half_of=fin_inner):
        own = done if part == 0 else dones
        return remote(own, final_rows(part, c, k, half_of), c4_send.at[part, turn - 1], c4_recv.at[part, c], 2 * ((c + turn) % columns) + k, z)

    def final_local(part, half_of=fin_inner):
        return pltpu.make_async_copy(done if part == 0 else dones, final_rows(part, c, k, half_of), load_sem.at[6 + part])

    def finish_planes(part):
        first, size = (mine, piece) if part == 0 else (smine, spiece)
        got = got3 if part == 0 else got3s
        own = done if part == 0 else dones

        @pl.when(reduces)
        def _():
            for r in range(1, 4):
                plane_copy(part, r).wait_recv()

            def body(t, carry):
                at = pl.ds(pl.multiple_of(first + 16 * t, 16), 16)
                from_ = pl.ds(pl.multiple_of(16 * t, 16), 16)
                total = g[z, at, :].astype(f32)
                for step in range(3):
                    total += got[step, from_, :].astype(f32)
                own[from_, :] = total.astype(bf16)
                return carry

            lax.fori_loop(0, size // 16, body, 0)

            def send(half_of):
                final_local(part, half_of).start()

                @pl.loop(1, columns)
                def _(turn):
                    final_copy(part, turn, half_of).start()

            by_core(send)

    def mate_copy(part, core, half_of=fin_inner):
        rows = half_of if part == 0 else fin_tail.at[rows_at(small * core, small, 16)]
        return remote(rows, rows, c5_send.at[part], c5_recv.at[part], mate, z)

    def spread_final(part):
        for peer in range(reducers):
            @pl.when(c != peer)
            def _():
                rows = final_rows(part, peer, k)
                remote(rows, rows, c4_send.at[part, 0], c4_recv.at[part, peer], s, z).wait_recv()
        @pl.when(reduces)
        def _():
            final_local(part).wait()

        by_core(lambda half_of: mate_copy(part, k, half_of).start())

    lo_copy = remote(lo_src, lo_ref, lo_sem.at[0], lo_sem.at[1], owner_seq, owner_tp)
    lo_local = pltpu.make_async_copy(lo_src, lo_ref, lo_sem.at[1])

    def gm_copy(q):
        home_z = 2 * half + q % 2
        home_k = ((q - home_z + 4) % 4) // 2
        return remote(gsend.at[q], gm.at[:, rows_at(QUARTER * member, QUARTER, QUARTER)], gm_send.at[q], gm_recv.at[member], 2 * c + home_k, home_z)

    dwb = got1.at[3, 0 : dw_ref.shape[0]]
    dxp = [got1.at[i, 0:QUARTER] for i in range(3)]
    wrow = dwb.shape[0] // reducers

    def dw_rows(ref, part):
        return ref.at[rows_at(wrow * part, wrow, 16)]

    def e1(turn):
        dest = (c + turn) % columns
        return remote(dw_rows(dwb, dest), e1_got.at[turn - 1], e1_send.at[turn - 1], e1_recv.at[turn - 1], 2 * dest + k, z)

    def attention(qt, table, onehot, rt, mx):
        finish(cl_self, cl_local, cl_copy)
        low_iota = lax.broadcasted_iota(jnp.int32, (CLUSTER, CLUSTER), 0)
        high_iota = lax.broadcasted_iota(jnp.int32, (CLUSTER, CLUSTER), 1)
        upper = jnp.concatenate([(low_iota < high_iota).astype(f32), jnp.ones((CLUSTER, CLUSTER), f32)], axis=1).astype(bf16)
        names = lax.broadcasted_iota(jnp.int32, (BLOCKS, CLUSTER), 0).astype(f32)
        base = jnp.zeros((3 * BLOCKS, CLUSTER), f32)
        slot_ref[...] = jnp.zeros_like(slot_ref)
        for b in range(BLOCKS):
            lanes = slice(CLUSTER * b, CLUSTER * (b + 1))
            block = cl[:, lanes].astype(f32)
            belongs = jnp.concatenate([(block[h : h + 1] == names).astype(f32) for h in range(3)], axis=0)
            counts = nn(belongs.astype(bf16), upper)
            seen = (counts[:, :CLUSTER] + base) * belongs
            base = base + counts[:, CLUSTER:]
            for h in range(3):
                rank = jnp.sum(seen[BLOCKS * h : BLOCKS * (h + 1)], axis=0, keepdims=True)
                slot_ref[h : h + 1, lanes] = rank
                slot_ref[h + 3 : h + 4, lanes] = block[h : h + 1]
        valid = cl[3:4, :].astype(f32)
        fill = lax.broadcasted_iota(jnp.int32, (16, TOK), 0) == 0
        mask_rows = jnp.where(fill, jnp.where(valid > 0.5, 0.0, -1e30), 0.0).astype(bf16)
        ones_rows = jnp.where(fill, 1.0, 0.0).astype(bf16)
        for h in range(3):
            qt[h, 64:80, :] = mask_rows
            qt[h, 144:160, :] = ones_rows

        def canon(q):
            return jnp.where(half == 1, 3 - q, q)

        first_half = canon(z)
        order = [z, canon(1 - first_half), canon(2), canon(3)]
        order[0] = jnp.where(primary, z, canon(0))
        order[1] = jnp.where(primary, order[1], canon(1))

        def arrived(q, j):
            return remote(x_rows(q, j), x_rows(q, j), x_send.at[0], x_recv.at[q, j], s, z)

        def pass_on():
            for j in range(CHUNKS):
                for i in (2, 3):
                    arrived(order[i], j).wait_recv()

                    @pl.when(is_inner)
                    def _():
                        x_forward(order[i], i - 2, j).start()

                    x_mate(order[i], i, j).start()

        def project(i):
            q = order[i]
            if i == 0:
                @pl.when(jnp.logical_not(primary))
                def _():
                    for j in range(CHUNKS):
                        arrived(q, j).wait_recv()
            elif i == 1:
                for j in range(CHUNKS):
                    arrived(q, j).wait_recv()

                    @pl.when(primary)
                    def _():
                        x_mate(q, 1, j).start()
            else:
                @pl.when(jnp.logical_not(primary))
                def _():
                    for j in range(CHUNKS):
                        arrived(q, j).wait_recv()
            lanes = rows_at(QUARTER * q, QUARTER, QUARTER)
            tokens = xg[lanes, :]
            found = (nt(wg[...], tokens) + bias_col).astype(bf16)
            for h in range(3):
                for place_at, i in ((K_ROWS, 0), (Q_ROWS, 1), (V_ROWS, 2)):
                    qt[h, place_at : place_at + 64, lanes] = found[GROUP * i + HEAD_DIM * h : GROUP * i + HEAD_DIM * (h + 1)]

        @pl.when(primary)
        def _():
            x_local.wait()
            for j in range(CHUNKS):
                x_mate(z, 0, j).start()

        @pl.when(is_inner)
        def _():
            pass_on()
            send_end(1)
            send_end(0)

        @pl.when(k == 0)
        def _():
            w_local.wait()
            b_local.wait()

        @pl.when((k == 1) & gathers)
        def _():
            w_copy.wait()

            @pl.loop(1, columns)
            def _(turn):
                wq_copy(turn).start()

        @pl.when(k == 1)
        def _():
            b_copy.wait()
            for peer in range(4):
                @pl.when(c != peer)
                def _():
                    remote(wq_rows(peer), wq_rows(peer), q_send.at[0], q_recv.at[peer], s, z).wait_recv()

        bias_col = jnp.transpose(bias[...], (1, 0))[0 : 3 * GROUP, 0:1]
        project(0)
        project(1)

        @pl.when(primary & jnp.logical_not(is_inner))
        def _():
            pass_on()

        project(2)
        project(3)

        @pl.when(jnp.logical_not(is_inner))
        def _():
            send_end(1)
            send_end(0)

        relay_ends(1)
        relay_ends(0)

        spread(1, 0)
        for r in range(1, 4):
            spread(r, 1)
        start(cot_self, cot_local, cot_copy)
        ib_ref[pl.ds(z, 1)] = ib_in[...][None]
        for r in range(1, 4):
            ib_copy(r).start()

        def mixed_at(h, grp):
            return mixed.at[rows_at(GROUP * grp + HEAD_DIM * h, HEAD_DIM, HEAD_DIM)]

        rank_iota = lax.broadcasted_iota(jnp.int32, (CLUSTER, TOK), 0).astype(f32)

        def head(h, carry):
            rank_row = slot_ref[pl.ds(h, 1), :]
            name_row = slot_ref[pl.ds(h + 3, 1), :]
            onehot[...] = (rank_row == rank_iota).astype(f32).astype(bf16)

            def build(b, carry):
                name = b.astype(f32)
                table[rows_at(CLUSTER * b, CLUSTER, CLUSTER), :] = onehot[...] * (name_row == name).astype(f32).astype(bf16)
                return carry

            lax.fori_loop(0, BLOCKS, build, 0)

            def sort(b, carry):
                rows = rows_at(TOK // 2 * b, TOK // 2, TOK // 2)
                srt[h, :, rows] = nt(qt[h], table[rows, :]).astype(bf16)
                return carry

            lax.fori_loop(0, 2, sort, 0)

            for b in range(BLOCKS):
                lanes = slice(CLUSTER * b, CLUSTER * (b + 1))
                scores = tn(srt[h, K_ROWS : K_ROWS + 80, lanes], srt[h, Q_ROWS : Q_ROWS + 80, lanes]) * scale
                top = jnp.maximum(jnp.max(scores, axis=0, keepdims=True), -1e20)
                weights = jnp.exp(scores - top)
                total = jnp.sum(weights, axis=0, keepdims=True)
                part = weights / jnp.where(total > 0.5, total, 1.0)
                share[h, b] = part
                rt[:, lanes] = nn(srt[h, V_ROWS : V_ROWS + 64, lanes], part.astype(bf16)).astype(bf16)

            def send_back(d):
                @pl.when(d == member)
                def _():
                    pltpu.make_async_copy(mx.at[h, d], mixed_at(h, group), m_recv.at[h, d]).start()

                @pl.when(d != member)
                def _():
                    remote(
                        mx.at[h, d], mixed_at(h, group), m_send.at[h, d], m_recv.at[h, member], 2 * c + d % 2, 2 * half + d // 2
                    ).start()

            def back(e, carry):
                found = nn(rt[...], table[:, rows_at(TOK // 2 * e, TOK // 2, TOK // 2)]).astype(bf16)
                for f in range(2):
                    mx[h, 2 * e + f] = found[:, QUARTER * f : QUARTER * (f + 1)]
                    send_back(2 * e + f)
                return carry

            lax.fori_loop(0, 2, back, 0)

            for r in (2, 3):
                @pl.when(h == r - 2)
                def _():
                    spread(r, 0)

            return carry

        lax.fori_loop(0, 3, head, 0)
        for r in range(1, 4):
            share_core(r, 1)

        def await_mixed(h, carry):
            def one(d, carry):
                grp = (2 * half + d // 2 + 2 * (d % 2)) % 4
                remote(mx.at[h, d], mixed_at(h, grp), m_send.at[h, d], m_recv.at[h, d], s, z).wait_recv()

                @pl.when(d != member)
                def _():
                    remote(mx.at[h, d], mixed_at(h, grp), m_send.at[h, d], m_recv.at[h, d], s, z).wait_send()

                return carry

            return lax.fori_loop(0, 4, one, carry)

        lax.fori_loop(0, 3, await_mixed, 0)

    pl.run_scoped(
        attention,
        pltpu.VMEM((3, AUG, TOK), bf16), pltpu.VMEM((TOK, TOK), bf16), pltpu.VMEM((CLUSTER, TOK), bf16),
        pltpu.VMEM((HEAD_DIM, TOK), bf16), pltpu.VMEM((3, 4, HEAD_DIM, QUARTER), bf16),
    )

    def feed_forward(gi, mixt, norm, rstd, low, turned, act, slope):
        for r in range(1, 4):
            have(r, 1)
        for q in range(4):
            mixt[q] = jnp.transpose(mixed[GROUP * q : GROUP * (q + 1), :], (1, 0))
        for n in wide:
            total = nn(mixt[0], g[0, 2 * D : 2 * D + GROUP, n])
            for q in range(1, 4):
                total += nn(mixt[q], g[q, 2 * D : 2 * D + GROUP, n])
            two[:, n] = total

        def mean_of(rows):
            return jnp.mean(rows, axis=-1, keepdims=True)

        def first_norm(t, carry):
            at = rows_at(ROWS * t, ROWS, ROWS)
            rows = two[at, :] + xg[rows_at(QUARTER * member + ROWS * t, ROWS, ROWS), :].astype(f32) + vec[0]
            centred = rows - mean_of(rows)
            scaled = lax.rsqrt(mean_of(centred * centred) + 1e-6)
            normed = centred * scaled
            norm[at, :] = normed
            rstd[at, :] = jnp.broadcast_to(scaled, (ROWS, 128))
            low[at, :] = (normed * vec[1] + vec[2]).astype(bf16)
            return carry

        lax.fori_loop(0, QUARTER // ROWS, first_norm, 0)

        for r in range(1, 4):
            ib_copy(r).wait_send()
            remote(ib_in, ib_ref.at[planes[r]], ib_send.at[r - 1], ib_recv.at[r - 1], s, z).wait_recv()

        def forward_slice(step, carry):
            j = jnp.where(step == 0, z, jnp.where(step == 1, pair, jnp.where(step == 2, across, 3 - z)))
            for r in range(1, 4):
                @pl.when(step == r)
                def _():
                    have(r, 0)

            for n in wide:
                slope[j, :, n] = nn(low[...], g[j, 0:D, n]) + ib_ref[j, 0:1, n]

            def bend(t, carry):
                at = rows_at(ROWS * t, ROWS, ROWS)
                v = slope[j, at, :]
                phi = 0.5 + 0.5 * lax.erf(v * (0.5 ** 0.5))
                act[j, at, :] = (v * phi).astype(bf16)
                slope[j, at, :] = phi + v * (jnp.exp(v * v * -0.5) * 0.3989422804014327)
                return carry

            lax.fori_loop(0, QUARTER // ROWS, bend, 0)
            for r in range(1, 4):
                @pl.when(step == r - 1)
                def _():
                    share_core(r, 0)

            for n in wide:
                part = nn(act[j], g[j, D : 2 * D, n])

                @pl.when(step == 0)
                def _():
                    two[:, n] = part

                @pl.when(step > 0)
                def _():
                    two[:, n] += part

            return carry

        lax.fori_loop(0, 4, forward_slice, 0)

        for part in range(2):
            for r in range(1, 4):
                w3(r, part, k).wait_send()

                @pl.when(gathers)
                def _():
                    if r < 3:
                        w1(r, part).wait_send()
                    else:
                        @pl.when(jnp.logical_not(at_end))
                        def _():
                            w1(r, part).wait_send()

                    @pl.loop(1, columns)
                    def _(turn):
                        w2(r, part, turn).wait_send()

        finish(cot_self, cot_local, cot_copy)

        zero_row = jnp.zeros((1, D), f32)

        def second_norm(t, carry):
            gain_sum, shift_sum, bias_sum = carry
            at = rows_at(ROWS * t, ROWS, ROWS)
            rows = norm[at, :] * vec[1] + vec[2] + two[at, :] + vec[3]
            centred = rows - mean_of(rows)
            scaled = lax.rsqrt(mean_of(centred * centred) + 1e-6)
            normed = centred * scaled
            lo_src[at, :] = (normed * vec[4] + vec[5]).astype(bf16)
            up = cot[at, :].astype(f32)
            e = up * vec[4]
            grad = (e - mean_of(e) - normed * mean_of(e * normed)) * scaled
            two[at, :] = grad
            grad_low = grad.astype(bf16)
            gb[at, :] = grad_low
            return (
                gain_sum + jnp.sum(up * normed, axis=0, keepdims=True),
                shift_sum + jnp.sum(up, axis=0, keepdims=True),
                bias_sum + jnp.sum(grad_low.astype(f32), axis=0, keepdims=True),
            )

        gain2, shift2, outer_bias = lax.fori_loop(0, QUARTER // ROWS, second_norm, (zero_row, zero_row, zero_row))

        start(own_home, lo_local, lo_copy)

        turned[...] = jnp.transpose(low[...], (1, 0))
        inner_bias = []
        for j in range(4):
            sums = []
            for n in wide:
                found = (nt(gb[...], g[j, D + n.start : D + n.stop, :]) * slope[j, :, n]).astype(bf16)
                gi[:, n] = found
                sums.append(jnp.sum(found.astype(f32), axis=0, keepdims=True))
            inner_bias.append(jnp.concatenate(sums, axis=1))
            act_turned = jnp.transpose(act[j], (1, 0))
            for n in wide:
                g[j, D : 2 * D, n] = nn(act_turned, gb[:, n]).astype(bf16)
            for n in wide:
                part = nt(gi[...], g[j, n.start : n.stop, :])
                gf[:, n] = part if j == 0 else gf[:, n] + part
            for n in wide:
                g[j, 0:D, n] = nn(turned[...], gi[:, n]).astype(bf16)
            core_copy(j).start()
            if j > 0:
                core_add(j - 1)

        def first_back(t, carry):
            gain_sum, shift_sum, bias_sum = carry
            at = rows_at(ROWS * t, ROWS, ROWS)
            up = two[at, :] + gf[at, :]
            e = up * vec[1]
            normed = norm[at, :]
            grad = (e - mean_of(e) - normed * mean_of(e * normed)) * rstd[at, 0:1]
            two[at, :] = grad
            grad_low = grad.astype(bf16)
            gb[at, :] = grad_low
            return (
                gain_sum + jnp.sum(up * normed, axis=0, keepdims=True),
                shift_sum + jnp.sum(up, axis=0, keepdims=True),
                bias_sum + jnp.sum(grad_low.astype(f32), axis=0, keepdims=True),
            )

        gain1, shift1, output_bias = lax.fori_loop(0, QUARTER // ROWS, first_back, (zero_row, zero_row, zero_row))

        for q in range(4):
            gsend[q] = nt(g[q, 2 * D : 2 * D + GROUP, :], gb[...]).astype(bf16)

            @pl.when(group == q)
            def _():
                gm[:, rows_at(QUARTER * member, QUARTER, QUARTER)] = gsend[q]

            @pl.when(group != q)
            def _():
                gm_copy(q).start()

        head_rows = jnp.concatenate([gain2, shift2, outer_bias, gain1, shift1, output_bias], axis=0)
        for q in range(4):
            g[q, 2 * D : 2 * D + GROUP, :] = nn(mixed[GROUP * q : GROUP * (q + 1), :], gb[...]).astype(bf16)
            g[q, 2 * D + GROUP : 2 * D + GROUP + 16, :] = jnp.concatenate(
                [head_rows, inner_bias[q], jnp.zeros((9, D), f32)], axis=0
            ).astype(bf16)
        core_copy_small().start()
        core_add(3)

    pl.run_scoped(
        feed_forward,
        pltpu.VMEM((QUARTER, D), bf16), pltpu.VMEM((4, QUARTER, GROUP), bf16), pltpu.VMEM((QUARTER, D), f32), pltpu.VMEM((QUARTER, 128), f32),
        pltpu.VMEM((QUARTER, D), bf16), pltpu.VMEM((D, QUARTER), bf16), pltpu.VMEM((4, QUARTER, D), bf16), pltpu.VMEM((4, QUARTER, D), f32),
    )

    def attention_back(table, onehot, gs, ds, dt):
        for m in range(4):
            @pl.when(m != member)
            def _():
                rows = gm.at[:, QUARTER * m : QUARTER * (m + 1)]
                remote(rows, rows, gm_send.at[0], gm_recv.at[m], s, z).wait_recv()

        rank_iota = lax.broadcasted_iota(jnp.int32, (CLUSTER, TOK), 0).astype(f32)

        def head(h, carry):
            rank_row = slot_ref[pl.ds(h, 1), :]
            name_row = slot_ref[pl.ds(h + 3, 1), :]
            onehot[...] = (rank_row == rank_iota).astype(f32).astype(bf16)

            def build(b, carry):
                name = b.astype(f32)
                table[rows_at(CLUSTER * b, CLUSTER, CLUSTER), :] = onehot[...] * (name_row == name).astype(f32).astype(bf16)
                return carry

            lax.fori_loop(0, BLOCKS, build, 0)

            def sort(b, carry):
                rows = rows_at(TOK // 2 * b, TOK // 2, TOK // 2)
                gs[:, rows] = nt(gm[rows_at(HEAD_DIM * h, HEAD_DIM, HEAD_DIM), :], table[rows, :]).astype(bf16)
                return carry

            lax.fori_loop(0, 2, sort, 0)

            for b in range(BLOCKS // 2):
                lanes = slice(2 * CLUSTER * b, 2 * CLUSTER * (b + 1))
                grad = gs[:, lanes]
                grad_part = tn(srt[h, V_ROWS : V_ROWS + 64, lanes], grad)
                scores, probs = [], []
                for e in range(2):
                    at = slice(CLUSTER * e, CLUSTER * (e + 1))
                    part = share[h, 2 * b + e]
                    block = grad_part[at, at]
                    inside = jnp.sum(block * part, axis=0, keepdims=True)
                    scores.append((part * (block - inside)).astype(bf16))
                    probs.append(part.astype(bf16))
                scores, probs = diagonal(*scores), diagonal(*probs)
                ds[0:64, lanes] = (nt(srt[h, Q_ROWS : Q_ROWS + 64, lanes], scores) * scale).astype(bf16)
                ds[64:128, lanes] = (nn(srt[h, K_ROWS : K_ROWS + 64, lanes], scores) * scale).astype(bf16)
                ds[128:192, lanes] = nt(grad, probs).astype(bf16)

            def back(d, carry):
                rows = rows_at(TOK // 2 * d, TOK // 2, TOK // 2)
                found = nn(ds[...], table[:, rows]).astype(bf16)
                for i in range(3):
                    dt[rows_at(GROUP * i + HEAD_DIM * h, HEAD_DIM, HEAD_DIM), rows] = found[HEAD_DIM * i : HEAD_DIM * (i + 1)]
                return carry

            lax.fori_loop(0, 2, back, 0)

            @pl.when(h == 0)
            def _():
                core_add_small()
                column_add(0)
                start_plane(0, 0)

            @pl.when(h == 1)
            def _():
                column_add(1)
                start_plane(0, 1)

            return carry

        lax.fori_loop(0, 3, head, 0)


        here = 2 * zb
        there = 2 * (1 - zb)

        def partial_rows(quarter, n):
            return tn(dt[:, rows_at(QUARTER * quarter, QUARTER, QUARTER)], wg[:, n])

        def d1(i):
            return remote(dxp[i], rd1.at[i], d1_send.at[i], d1_recv.at[i], mate, z)

        def d2(i):
            rows = slice(256 * i, 256 * (i + 1))
            return remote(dxp[2].at[rows], rd2.at[rows], d2_send.at[i], d2_recv.at[i], s, pair)

        def d3(i):
            rows = slice(256 * i, 256 * (i + 1))
            return remote(dx_src.at[rows], dx_ref.at[rows], d3_send.at[i], d3_recv.at[i], owner_seq, owner_tp)

        def d3_local(i):
            rows = slice(256 * i, 256 * (i + 1))
            return pltpu.make_async_copy(dx_src.at[rows], dx_ref.at[rows], d3_recv.at[i])

        for n in wide:
            dxp[0][:, n] = partial_rows(there + 1 - k, n).astype(bf16)
        d1(0).start()
        for n in wide:
            gf[:, n] = partial_rows(there + k, n)
        d1(0).wait_recv()
        for i in range(2):
            def add_there(t, carry):
                at = rows_at(256 * i + 16 * t, 16, 16)
                dxp[2][at, :] = (gf[at, :] + rd1[0, at, :].astype(f32)).astype(bf16)
                return carry

            lax.fori_loop(0, 16, add_there, 0)
            d2(i).start()
        for n in wide:
            dxp[1][:, n] = partial_rows(here + 1 - k, n).astype(bf16)
        d1(1).start()
        for n in wide:
            two[:, n] += partial_rows(here + k, n)
        d1(1).wait_recv()

        for n in wide:
            dwb[0 : 3 * GROUP, n] = nn(dt[...], xg[:, n]).astype(bf16)
        ones = jnp.ones((16, TOK), bf16)
        dwb[3 * GROUP : 3 * GROUP + 16, 0 : 3 * GROUP] = nt(ones, dt[...]).astype(bf16)
        dwb[3 * GROUP : 3 * GROUP + 16, 3 * GROUP :] = jnp.zeros((16, D - 3 * GROUP), bf16)
        dwb[3 * GROUP + 16 :, :] = jnp.zeros((dwb.shape[0] - 3 * GROUP - 16, D), bf16)

        @pl.loop(1, columns)
        def _(turn):
            @pl.when((c + turn) % columns < reducers)
            def _():
                e1(turn).start()


        for j in (2, 3):
            column_add(j)
            start_plane(0, j)
        column_add(4)
        for j in range(4):
            start_plane(1, j)

        for i in range(2):
            d2(i).wait_recv()

            def add_here(t, carry):
                at = rows_at(256 * i + 16 * t, 16, 16)
                dx_src[at, :] = (two[at, :] + rd1[1, at, :].astype(f32) + rd2[at, :].astype(f32)).astype(bf16)
                return carry

            lax.fori_loop(0, 16, add_here, 0)

            start(own_home, d3_local(i), d3(i))

        @pl.when(reduces)
        def _():
            @pl.loop(1, columns)
            def _(turn):
                e1(turn).wait_recv()
                bump(dwb, e1_got.at[turn - 1], wrow, wrow * c)

        e2 = remote(dw_rows(dwb, c), e2_got, e2_send.at[0], e2_recv.at[0], s - 1, across)

        def e3(turn):
            return remote(dw_rows(dw_ref, c), dw_rows(dw_ref, c), e3_send.at[turn - 1], e3_recv.at[c], 2 * ((c + turn) % columns) + k, z)

        e4 = remote(dw_ref, dw_ref, e4_send.at[0], e4_recv.at[0], mate, z)

        @pl.when(reduces & (k == 1))
        def _():
            e2.start()

        finish_planes(0)
        finish_planes(1)

        @pl.when(reduces & (k == 0))
        def _():
            remote(e2_got, e2_got, e2_send.at[0], e2_recv.at[0], s, z).wait_recv()

            def add_dw(t, carry):
                at = rows_at(wrow * c + 16 * t, 16, 16)
                from_ = rows_at(16 * t, 16, 16)
                dw_ref[at, :] = (dwb[at, :].astype(f32) + e2_got[from_, :].astype(f32)).astype(bf16)
                return carry

            lax.fori_loop(0, wrow // 16, add_dw, 0)

            @pl.loop(1, columns)
            def _(turn):
                e3(turn).start()

        spread_final(0)
        spread_final(1)

        @pl.when(k == 0)
        def _():
            for peer in range(reducers):
                @pl.when(c != peer)
                def _():
                    remote(dw_rows(dw_ref, peer), dw_rows(dw_ref, peer), e3_send.at[0], e3_recv.at[peer], s, z).wait_recv()
            e4.start()
            e4.wait_send()

        @pl.when(k == 1)
        def _():
            e4.wait_recv()

        @pl.when(reduces & (k == 1))
        def _():
            e2.wait_send()

        @pl.when(reduces & (k == 0))
        def _():
            @pl.loop(1, columns)
            def _(turn):
                e3(turn).wait_send()

        @pl.loop(1, columns)
        def _(turn):
            @pl.when((c + turn) % columns < reducers)
            def _():
                e1(turn).wait_send()

            @pl.when((c + turn) % columns < reducers)
            def _():
                for j in range(5):
                    column_copy(j, turn).wait_send()

        for part in range(2):
            @pl.when(reduces)
            def _():
                for r in range(1, 4):
                    plane_copy(part, r).wait_send()

                @pl.loop(1, columns)
                def _(turn):
                    final_copy(part, turn).wait_send()

            mate_copy(part, k).wait_send()
            mate_copy(part, 1 - k).wait_recv()

        finish(own_home, lo_local, lo_copy)
        for i in range(2):
            finish(own_home, d3_local(i), d3(i))
        for q in range(4):
            @pl.when(group != q)
            def _():
                gm_copy(q).wait_send()
        for i in range(2):
            d1(i).wait_send()
            d2(i).wait_send()

        for j in range(CHUNKS):
            x_copy(j).wait_send()

            @pl.when(primary)
            def _():
                for i in range(4):
                    x_mate(0, i, j).wait_send()

            @pl.when(is_inner)
            def _():
                for i in range(2):
                    x_forward(0, i, j).wait_send()

        @pl.when((k == 1) & gathers)
        def _():
            @pl.loop(1, columns)
            def _(turn):
                wq_copy(turn).wait_send()

    pl.run_scoped(
        attention_back,
        pltpu.VMEM((TOK, TOK), bf16), pltpu.VMEM((CLUSTER, TOK), bf16), pltpu.VMEM((HEAD_DIM, TOK), bf16), pltpu.VMEM((GROUP, TOK), bf16),
        pltpu.VMEM((3 * GROUP, TOK), bf16),
    )


def layer_call(columns, reducers, tail, *arrays):
    vmem = pl.BlockSpec(memory_space=pltpu.VMEM)
    smem = pl.BlockSpec(memory_space=pltpu.SMEM)
    anyspec = pl.BlockSpec(memory_space=pl.ANY)
    dma = pltpu.SemaphoreType.DMA
    rows = 2 * D + tail
    piece, spiece = D // reducers, tail // 2 // reducers
    turns = columns - 1
    wide = 16 * reducers * -(-(3 * GROUP + 16) // (16 * reducers))
    far = columns > 4
    low = lambda *shape: pltpu.VMEM(shape, bf16)
    full = lambda *shape: pltpu.VMEM(shape, f32)
    out = lambda *shape: jax.ShapeDtypeStruct(shape, bf16)
    terms, sterms = (4, turns, piece, D), (turns, 4, spiece, D)
    return pl.pallas_call(
        functools.partial(layer, columns, reducers, tail, far),
        out_shape=[out(QUARTER, D), out(QUARTER, D), out(D, D), out(D, D), out(tail, D), out(wide, D)]
        + ([out(*terms), out(*sterms)] if far else []),
        in_specs=[anyspec, vmem, smem] + [vmem] * 3 + [anyspec] * 4 + [vmem],
        out_specs=[anyspec] * 5 + [vmem] + ([anyspec] * 2 if far else []),
        scratch_shapes=([low(piece, D), low(spiece, D)] if far else [low(*terms), low(*sterms)])
        + [
            low(4, rows, D), low(TOK, D), low(3, AUG, TOK), full(3, BLOCKS, CLUSTER, CLUSTER), low(3 * GROUP, D), low(16, TOK),
            full(8, TOK), full(8, 640), low(D, QUARTER), low(QUARTER, D), full(4, 8, D),
            full(QUARTER, D), full(QUARTER, D), low(QUARTER, D), low(4, GROUP, QUARTER), low(GROUP, TOK), low(QUARTER, D), low(QUARTER, D),
            low(4, D, D), low(4, tail // 2, D), low(3, piece, D), low(3, spiece, D),
            low(2, QUARTER, D), low(QUARTER, D), low(turns, wide // reducers, D), low(wide // reducers, D), low(piece, D), low(spiece, D),
            low(16, TOK), low(3 * GROUP, D), full(8, 640), full(8, D),
            dma((8,)), dma((CHUNKS,)), dma((4, CHUNKS)), dma((2, CHUNKS)), dma((4, CHUNKS)), dma((2,)), dma((columns,)), dma((4,)),
            dma((2,)), dma((2,)), dma((3,)), dma((3,)),
            dma((2, 3)), dma((2, 3)), dma((2, 3, turns)), dma((2, 3, 4)), dma((2, 3)), dma((2, 3)), dma((3, 4)), dma((3, 4)),
            dma((4,)), dma((4,)), dma((2,)),
            dma((5,)), dma((5,)), dma((5, turns)), dma((5, turns)), dma((2, 3)), dma((2, 3)), dma((2, turns)), dma((2, reducers)),
            dma((2,)), dma((2,)), dma((2,)), dma((2,)), dma((2,)), dma((2,)), dma((2,)), dma((2,)),
            dma((turns,)), dma((turns,)), dma((1,)), dma((1,)), dma((turns,)), dma((reducers,)), dma((1,)), dma((1,)),
        ],
        compiler_params=pltpu.CompilerParams(collective_id=0, has_side_effects=True, vmem_limit_bytes=63 * 2**20),
    )(*arrays)


def shards(
    layer_input, clusters, document_lengths, query_weight, key_weight, value_weight, query_bias, value_bias, output_weight,
    output_bias, first_gain, first_shift, inner_weight, inner_bias, outer_weight, outer_bias, second_gain, second_shift, cotangent,
):
    columns = lax.axis_size("seq") // 2
    reducers = min(columns, 16)
    tail = 32 * reducers * -(-(GROUP + 16) // (32 * reducers))
    vectors = jnp.concatenate(
        [output_bias, first_gain, first_shift, outer_bias, second_gain, second_shift, inner_bias]
        + [jnp.zeros((GROUP,), f32), query_bias, value_bias, jnp.zeros((64,), f32)]
    ).reshape(1, -1)
    lo, dx, fin_inner, fin_outer, fin_tail, dw, *_ = layer_call(
        columns, reducers, tail, layer_input, clusters.T, document_lengths, query_weight.T, key_weight.T, value_weight.T,
        inner_weight, outer_weight, output_weight, cotangent, vectors,
    )
    turned = lambda i: dw[GROUP * i : GROUP * (i + 1)].astype(f32).T
    bias_row = dw[3 * GROUP].astype(f32)
    sums = fin_tail[GROUP : GROUP + 16].astype(f32)
    return (
        lo,
        dx.astype(f32),
        turned(1),
        turned(0),
        turned(2),
        bias_row[GROUP : 2 * GROUP],
        bias_row[2 * GROUP : 3 * GROUP],
        fin_tail[:GROUP].astype(f32),
        sums[5],
        sums[3],
        sums[4],
        fin_inner.astype(f32),
        sums[6],
        fin_outer.astype(f32),
        sums[2],
        sums[0],
        sums[1],
    )


def solution(mesh):
    rows, cols = P(("seq", "tp"), None), P(None, "tp")
    return jax.shard_map(
        shards,
        mesh=mesh,
        in_specs=(
            rows, P("seq", "tp"), P("seq", None), cols, cols, cols, P("tp"), P("tp"), P("tp", None), P(), P(), P(),
            cols, P("tp"), P("tp", None), P(), P(), P(), rows,
        ),
        out_specs=(
            rows, rows, cols, cols, cols, P("tp"), P("tp"), P("tp", None), P(), P(), P(), cols, P("tp"), P("tp", None), P(), P(), P(),
        ),
        check_vma=False,
    )
```

```python
import functools
import jax
import jax.numpy as jnp
from jax import lax
from jax.experimental import pallas as pl
from jax.experimental.pallas import tpu as pltpu
from jax.sharding import PartitionSpec as P

MESH = pl.DeviceIdType.MESH
HEAD_DIM = 64
CLUSTER = 128
TOK = 2048
QUARTER = 512
D = 768
BLOCKS = TOK // CLUSTER
GROUP = 192
CHUNK = 128
CHUNKS = QUARTER // CHUNK
ROWS = 64
K_ROWS, Q_ROWS, V_ROWS, AUG = 0, 80, 160, 224
SLICES = (0, 3, 1, 2)
bf16, f32 = jnp.bfloat16, jnp.float32


def nn(a, b):
    return lax.dot_general(a, b, (((1,), (0,)), ((), ())), preferred_element_type=f32)


def nt(a, b):
    return lax.dot_general(a, b, (((1,), (1,)), ((), ())), preferred_element_type=f32)


def tn(a, b):
    return lax.dot_general(a, b, (((0,), (0,)), ((), ())), preferred_element_type=f32)


def diagonal(a, b):
    blank = jnp.zeros_like(a)
    return jnp.concatenate([jnp.concatenate([a, blank], axis=1), jnp.concatenate([blank, b], axis=1)], axis=0)


def remote(src, dst, send, recv, seq, tp):
    return pltpu.make_async_remote_copy(
        src_ref=src, dst_ref=dst, send_sem=send, recv_sem=recv, device_id=(seq, tp), device_id_type=MESH
    )


def place():
    s, z = lax.axis_index("seq"), lax.axis_index("tp")
    return s, z, s // 2, s % 2


def greet(columns):
    s, z, c, k = place()
    barrier = pltpu.get_barrier_semaphore()
    for step in range(1, 8):
        other = (k * 4 + z + step) % 8
        pl.semaphore_signal(barrier, inc=1, device_id=(2 * c + other // 4, other % 4), device_id_type=MESH)

    @pl.loop(1, columns)
    def _(step):
        pl.semaphore_signal(barrier, inc=1, device_id=(2 * ((c + step) % columns) + k, z), device_id_type=MESH)

    pl.semaphore_wait(barrier, 7 + columns - 1)


def rows_at(start, size, multiple):
    return pl.ds(pl.multiple_of(start, multiple), size)


def layer(
    columns, reducers, tail, far,
    x_in, groups_in, lengths, query_in, key_in, value_in, inner_in, outer_in, output_in, cot_in, vectors,
    lo_ref, dx_ref, fin_inner, fin_outer, fin_tail, dw_ref, *rest,
):
    got2, got2s, stage, stages = rest[:4] if far else (rest[0], rest[1], None, None)
    (
        g, xg, srt, share, wg, cl, slot_ref, bias, mixed, cot, ib_ref, two, gf, gb, gsend, gm, lo_src, dx_src,
        got1, got1s, got3, got3s, rd1, rd2, e1_got, e2_got, done, dones, cl_in, wt_ref, bias_in, ib_in,
        load_sem, x_send, x_recv, fwd_send, core_send, cl_sem, q_send, q_recv, b_sem, cot_sem, ib_send, ib_recv,
        w1_send, w1_recv, w2_send, w2_recv, w3_send, w3_recv, m_send, m_recv, gm_send, gm_recv, lo_sem,
        c1_send, c1_recv, c2_send, c2_recv, c3_send, c3_recv, c4_send, c4_recv, c5_send, c5_recv,
        d1_send, d1_recv, d2_send, d2_recv, d3_send, d3_recv, e1_send, e1_recv, e2_send, e2_recv, e3_send, e3_recv, e4_send, e4_recv,
    ) = rest[4 if far else 2 :]
    s, z, c, k = place()
    half, zb = z // 2, z % 2
    mate = s + 1 - 2 * k
    pair = z + 1 - 2 * zb
    across = (z + 2) % 4
    group = (z + 2 * k) % 4
    member = 2 * zb + k
    owner_seq, owner_tp = 2 * c + half, member
    own_home = (owner_seq == s) & (owner_tp == z)
    gathers = c < 4
    reduces = c < reducers
    inner, outer = 1 + k, 3 * k
    primary = k == half
    is_inner = z == inner
    scale = HEAD_DIM ** (-0.5)
    small = tail // 2
    piece, spiece = D // reducers, small // reducers
    square = columns == 4
    across_x, across_y, across_xy = c + 1 - 2 * (c % 2), (c + 2) % 4, 3 - c
    wide = [slice(256 * n, 256 * (n + 1)) for n in range(3)]
    planes = [z, pair, across, 3 - z]

    vec = [vectors[:, D * i : D * (i + 1)] for i in range(6)]

    def start(local, here, there):
        @pl.when(local)
        def _():
            here.start()

        @pl.when(jnp.logical_not(local))
        def _():
            there.start()

    def finish(local, here, there):
        @pl.when(local)
        def _():
            here.wait()

        @pl.when(jnp.logical_not(local))
        def _():
            there.wait()

    own_rows = rows_at(QUARTER * z, QUARTER, QUARTER)
    x_local = pltpu.make_async_copy(x_in, xg.at[own_rows], load_sem.at[0])
    g_loads = [
        pltpu.make_async_copy(inner_in, g.at[z, 0:D], load_sem.at[1]),
        pltpu.make_async_copy(outer_in, g.at[z, D : 2 * D], load_sem.at[2]),
        pltpu.make_async_copy(output_in, g.at[z, 2 * D : 2 * D + GROUP], load_sem.at[3]),
    ]

    @pl.when(primary)
    def _():
        x_local.start()

    for one in g_loads:
        one.start()
    g[z, 2 * D + GROUP :, :] = jnp.zeros((tail - GROUP, D), bf16)
    greet(columns)
    target = jnp.where(is_inner, outer, inner)

    def x_rows(q, j):
        return xg.at[rows_at(QUARTER * q + CHUNK * j, CHUNK, CHUNK)]

    def x_copy(j):
        return remote(x_in.at[pl.ds(CHUNK * j, CHUNK)], x_rows(z, j), x_send.at[j], x_recv.at[z, j], s, target)

    def x_forward(q, i, j):
        return remote(x_rows(q, j), x_rows(q, j), fwd_send.at[i, j], x_recv.at[q, j], s, outer)

    def x_mate(q, i, j):
        return remote(x_rows(q, j), x_rows(q, j), core_send.at[i, j], x_recv.at[q, j], mate, z)

    for j in range(CHUNKS):
        x_copy(j).start()

    spot = lax.broadcasted_iota(jnp.int32, (1, TOK), 1)
    valid = jnp.zeros((1, TOK), f32)
    first_spot = 0
    for i in range(lengths.shape[1]):
        real = lengths[0, i]
        valid += jnp.where((spot >= first_spot) & (spot < first_spot + real), 1.0, 0.0)
        first_spot += (real + CLUSTER - 1) // CLUSTER * CLUSTER
    cl_in[...] = jnp.concatenate([groups_in[...].astype(f32), valid, jnp.zeros((12, TOK), f32)], axis=0).astype(bf16)

    cl_z = 2 * k + zb
    cl_k = ((z - cl_z + 4) % 4) // 2
    cl_self = (cl_z == z) & (cl_k == k)
    cl_copy = remote(cl_in, cl, cl_sem.at[0], cl_sem.at[1], 2 * c + cl_k, cl_z)
    cl_local = pltpu.make_async_copy(cl_in, cl, cl_sem.at[1])
    start(cl_self, cl_local, cl_copy)

    for i, one in enumerate((key_in, query_in, value_in)):
        wt_ref[GROUP * i : GROUP * (i + 1), :] = one[...]
    bias_in[...] = jnp.broadcast_to(vectors[:, 7 * D :], bias_in.shape)
    ib_in[...] = jnp.broadcast_to(vectors[:, 6 * D : 7 * D], ib_in.shape)
    qrow = wt_ref.shape[0] // 4

    def wq_rows(part):
        return wg.at[rows_at(qrow * part, qrow, 16)]

    w_copy = remote(wt_ref.at[rows_at(qrow * c, qrow, 16)], wq_rows(c), q_send.at[0], q_recv.at[c], s, across)
    w_local = pltpu.make_async_copy(wt_ref, wg, q_send.at[0])
    b_copy = remote(bias_in, bias, b_sem.at[0], b_sem.at[1], s, across)
    b_local = pltpu.make_async_copy(bias_in, bias, b_sem.at[1])

    def wq_copy(turn):
        return remote(wq_rows(c), wq_rows(c), q_send.at[turn], q_recv.at[c], 2 * ((c + turn) % columns) + k, z)

    @pl.when((k == 1) & gathers)
    def _():
        w_copy.start()

    @pl.when(k == 1)
    def _():
        b_copy.start()

    @pl.when(k == 0)
    def _():
        w_local.start()
        b_local.start()

    bases, pieces = [0, 2 * D], [2 * D // 8, tail // 8]

    def w_rows(r, part, which):
        return g.at[planes[r], rows_at(bases[part] + pieces[part] * which, pieces[part], 16)]

    def w1(r, part):
        rows = w_rows(0, part, 4 * k + c)
        return remote(rows, rows, w1_send.at[part, r - 1], w1_recv.at[part, r - 1], s, planes[r])

    def w2(r, part, turn):
        rows = w_rows(r, part, 4 * k + c)
        dest = [across_x, across_y][turn - 1] if square else (c + turn) % columns
        return remote(rows, rows, w2_send.at[part, r - 1, turn - 1], w2_recv.at[part, r - 1, c], 2 * dest + k, z)

    def each_w2(r, part, action):
        if square:
            for turn in (1, 2):
                action(w2(r, part, turn))
        else:
            @pl.loop(1, columns)
            def _(turn):
                action(w2(r, part, turn))

    def w3(r, part, core):
        rows = g.at[planes[r], rows_at(bases[part] + 4 * pieces[part] * core, 4 * pieces[part], 16)]
        return remote(rows, rows, w3_send.at[part, r - 1], w3_recv.at[part, r - 1], mate, z)

    at_end = (z == 0) | (z == 3)

    def arrived_piece(r, part):
        rows = w_rows(r, part, 4 * k + c)
        return remote(rows, rows, w1_send.at[part, r - 1], w1_recv.at[part, r - 1], s, z)

    def relay_piece(r, part, index):
        rows = w_rows(r, part, 4 * k + c)
        return remote(rows, rows, w1_send.at[part, index - 1], w1_recv.at[part, index - 1], s, pair)

    def send_middle(part):
        @pl.when(gathers & at_end)
        def _():
            w1(1, part).start()
            w1(2, part).start()

        @pl.when(gathers & jnp.logical_not(at_end))
        def _():
            w1(3, part).start()

    def send_end(part):
        @pl.when(gathers & jnp.logical_not(at_end))
        def _():
            w1(1, part).start()

    def relay_ends(part):
        @pl.when(gathers & jnp.logical_not(at_end))
        def _():
            arrived_piece(3, part).wait_recv()
            w1(3, part).wait_send()
            relay_piece(3, part, 2).start()
            arrived_piece(2, part).wait_recv()
            relay_piece(2, part, 3).start()

    def spread(r, part):
        @pl.when(gathers)
        def _():
            if r == 1:
                arrived_piece(r, part).wait_recv()
            else:
                @pl.when(at_end)
                def _():
                    arrived_piece(r, part).wait_recv()

            each_w2(r, part, lambda copy: copy.start())

    def pass_piece(r, part, i):
        size = pieces[part] // 2
        dest, owner, sem = [(across_y, across_x, across_x), (across_x, across_y, 4)][i]
        rows = g.at[planes[r], rows_at(bases[part] + pieces[part] * (4 * k + owner) + size * i, size, 16)]
        return remote(rows, rows, w2_send.at[part, r - 1, 2 + i], w2_recv.at[part, r - 1, sem], 2 * dest + k, z)

    def relay_columns(r, part):
        if square:
            for i, peer in ((0, across_x), (1, across_y)):
                rows = w_rows(r, part, 4 * k + peer)
                remote(rows, rows, w1_send.at[part, 0], w2_recv.at[part, r - 1, peer], s, z).wait_recv()
                pass_piece(r, part, i).start()

    def share_core(r, part):
        if square:
            for i, sem in ((0, across_xy), (1, 4)):
                rows = g.at[planes[r], rows_at(bases[part] + pieces[part] * (4 * k + across_xy) + pieces[part] // 2 * i, pieces[part] // 2, 16)]
                remote(rows, rows, w1_send.at[part, 0], w2_recv.at[part, r - 1, sem], s, z).wait_recv()
        else:
            for peer in range(4):
                @pl.when(c != peer)
                def _():
                    rows = w_rows(r, part, 4 * k + peer)
                    remote(rows, rows, w1_send.at[part, 0], w2_recv.at[part, r - 1, peer], s, z).wait_recv()
        w3(r, part, k).start()

    def have(r, part):
        w3(r, part, 1 - k).wait_recv()

    for one in g_loads:
        one.wait()
    send_middle(1)
    send_middle(0)

    cot_k, cot_z = zb, 2 * k + half
    cot_self = (cot_k == k) & (cot_z == z)
    cot_copy = remote(cot_in, cot, cot_sem.at[0], cot_sem.at[1], 2 * c + cot_k, cot_z)
    cot_local = pltpu.make_async_copy(cot_in, cot, cot_sem.at[1])

    def ib_copy(r):
        return remote(ib_in, ib_ref.at[z], ib_send.at[r - 1], ib_recv.at[r - 1], s, planes[r])

    def bump(dst, src, rows, first=0):
        def body(t, carry):
            at = pl.ds(pl.multiple_of(first + 16 * t, 16), 16)
            from_ = pl.ds(pl.multiple_of(16 * t, 16), 16)
            dst[at, :] = (dst[at, :].astype(f32) + src[from_, :].astype(f32)).astype(bf16)
            return carry

        lax.fori_loop(0, rows // 16, body, 0)

    def core_copy(j):
        rows = rows_at(D * (1 - k), D, 16)
        return remote(g.at[j, rows], got1.at[j], c1_send.at[j], c1_recv.at[j], mate, z)

    def core_copy_small():
        rows = rows_at(2 * D + small * (1 - k), small, 16)
        return remote(g.at[:, rows], got1s, c1_send.at[4], c1_recv.at[4], mate, z)

    def column_copy(j, turn):
        dest = (c + turn) % columns
        if j < 4:
            rows = rows_at(D * k + piece * dest, piece, 16)
            return remote(g.at[j, rows], got2.at[j, turn - 1], c2_send.at[j, turn - 1], c2_recv.at[j, turn - 1], 2 * dest + k, z)
        rows = rows_at(2 * D + small * k + spiece * dest, spiece, 16)
        return remote(g.at[:, rows], got2s.at[turn - 1], c2_send.at[j, turn - 1], c2_recv.at[j, turn - 1], 2 * dest + k, z)

    def hop(j, i):
        dest, owner, part = [
            (across_x, across_x, 0), (across_x, across_xy, 0), (across_y, across_y, 1), (across_y, across_xy, 1),
            (across_y, across_y, 0), (across_x, across_x, 1),
        ][i]
        if j < 4:
            half_piece = piece // 2
            rows = rows_at(D * k + piece * owner + half_piece * part, half_piece, 16)
            return remote(g.at[j, rows], got2.at[j, i], c2_send.at[j, i], c2_recv.at[j, i], 2 * dest + k, z)
        half_piece = spiece // 2
        rows = rows_at(2 * D + small * k + spiece * owner + half_piece * part, half_piece, 16)
        return remote(g.at[:, rows], got2s.at[i], c2_send.at[j, i], c2_recv.at[j, i], 2 * dest + k, z)

    def take(j, i):
        owner, part = [(c, 0), (across_y, 0), (c, 1), (across_x, 1), (c, 0), (c, 1)][i]
        hop(j, i).wait_recv()
        if j < 4:
            bump(g.at[j], got2.at[j, i], piece // 2, D * k + piece * owner + piece // 2 * part)
        else:
            def one(q, carry):
                bump(g.at[q], got2s.at[i, q], spiece // 2, 2 * D + small * k + spiece * owner + spiece // 2 * part)
                return carry

            lax.fori_loop(0, 4, one, 0)

    def start_columns(j):
        if square:
            for i in range(4):
                hop(j, i).start()
            return

        @pl.loop(1, columns)
        def _(turn):
            @pl.when((c + turn) % columns < reducers)
            def _():
                column_copy(j, turn).start()

    def middle(j):
        if square:
            take(j, 1)
            hop(j, 4).start()
            take(j, 3)
            hop(j, 5).start()
            take(j, 0)
            take(j, 2)

    def core_add(j):
        core_copy(j).wait()
        bump(g.at[j], got1.at[j], D, D * k)
        start_columns(j)

    def core_add_small():
        core_copy_small().wait()

        def one(j, carry):
            bump(g.at[j], got1s.at[j], small, 2 * D + small * k)
            return carry

        lax.fori_loop(0, 4, one, 0)
        start_columns(4)

    mine = D * k + piece * c
    smine = 2 * D + small * k + spiece * c

    def column_add(j):
        if square:
            take(j, 4)
            take(j, 5)
            return

        @pl.when(reduces)
        def _():
            @pl.loop(1, columns)
            def _(turn):
                if j < 4:
                    column_copy(j, turn).wait_recv()
                    term = got2.at[j, turn - 1]
                    if far:
                        fetch = pltpu.make_async_copy(term, stage, load_sem.at[4])
                        fetch.start()
                        fetch.wait()
                        term = stage
                    bump(g.at[j], term, piece, mine)
                else:
                    column_copy(j, turn).wait_recv()

                    def one(i, carry):
                        term = got2s.at[turn - 1, i]
                        if far:
                            fetch = pltpu.make_async_copy(term, stages, load_sem.at[4])
                            fetch.start()
                            fetch.wait()
                            term = stages
                        bump(g.at[i], term, spiece, smine)
                        return carry

                    lax.fori_loop(0, 4, one, 0)

    def plane_rows(part):
        return rows_at(mine if part == 0 else smine, piece if part == 0 else spiece, 16)

    def plane_copy(part, r):
        got = got3 if part == 0 else got3s
        return remote(g.at[planes[r], plane_rows(part)], got.at[r - 1], c3_send.at[part, r - 1], c3_recv.at[part, r - 1], s, planes[r])

    def start_plane(part, j):
        got = got3 if part == 0 else got3s
        r = planes[j]

        @pl.when(reduces & (z != j))
        def _():
            remote(g.at[j, plane_rows(part)], got.at[r - 1], c3_send.at[part, r - 1], c3_recv.at[part, r - 1], s, j).start()

    def finish_columns(turn):
        column_add(SLICES[turn])
        start_plane(0, SLICES[turn])

    def by_core(action):
        for core, half_of in ((0, fin_inner), (1, fin_outer)):
            @pl.when(k == core)
            def _():
                action(half_of)

    def final_rows(part, column, core, half_of=fin_inner):
        if part == 0:
            return half_of.at[rows_at(piece * column, piece, 16)]
        return fin_tail.at[rows_at(small * core + spiece * column, spiece, 16)]

    def final_copy(part, turn, half_of=fin_inner):
        own = done if part == 0 else dones
        return remote(own, final_rows(part, c, k, half_of), c4_send.at[part, turn - 1], c4_recv.at[part, c], 2 * ((c + turn) % columns) + k, z)

    def final_local(part, half_of=fin_inner):
        return pltpu.make_async_copy(done if part == 0 else dones, final_rows(part, c, k, half_of), load_sem.at[6 + part])

    def finish_planes(part):
        first, size = (mine, piece) if part == 0 else (smine, spiece)
        got = got3 if part == 0 else got3s
        own = done if part == 0 else dones

        @pl.when(reduces)
        def _():
            for r in range(1, 4):
                plane_copy(part, r).wait_recv()

            def body(t, carry):
                at = pl.ds(pl.multiple_of(first + 16 * t, 16), 16)
                from_ = pl.ds(pl.multiple_of(16 * t, 16), 16)
                total = g[z, at, :].astype(f32)
                for step in range(3):
                    total += got[step, from_, :].astype(f32)
                own[from_, :] = total.astype(bf16)
                return carry

            lax.fori_loop(0, size // 16, body, 0)

            def send(half_of):
                final_local(part, half_of).start()

                @pl.loop(1, columns)
                def _(turn):
                    final_copy(part, turn, half_of).start()

            by_core(send)

    def mate_copy(part, core, half_of=fin_inner):
        rows = half_of if part == 0 else fin_tail.at[rows_at(small * core, small, 16)]
        return remote(rows, rows, c5_send.at[part], c5_recv.at[part], mate, z)

    def spread_final(part):
        for peer in range(reducers):
            @pl.when(c != peer)
            def _():
                rows = final_rows(part, peer, k)
                remote(rows, rows, c4_send.at[part, 0], c4_recv.at[part, peer], s, z).wait_recv()
        @pl.when(reduces)
        def _():
            final_local(part).wait()

        by_core(lambda half_of: mate_copy(part, k, half_of).start())

    lo_copy = remote(lo_src, lo_ref, lo_sem.at[0], lo_sem.at[1], owner_seq, owner_tp)
    lo_local = pltpu.make_async_copy(lo_src, lo_ref, lo_sem.at[1])

    def gm_copy(q, h):
        home_z = 2 * half + q % 2
        home_k = ((q - home_z + 4) % 4) // 2
        rows = slice(HEAD_DIM * h, HEAD_DIM * (h + 1))
        return remote(
            gsend.at[q, rows], gm.at[rows, rows_at(QUARTER * member, QUARTER, QUARTER)],
            gm_send.at[q, h], gm_recv.at[member, h], 2 * c + home_k, home_z,
        )

    dwb = got1.at[3, 0 : dw_ref.shape[0]]
    dxp = [got1.at[i, 0:QUARTER] for i in range(3)]
    wrow = dwb.shape[0] // reducers

    def dw_rows(ref, part):
        return ref.at[rows_at(wrow * part, wrow, 16)]

    def e1(turn):
        dest = (c + turn) % columns
        return remote(dw_rows(dwb, dest), e1_got.at[turn - 1], e1_send.at[turn - 1], e1_recv.at[turn - 1], 2 * dest + k, z)

    def attention(qt, table, onehot, rt, mx):
        finish(cl_self, cl_local, cl_copy)
        low_iota = lax.broadcasted_iota(jnp.int32, (CLUSTER, CLUSTER), 0)
        high_iota = lax.broadcasted_iota(jnp.int32, (CLUSTER, CLUSTER), 1)
        upper = jnp.concatenate([(low_iota < high_iota).astype(f32), jnp.ones((CLUSTER, CLUSTER), f32)], axis=1).astype(bf16)
        names = lax.broadcasted_iota(jnp.int32, (BLOCKS, CLUSTER), 0).astype(f32)
        base = jnp.zeros((3 * BLOCKS, CLUSTER), f32)
        slot_ref[...] = jnp.zeros_like(slot_ref)
        for b in range(BLOCKS):
            lanes = slice(CLUSTER * b, CLUSTER * (b + 1))
            block = cl[:, lanes].astype(f32)
            belongs = jnp.concatenate([(block[h : h + 1] == names).astype(f32) for h in range(3)], axis=0)
            counts = nn(belongs.astype(bf16), upper)
            seen = (counts[:, :CLUSTER] + base) * belongs
            base = base + counts[:, CLUSTER:]
            for h in range(3):
                rank = jnp.sum(seen[BLOCKS * h : BLOCKS * (h + 1)], axis=0, keepdims=True)
                slot_ref[h : h + 1, lanes] = rank
                slot_ref[h + 3 : h + 4, lanes] = block[h : h + 1]
        valid = cl[3:4, :].astype(f32)
        fill = lax.broadcasted_iota(jnp.int32, (16, TOK), 0) == 0
        mask_rows = jnp.where(fill, jnp.where(valid > 0.5, 0.0, -1e30), 0.0).astype(bf16)
        ones_rows = jnp.where(fill, 1.0, 0.0).astype(bf16)
        for h in range(3):
            qt[h, 64:80, :] = mask_rows
            qt[h, 144:160, :] = ones_rows

        def canon(q):
            return jnp.where(half == 1, 3 - q, q)

        first_half = canon(z)
        order = [z, canon(1 - first_half), canon(2), canon(3)]
        order[0] = jnp.where(primary, z, canon(0))
        order[1] = jnp.where(primary, order[1], canon(1))

        def arrived(q, j):
            return remote(x_rows(q, j), x_rows(q, j), x_send.at[0], x_recv.at[q, j], s, z)

        def pass_on():
            for j in range(CHUNKS):
                for i in (2, 3):
                    arrived(order[i], j).wait_recv()

                    @pl.when(is_inner)
                    def _():
                        x_forward(order[i], i - 2, j).start()

                    x_mate(order[i], i, j).start()

        def project(i):
            q = order[i]
            if i == 0:
                @pl.when(jnp.logical_not(primary))
                def _():
                    for j in range(CHUNKS):
                        arrived(q, j).wait_recv()
            elif i == 1:
                for j in range(CHUNKS):
                    arrived(q, j).wait_recv()

                    @pl.when(primary)
                    def _():
                        x_mate(q, 1, j).start()
            else:
                @pl.when(jnp.logical_not(primary))
                def _():
                    for j in range(CHUNKS):
                        arrived(q, j).wait_recv()
            lanes = rows_at(QUARTER * q, QUARTER, QUARTER)
            tokens = xg[lanes, :]
            found = (nt(wg[...], tokens) + bias_col).astype(bf16)
            for h in range(3):
                for place_at, i in ((K_ROWS, 0), (Q_ROWS, 1), (V_ROWS, 2)):
                    qt[h, place_at : place_at + 64, lanes] = found[GROUP * i + HEAD_DIM * h : GROUP * i + HEAD_DIM * (h + 1)]

        @pl.when(primary)
        def _():
            x_local.wait()
            for j in range(CHUNKS):
                x_mate(z, 0, j).start()

        @pl.when(is_inner)
        def _():
            pass_on()
            send_end(1)
            send_end(0)

        @pl.when(k == 0)
        def _():
            w_local.wait()
            b_local.wait()

        @pl.when((k == 1) & gathers)
        def _():
            w_copy.wait()

            @pl.loop(1, columns)
            def _(turn):
                wq_copy(turn).start()

        @pl.when(k == 1)
        def _():
            b_copy.wait()
            for peer in range(4):
                @pl.when(c != peer)
                def _():
                    remote(wq_rows(peer), wq_rows(peer), q_send.at[0], q_recv.at[peer], s, z).wait_recv()

        bias_col = jnp.transpose(bias[...], (1, 0))[0 : 3 * GROUP, 0:1]
        project(0)
        project(1)

        @pl.when(primary & jnp.logical_not(is_inner))
        def _():
            pass_on()

        project(2)
        project(3)

        @pl.when(jnp.logical_not(is_inner))
        def _():
            send_end(1)
            send_end(0)

        relay_ends(1)
        relay_ends(0)

        start(cot_self, cot_local, cot_copy)
        ib_ref[pl.ds(z, 1)] = ib_in[...][None]
        for r in range(1, 4):
            ib_copy(r).start()

        def mixed_at(h, grp):
            return mixed.at[rows_at(GROUP * grp + HEAD_DIM * h, HEAD_DIM, HEAD_DIM)]

        rank_iota = lax.broadcasted_iota(jnp.int32, (CLUSTER, TOK), 0).astype(f32)

        def head(h, carry):
            rank_row = slot_ref[pl.ds(h, 1), :]
            name_row = slot_ref[pl.ds(h + 3, 1), :]
            onehot[...] = (rank_row == rank_iota).astype(f32).astype(bf16)

            def build(b, carry):
                name = b.astype(f32)
                table[rows_at(CLUSTER * b, CLUSTER, CLUSTER), :] = onehot[...] * (name_row == name).astype(f32).astype(bf16)
                return carry

            lax.fori_loop(0, BLOCKS, build, 0)

            def sort(b, carry):
                rows = rows_at(TOK // 2 * b, TOK // 2, TOK // 2)
                srt[h, :, rows] = nt(qt[h], table[rows, :]).astype(bf16)
                return carry

            lax.fori_loop(0, 2, sort, 0)

            @pl.when(h == 0)
            def _():
                for r in range(1, 4):
                    spread(r, 1)
                spread(1, 0)

            @pl.when(h == 1)
            def _():
                spread(2, 0)

            @pl.when(h == 2)
            def _():
                spread(3, 0)
                share_core(1, 0)

            for b in range(BLOCKS):
                lanes = slice(CLUSTER * b, CLUSTER * (b + 1))
                scores = tn(srt[h, K_ROWS : K_ROWS + 80, lanes], srt[h, Q_ROWS : Q_ROWS + 80, lanes]) * scale
                top = jnp.maximum(jnp.max(scores, axis=0, keepdims=True), -1e20)
                weights = jnp.exp(scores - top)
                total = jnp.sum(weights, axis=0, keepdims=True)
                part = weights / jnp.where(total > 0.5, total, 1.0)
                share[h, b] = part
                rt[:, lanes] = nn(srt[h, V_ROWS : V_ROWS + 64, lanes], part.astype(bf16)).astype(bf16)

            def send_back(d):
                @pl.when(d == member)
                def _():
                    pltpu.make_async_copy(mx.at[h, d], mixed_at(h, group), m_recv.at[h, d]).start()

                @pl.when(d != member)
                def _():
                    remote(
                        mx.at[h, d], mixed_at(h, group), m_send.at[h, d], m_recv.at[h, member], 2 * c + d % 2, 2 * half + d // 2
                    ).start()

            def back(e, carry):
                found = nn(rt[...], table[:, rows_at(TOK // 2 * e, TOK // 2, TOK // 2)]).astype(bf16)
                for f in range(2):
                    mx[h, 2 * e + f] = found[:, QUARTER * f : QUARTER * (f + 1)]
                    send_back(2 * e + f)
                return carry

            lax.fori_loop(0, 2, back, 0)

            @pl.when(h == 1)
            def _():
                for r in range(1, 4):
                    relay_columns(r, 1)
                relay_columns(1, 0)

            @pl.when(h == 2)
            def _():
                relay_columns(2, 0)

            return carry

        lax.fori_loop(0, 3, head, 0)
        for r in range(1, 4):
            share_core(r, 1)

        def await_mixed(h, carry):
            def one(d, carry):
                grp = (2 * half + d // 2 + 2 * (d % 2)) % 4
                remote(mx.at[h, d], mixed_at(h, grp), m_send.at[h, d], m_recv.at[h, d], s, z).wait_recv()

                @pl.when(d != member)
                def _():
                    remote(mx.at[h, d], mixed_at(h, grp), m_send.at[h, d], m_recv.at[h, d], s, z).wait_send()

                return carry

            return lax.fori_loop(0, 4, one, carry)

        lax.fori_loop(0, 3, await_mixed, 0)
        relay_columns(3, 0)
        share_core(2, 0)

    pl.run_scoped(
        attention,
        pltpu.VMEM((3, AUG, TOK), bf16), pltpu.VMEM((TOK, TOK), bf16), pltpu.VMEM((CLUSTER, TOK), bf16),
        pltpu.VMEM((HEAD_DIM, TOK), bf16), pltpu.VMEM((3, 4, HEAD_DIM, QUARTER), bf16),
    )

    def feed_forward(gi, mixt, norm, rstd, low, turned, act, slope):
        for r in range(1, 4):
            have(r, 1)
        for q in range(4):
            mixt[q] = jnp.transpose(mixed[GROUP * q : GROUP * (q + 1), :], (1, 0))
        for n in wide:
            total = nn(mixt[0], g[0, 2 * D : 2 * D + GROUP, n])
            for q in range(1, 4):
                total += nn(mixt[q], g[q, 2 * D : 2 * D + GROUP, n])
            two[:, n] = total

        def mean_of(rows):
            return jnp.mean(rows, axis=-1, keepdims=True)

        def first_norm(t, carry):
            at = rows_at(ROWS * t, ROWS, ROWS)
            rows = two[at, :] + xg[rows_at(QUARTER * member + ROWS * t, ROWS, ROWS), :].astype(f32) + vec[0]
            centred = rows - mean_of(rows)
            scaled = lax.rsqrt(mean_of(centred * centred) + 1e-6)
            normed = centred * scaled
            norm[at, :] = normed
            rstd[at, :] = jnp.broadcast_to(scaled, (ROWS, 128))
            low[at, :] = (normed * vec[1] + vec[2]).astype(bf16)
            return carry

        lax.fori_loop(0, QUARTER // ROWS, first_norm, 0)

        share_core(3, 0)

        for r in range(1, 4):
            ib_copy(r).wait_send()
            remote(ib_in, ib_ref.at[planes[r]], ib_send.at[r - 1], ib_recv.at[r - 1], s, z).wait_recv()

        def forward_slice(step, carry):
            j = jnp.where(step == 0, z, jnp.where(step == 1, pair, jnp.where(step == 2, across, 3 - z)))
            for r in range(1, 4):
                @pl.when(step == r)
                def _():
                    have(r, 0)

            for n in wide:
                slope[j, :, n] = nn(low[...], g[j, 0:D, n]) + ib_ref[j, 0:1, n]

            def bend(t, carry):
                at = rows_at(ROWS * t, ROWS, ROWS)
                v = slope[j, at, :]
                phi = 0.5 + 0.5 * lax.erf(v * (0.5 ** 0.5))
                act[j, at, :] = (v * phi).astype(bf16)
                slope[j, at, :] = phi + v * (jnp.exp(v * v * -0.5) * 0.3989422804014327)
                return carry

            lax.fori_loop(0, QUARTER // ROWS, bend, 0)

            for n in wide:
                part = nn(act[j], g[j, D : 2 * D, n])

                @pl.when(step == 0)
                def _():
                    two[:, n] = part

                @pl.when(step > 0)
                def _():
                    two[:, n] += part

            return carry

        lax.fori_loop(0, 4, forward_slice, 0)

        for part in range(2):
            for r in range(1, 4):
                w3(r, part, k).wait_send()

                @pl.when(gathers)
                def _():
                    if r < 3:
                        w1(r, part).wait_send()
                    else:
                        @pl.when(jnp.logical_not(at_end))
                        def _():
                            w1(r, part).wait_send()

                    each_w2(r, part, lambda copy: copy.wait_send())

                if square:
                    for i in range(2):
                        pass_piece(r, part, i).wait_send()

        finish(cot_self, cot_local, cot_copy)

        zero_row = jnp.zeros((1, D), f32)

        def second_norm(t, carry):
            gain_sum, shift_sum, bias_sum = carry
            at = rows_at(ROWS * t, ROWS, ROWS)
            rows = norm[at, :] * vec[1] + vec[2] + two[at, :] + vec[3]
            centred = rows - mean_of(rows)
            scaled = lax.rsqrt(mean_of(centred * centred) + 1e-6)
            normed = centred * scaled
            lo_src[at, :] = (normed * vec[4] + vec[5]).astype(bf16)
            up = cot[at, :].astype(f32)
            e = up * vec[4]
            grad = (e - mean_of(e) - normed * mean_of(e * normed)) * scaled
            two[at, :] = grad
            grad_low = grad.astype(bf16)
            gb[at, :] = grad_low
            return (
                gain_sum + jnp.sum(up * normed, axis=0, keepdims=True),
                shift_sum + jnp.sum(up, axis=0, keepdims=True),
                bias_sum + jnp.sum(grad_low.astype(f32), axis=0, keepdims=True),
            )

        gain2, shift2, outer_bias = lax.fori_loop(0, QUARTER // ROWS, second_norm, (zero_row, zero_row, zero_row))

        start(own_home, lo_local, lo_copy)

        turned[...] = jnp.transpose(low[...], (1, 0))
        inner_bias = {}
        for turn, j in enumerate(SLICES):
            sums = []
            for n in wide:
                found = (nt(gb[...], g[j, D + n.start : D + n.stop, :]) * slope[j, :, n]).astype(bf16)
                gi[:, n] = found
                sums.append(jnp.sum(found.astype(f32), axis=0, keepdims=True))
            inner_bias[j] = jnp.concatenate(sums, axis=1)
            act_turned = jnp.transpose(act[j], (1, 0))
            for n in wide:
                g[j, D : 2 * D, n] = nn(act_turned, gb[:, n]).astype(bf16)
            for n in wide:
                part = nt(gi[...], g[j, n.start : n.stop, :])
                gf[:, n] = part if turn == 0 else gf[:, n] + part
            for n in wide:
                g[j, 0:D, n] = nn(turned[...], gi[:, n]).astype(bf16)
            core_copy(j).start()
            if turn > 0:
                core_add(SLICES[turn - 1])

        def first_back(t, carry):
            gain_sum, shift_sum, bias_sum = carry
            at = rows_at(ROWS * t, ROWS, ROWS)
            up = two[at, :] + gf[at, :]
            e = up * vec[1]
            normed = norm[at, :]
            grad = (e - mean_of(e) - normed * mean_of(e * normed)) * rstd[at, 0:1]
            two[at, :] = grad
            grad_low = grad.astype(bf16)
            gb[at, :] = grad_low
            return (
                gain_sum + jnp.sum(up * normed, axis=0, keepdims=True),
                shift_sum + jnp.sum(up, axis=0, keepdims=True),
                bias_sum + jnp.sum(grad_low.astype(f32), axis=0, keepdims=True),
            )

        gain1, shift1, output_bias = lax.fori_loop(0, QUARTER // ROWS, first_back, (zero_row, zero_row, zero_row))

        for q in range(4):
            gsend[q] = nt(g[q, 2 * D : 2 * D + GROUP, :], gb[...]).astype(bf16)

            @pl.when(group == q)
            def _():
                gm[:, rows_at(QUARTER * member, QUARTER, QUARTER)] = gsend[q]

        for h in range(3):
            for q in range(4):
                @pl.when(group != q)
                def _():
                    gm_copy(q, h).start()

        middle(SLICES[0])
        head_rows = jnp.concatenate([gain2, shift2, outer_bias, gain1, shift1, output_bias], axis=0)
        for q in range(4):
            g[q, 2 * D : 2 * D + GROUP, :] = nn(mixed[GROUP * q : GROUP * (q + 1), :], gb[...]).astype(bf16)
            g[q, 2 * D + GROUP : 2 * D + GROUP + 16, :] = jnp.concatenate(
                [head_rows, inner_bias[q], jnp.zeros((9, D), f32)], axis=0
            ).astype(bf16)
        core_copy_small().start()
        core_add(SLICES[3])

    pl.run_scoped(
        feed_forward,
        pltpu.VMEM((QUARTER, D), bf16), pltpu.VMEM((4, QUARTER, GROUP), bf16), pltpu.VMEM((QUARTER, D), f32), pltpu.VMEM((QUARTER, 128), f32),
        pltpu.VMEM((QUARTER, D), bf16), pltpu.VMEM((D, QUARTER), bf16), pltpu.VMEM((4, QUARTER, D), bf16), pltpu.VMEM((4, QUARTER, D), f32),
    )

    def attention_back(table, onehot, gs, ds, dt):
        rank_iota = lax.broadcasted_iota(jnp.int32, (CLUSTER, TOK), 0).astype(f32)

        def head(h, carry):
            rank_row = slot_ref[pl.ds(h, 1), :]
            for m in range(4):
                @pl.when(m != member)
                def _():
                    part = gm.at[rows_at(HEAD_DIM * h, HEAD_DIM, HEAD_DIM), QUARTER * m : QUARTER * (m + 1)]
                    remote(part, part, gm_send.at[0, 0], gm_recv.at[m, h], s, z).wait_recv()

            name_row = slot_ref[pl.ds(h + 3, 1), :]
            onehot[...] = (rank_row == rank_iota).astype(f32).astype(bf16)

            def build(b, carry):
                name = b.astype(f32)
                table[rows_at(CLUSTER * b, CLUSTER, CLUSTER), :] = onehot[...] * (name_row == name).astype(f32).astype(bf16)
                return carry

            lax.fori_loop(0, BLOCKS, build, 0)

            def sort(b, carry):
                rows = rows_at(TOK // 2 * b, TOK // 2, TOK // 2)
                gs[:, rows] = nt(gm[rows_at(HEAD_DIM * h, HEAD_DIM, HEAD_DIM), :], table[rows, :]).astype(bf16)
                return carry

            lax.fori_loop(0, 2, sort, 0)

            @pl.when(h == 1)
            def _():
                middle(SLICES[2])

            @pl.when(h == 2)
            def _():
                middle(SLICES[3])
                finish_columns(1)

            for b in range(BLOCKS // 2):
                lanes = slice(2 * CLUSTER * b, 2 * CLUSTER * (b + 1))
                grad = gs[:, lanes]
                grad_part = tn(srt[h, V_ROWS : V_ROWS + 64, lanes], grad)
                scores, probs = [], []
                for e in range(2):
                    at = slice(CLUSTER * e, CLUSTER * (e + 1))
                    part = share[h, 2 * b + e]
                    block = grad_part[at, at]
                    inside = jnp.sum(block * part, axis=0, keepdims=True)
                    scores.append((part * (block - inside)).astype(bf16))
                    probs.append(part.astype(bf16))
                scores, probs = diagonal(*scores), diagonal(*probs)
                ds[0:64, lanes] = (nt(srt[h, Q_ROWS : Q_ROWS + 64, lanes], scores) * scale).astype(bf16)
                ds[64:128, lanes] = (nn(srt[h, K_ROWS : K_ROWS + 64, lanes], scores) * scale).astype(bf16)
                ds[128:192, lanes] = nt(grad, probs).astype(bf16)

            def back(d, carry):
                rows = rows_at(TOK // 2 * d, TOK // 2, TOK // 2)
                found = nn(ds[...], table[:, rows]).astype(bf16)
                for i in range(3):
                    dt[rows_at(GROUP * i + HEAD_DIM * h, HEAD_DIM, HEAD_DIM), rows] = found[HEAD_DIM * i : HEAD_DIM * (i + 1)]
                return carry

            lax.fori_loop(0, 2, back, 0)

            @pl.when(h == 0)
            def _():
                core_add_small()
                middle(SLICES[1])
                finish_columns(0)

            @pl.when(h == 2)
            def _():
                middle(4)
                finish_columns(2)

            return carry

        lax.fori_loop(0, 3, head, 0)


        here = 2 * zb
        there = 2 * (1 - zb)

        def partial_rows(quarter, n):
            return tn(dt[:, rows_at(QUARTER * quarter, QUARTER, QUARTER)], wg[:, n])

        def d1(i):
            return remote(dxp[i], rd1.at[i], d1_send.at[i], d1_recv.at[i], mate, z)

        def d2(i):
            rows = slice(CHUNK * i, CHUNK * (i + 1))
            return remote(dxp[2].at[rows], rd2.at[rows], d2_send.at[i], d2_recv.at[i], s, pair)

        def d3(i):
            rows = slice(CHUNK * i, CHUNK * (i + 1))
            return remote(dx_src.at[rows], dx_ref.at[rows], d3_send.at[i], d3_recv.at[i], owner_seq, owner_tp)

        def d3_local(i):
            rows = slice(CHUNK * i, CHUNK * (i + 1))
            return pltpu.make_async_copy(dx_src.at[rows], dx_ref.at[rows], d3_recv.at[i])

        for n in wide:
            dxp[0][:, n] = partial_rows(there + 1 - k, n).astype(bf16)
        d1(0).start()
        for n in wide:
            gf[:, n] = partial_rows(there + k, n)
        d1(0).wait_recv()
        for i in range(CHUNKS):
            def add_there(t, carry):
                at = rows_at(CHUNK * i + 16 * t, 16, 16)
                dxp[2][at, :] = (gf[at, :] + rd1[0, at, :].astype(f32)).astype(bf16)
                return carry

            lax.fori_loop(0, CHUNK // 16, add_there, 0)
            d2(i).start()
        for n in wide:
            dxp[1][:, n] = partial_rows(here + 1 - k, n).astype(bf16)
        d1(1).start()
        for n in wide:
            two[:, n] += partial_rows(here + k, n)
        d1(1).wait_recv()

        for n in wide:
            dwb[0 : 3 * GROUP, n] = nn(dt[...], xg[:, n]).astype(bf16)
        ones = jnp.ones((16, TOK), bf16)
        dwb[3 * GROUP : 3 * GROUP + 16, 0 : 3 * GROUP] = nt(ones, dt[...]).astype(bf16)
        dwb[3 * GROUP : 3 * GROUP + 16, 3 * GROUP :] = jnp.zeros((16, D - 3 * GROUP), bf16)
        dwb[3 * GROUP + 16 :, :] = jnp.zeros((dwb.shape[0] - 3 * GROUP - 16, D), bf16)

        @pl.loop(1, columns)
        def _(turn):
            @pl.when((c + turn) % columns < reducers)
            def _():
                e1(turn).start()


        def finish_tokens(i):
            d2(i).wait_recv()

            def add_here(t, carry):
                at = rows_at(CHUNK * i + 16 * t, 16, 16)
                dx_src[at, :] = (two[at, :] + rd1[1, at, :].astype(f32) + rd2[at, :].astype(f32)).astype(bf16)
                return carry

            lax.fori_loop(0, CHUNK // 16, add_here, 0)
            start(own_home, d3_local(i), d3(i))

        finish_tokens(0)
        finish_columns(3)
        column_add(4)
        for j in range(4):
            start_plane(1, j)
        for i in range(1, CHUNKS):
            finish_tokens(i)

        @pl.when(reduces)
        def _():
            @pl.loop(1, columns)
            def _(turn):
                e1(turn).wait_recv()
                bump(dwb, e1_got.at[turn - 1], wrow, wrow * c)

        e2 = remote(dw_rows(dwb, c), e2_got, e2_send.at[0], e2_recv.at[0], s - 1, across)

        def e3(turn):
            return remote(dw_rows(dw_ref, c), dw_rows(dw_ref, c), e3_send.at[turn - 1], e3_recv.at[c], 2 * ((c + turn) % columns) + k, z)

        e4 = remote(dw_ref, dw_ref, e4_send.at[0], e4_recv.at[0], mate, z)

        @pl.when(reduces & (k == 1))
        def _():
            e2.start()

        finish_planes(0)
        finish_planes(1)

        @pl.when(reduces & (k == 0))
        def _():
            remote(e2_got, e2_got, e2_send.at[0], e2_recv.at[0], s, z).wait_recv()

            def add_dw(t, carry):
                at = rows_at(wrow * c + 16 * t, 16, 16)
                from_ = rows_at(16 * t, 16, 16)
                dw_ref[at, :] = (dwb[at, :].astype(f32) + e2_got[from_, :].astype(f32)).astype(bf16)
                return carry

            lax.fori_loop(0, wrow // 16, add_dw, 0)

            @pl.loop(1, columns)
            def _(turn):
                e3(turn).start()

        spread_final(0)
        spread_final(1)

        @pl.when(k == 0)
        def _():
            for peer in range(reducers):
                @pl.when(c != peer)
                def _():
                    remote(dw_rows(dw_ref, peer), dw_rows(dw_ref, peer), e3_send.at[0], e3_recv.at[peer], s, z).wait_recv()
            e4.start()
            e4.wait_send()

        @pl.when(k == 1)
        def _():
            e4.wait_recv()

        @pl.when(reduces & (k == 1))
        def _():
            e2.wait_send()

        @pl.when(reduces & (k == 0))
        def _():
            @pl.loop(1, columns)
            def _(turn):
                e3(turn).wait_send()

        @pl.loop(1, columns)
        def _(turn):
            @pl.when((c + turn) % columns < reducers)
            def _():
                e1(turn).wait_send()
                if not square:
                    for j in range(5):
                        column_copy(j, turn).wait_send()

        if square:
            for j in range(5):
                for i in range(6):
                    hop(j, i).wait_send()

        for part in range(2):
            @pl.when(reduces)
            def _():
                for r in range(1, 4):
                    plane_copy(part, r).wait_send()

                @pl.loop(1, columns)
                def _(turn):
                    final_copy(part, turn).wait_send()

            mate_copy(part, k).wait_send()
            mate_copy(part, 1 - k).wait_recv()

        finish(own_home, lo_local, lo_copy)
        for i in range(CHUNKS):
            finish(own_home, d3_local(i), d3(i))
        for q in range(4):
            @pl.when(group != q)
            def _():
                for h in range(3):
                    gm_copy(q, h).wait_send()
        for i in range(2):
            d1(i).wait_send()
        for i in range(CHUNKS):
            d2(i).wait_send()

        for j in range(CHUNKS):
            x_copy(j).wait_send()

            @pl.when(primary)
            def _():
                for i in range(4):
                    x_mate(0, i, j).wait_send()

            @pl.when(is_inner)
            def _():
                for i in range(2):
                    x_forward(0, i, j).wait_send()

        @pl.when((k == 1) & gathers)
        def _():
            @pl.loop(1, columns)
            def _(turn):
                wq_copy(turn).wait_send()

    pl.run_scoped(
        attention_back,
        pltpu.VMEM((TOK, TOK), bf16), pltpu.VMEM((CLUSTER, TOK), bf16), pltpu.VMEM((HEAD_DIM, TOK), bf16), pltpu.VMEM((GROUP, TOK), bf16),
        pltpu.VMEM((3 * GROUP, TOK), bf16),
    )


def layer_call(columns, reducers, tail, *arrays):
    vmem = pl.BlockSpec(memory_space=pltpu.VMEM)
    smem = pl.BlockSpec(memory_space=pltpu.SMEM)
    anyspec = pl.BlockSpec(memory_space=pl.ANY)
    dma = pltpu.SemaphoreType.DMA
    rows = 2 * D + tail
    piece, spiece = D // reducers, tail // 2 // reducers
    turns = columns - 1
    wide = 16 * reducers * -(-(3 * GROUP + 16) // (16 * reducers))
    far = columns > 4
    low = lambda *shape: pltpu.VMEM(shape, bf16)
    full = lambda *shape: pltpu.VMEM(shape, f32)
    out = lambda *shape: jax.ShapeDtypeStruct(shape, bf16)
    terms, sterms = (4, turns, piece, D), (turns, 4, spiece, D)
    if columns == 4:
        terms, sterms = (4, 6, piece // 2, D), (6, 4, spiece // 2, D)
    return pl.pallas_call(
        functools.partial(layer, columns, reducers, tail, far),
        out_shape=[out(QUARTER, D), out(QUARTER, D), out(D, D), out(D, D), out(tail, D), out(wide, D)]
        + ([out(*terms), out(*sterms)] if far else []),
        in_specs=[anyspec, vmem, smem] + [vmem] * 3 + [anyspec] * 4 + [vmem],
        out_specs=[anyspec] * 5 + [vmem] + ([anyspec] * 2 if far else []),
        scratch_shapes=([low(piece, D), low(spiece, D)] if far else [low(*terms), low(*sterms)])
        + [
            low(4, rows, D), low(TOK, D), low(3, AUG, TOK), full(3, BLOCKS, CLUSTER, CLUSTER), low(3 * GROUP, D), low(16, TOK),
            full(8, TOK), full(8, 640), low(D, QUARTER), low(QUARTER, D), full(4, 8, D),
            full(QUARTER, D), full(QUARTER, D), low(QUARTER, D), low(4, GROUP, QUARTER), low(GROUP, TOK), low(QUARTER, D), low(QUARTER, D),
            low(4, D, D), low(4, tail // 2, D), low(3, piece, D), low(3, spiece, D),
            low(2, QUARTER, D), low(QUARTER, D), low(turns, wide // reducers, D), low(wide // reducers, D), low(piece, D), low(spiece, D),
            low(16, TOK), low(3 * GROUP, D), full(8, 640), full(8, D),
            dma((8,)), dma((CHUNKS,)), dma((4, CHUNKS)), dma((2, CHUNKS)), dma((4, CHUNKS)), dma((2,)), dma((columns,)), dma((4,)),
            dma((2,)), dma((2,)), dma((3,)), dma((3,)),
            dma((2, 3)), dma((2, 3)), dma((2, 3, max(turns, 4))), dma((2, 3, 5)), dma((2, 3)), dma((2, 3)), dma((3, 4)), dma((3, 4)),
            dma((4, 3)), dma((4, 3)), dma((2,)),
            dma((5,)), dma((5,)), dma((5, max(turns, 6))), dma((5, max(turns, 6))), dma((2, 3)), dma((2, 3)), dma((2, turns)), dma((2, reducers)),
            dma((2,)), dma((2,)), dma((2,)), dma((2,)), dma((CHUNKS,)), dma((CHUNKS,)), dma((CHUNKS,)), dma((CHUNKS,)),
            dma((turns,)), dma((turns,)), dma((1,)), dma((1,)), dma((turns,)), dma((reducers,)), dma((1,)), dma((1,)),
        ],
        compiler_params=pltpu.CompilerParams(collective_id=0, has_side_effects=True, vmem_limit_bytes=63 * 2**20),
    )(*arrays)


def shards(
    layer_input, clusters, document_lengths, query_weight, key_weight, value_weight, query_bias, value_bias, output_weight,
    output_bias, first_gain, first_shift, inner_weight, inner_bias, outer_weight, outer_bias, second_gain, second_shift, cotangent,
):
    columns = lax.axis_size("seq") // 2
    reducers = min(columns, 16)
    tail = 32 * reducers * -(-(GROUP + 16) // (32 * reducers))
    vectors = jnp.concatenate(
        [output_bias, first_gain, first_shift, outer_bias, second_gain, second_shift, inner_bias]
        + [jnp.zeros((GROUP,), f32), query_bias, value_bias, jnp.zeros((64,), f32)]
    ).reshape(1, -1)
    lo, dx, fin_inner, fin_outer, fin_tail, dw, *_ = layer_call(
        columns, reducers, tail, layer_input, clusters.T, document_lengths, query_weight.T, key_weight.T, value_weight.T,
        inner_weight, outer_weight, output_weight, cotangent, vectors,
    )
    turned = lambda i: dw[GROUP * i : GROUP * (i + 1)].astype(f32).T
    bias_row = dw[3 * GROUP].astype(f32)
    sums = fin_tail[GROUP : GROUP + 16].astype(f32)
    return (
        lo,
        dx.astype(f32),
        turned(1),
        turned(0),
        turned(2),
        bias_row[GROUP : 2 * GROUP],
        bias_row[2 * GROUP : 3 * GROUP],
        fin_tail[:GROUP].astype(f32),
        sums[5],
        sums[3],
        sums[4],
        fin_inner.astype(f32),
        sums[6],
        fin_outer.astype(f32),
        sums[2],
        sums[0],
        sums[1],
    )


def solution(mesh):
    rows, cols = P(("seq", "tp"), None), P(None, "tp")
    return jax.shard_map(
        shards,
        mesh=mesh,
        in_specs=(
            rows, P("seq", "tp"), P("seq", None), cols, cols, cols, P("tp"), P("tp"), P("tp", None), P(), P(), P(),
            cols, P("tp"), P("tp", None), P(), P(), P(), rows,
        ),
        out_specs=(
            rows, rows, cols, cols, cols, P("tp"), P("tp"), P("tp", None), P(), P(), P(), cols, P("tp"), P("tp", None), P(), P(), P(),
        ),
        check_vma=False,
    )
```

```python
import functools
import jax
import jax.numpy as jnp
from jax import lax
from jax.experimental import pallas as pl
from jax.experimental.pallas import tpu as pltpu
from jax.sharding import PartitionSpec as P

MESH = pl.DeviceIdType.MESH
HEAD_DIM = 64
CLUSTER = 128
TOK = 2048
QUARTER = 512
D = 768
BLOCKS = TOK // CLUSTER
GROUP = 192
CHUNK = 128
CHUNKS = QUARTER // CHUNK
ROWS = 64
K_ROWS, Q_ROWS, V_ROWS, AUG = 0, 80, 160, 224
SLICES = (0, 3, 1, 2)
bf16, f32 = jnp.bfloat16, jnp.float32


def nn(a, b):
    return lax.dot_general(a, b, (((1,), (0,)), ((), ())), preferred_element_type=f32)


def nt(a, b):
    return lax.dot_general(a, b, (((1,), (1,)), ((), ())), preferred_element_type=f32)


def tn(a, b):
    return lax.dot_general(a, b, (((0,), (0,)), ((), ())), preferred_element_type=f32)


def diagonal(a, b):
    blank = jnp.zeros_like(a)
    return jnp.concatenate([jnp.concatenate([a, blank], axis=1), jnp.concatenate([blank, b], axis=1)], axis=0)


def remote(src, dst, send, recv, seq, tp):
    return pltpu.make_async_remote_copy(
        src_ref=src, dst_ref=dst, send_sem=send, recv_sem=recv, device_id=(seq, tp), device_id_type=MESH
    )


class Dummy:
    def start(self): pass
    def wait(self): pass
    def wait_send(self): pass
    def wait_recv(self): pass
def dummy(*a): return Dummy()


def place():
    s, z = lax.axis_index("seq"), lax.axis_index("tp")
    return s, z, s // 2, s % 2


def greet(columns):
    s, z, c, k = place()
    barrier = pltpu.get_barrier_semaphore()
    for step in range(1, 8):
        other = (k * 4 + z + step) % 8
        pl.semaphore_signal(barrier, inc=1, device_id=(2 * c + other // 4, other % 4), device_id_type=MESH)

    @pl.loop(1, columns)
    def _(step):
        pl.semaphore_signal(barrier, inc=1, device_id=(2 * ((c + step) % columns) + k, z), device_id_type=MESH)

    pl.semaphore_wait(barrier, 7 + columns - 1)


def rows_at(start, size, multiple):
    return pl.ds(pl.multiple_of(start, multiple), size)


def layer(
    columns, reducers, tail, far,
    x_in, groups_in, lengths, query_in, key_in, value_in, inner_in, outer_in, output_in, cot_in, vectors,
    lo_ref, dx_ref, fin_inner, fin_outer, fin_tail, dw_ref, *rest,
):
    got2, got2s, stage, stages = rest[:4] if far else (rest[0], rest[1], None, None)
    (
        g, xg, srt, share, wg, cl, slot_ref, bias, mixed, cot, ib_ref, two, gf, gb, gsend, gm, lo_src, dx_src,
        got1, got1s, got3, got3s, rd1, rd2, e1_got, e2_got, done, dones, cl_in, wt_ref, bias_in, ib_in,
        load_sem, x_send, x_recv, fwd_send, core_send, cl_sem, q_send, q_recv, b_sem, cot_sem, ib_send, ib_recv,
        w1_send, w1_recv, w2_send, w2_recv, w3_send, w3_recv, m_send, m_recv, gm_send, gm_recv, lo_sem,
        c1_send, c1_recv, c2_send, c2_recv, c3_send, c3_recv, c4_send, c4_recv, c5_send, c5_recv,
        d1_send, d1_recv, d2_send, d2_recv, d3_send, d3_recv, e1_send, e1_recv, e2_send, e2_recv, e3_send, e3_recv, e4_send, e4_recv,
    ) = rest[4 if far else 2 :]
    s, z, c, k = place()
    half, zb = z // 2, z % 2
    mate = s + 1 - 2 * k
    pair = z + 1 - 2 * zb
    across = (z + 2) % 4
    group = (z + 2 * k) % 4
    member = 2 * zb + k
    owner_seq, owner_tp = 2 * c + half, member
    own_home = (owner_seq == s) & (owner_tp == z)
    gathers = c < 4
    reduces = c < reducers
    inner, outer = 1 + k, 3 * k
    primary = k == half
    is_inner = z == inner
    scale = HEAD_DIM ** (-0.5)
    small = tail // 2
    piece, spiece = D // reducers, small // reducers
    square = columns == 4
    across_x, across_y, across_xy = c + 1 - 2 * (c % 2), (c + 2) % 4, 3 - c
    wide = [slice(256 * n, 256 * (n + 1)) for n in range(3)]
    planes = [z, pair, across, 3 - z]

    vec = [vectors[:, D * i : D * (i + 1)] for i in range(6)]

    def start(local, here, there):
        @pl.when(local)
        def _():
            here.start()

        @pl.when(jnp.logical_not(local))
        def _():
            there.start()

    def finish(local, here, there):
        @pl.when(local)
        def _():
            here.wait()

        @pl.when(jnp.logical_not(local))
        def _():
            there.wait()

    own_rows = rows_at(QUARTER * z, QUARTER, QUARTER)
    x_local = pltpu.make_async_copy(x_in, xg.at[own_rows], load_sem.at[0])
    g_loads = [
        pltpu.make_async_copy(inner_in, g.at[z, 0:D], load_sem.at[1]),
        pltpu.make_async_copy(outer_in, g.at[z, D : 2 * D], load_sem.at[2]),
        pltpu.make_async_copy(output_in, g.at[z, 2 * D : 2 * D + GROUP], load_sem.at[3]),
    ]

    @pl.when(primary)
    def _():
        x_local.start()

    for one in g_loads:
        one.start()
    g[z, 2 * D + GROUP :, :] = jnp.zeros((tail - GROUP, D), bf16)
    greet(columns)
    target = jnp.where(is_inner, outer, inner)

    def x_rows(q, j):
        return xg.at[rows_at(QUARTER * q + CHUNK * j, CHUNK, CHUNK)]

    def x_copy(j):
        return remote(x_in.at[pl.ds(CHUNK * j, CHUNK)], x_rows(z, j), x_send.at[j], x_recv.at[z, j], s, target)

    def x_forward(q, i, j):
        return remote(x_rows(q, j), x_rows(q, j), fwd_send.at[i, j], x_recv.at[q, j], s, outer)

    def x_mate(q, i, j):
        return remote(x_rows(q, j), x_rows(q, j), core_send.at[i, j], x_recv.at[q, j], mate, z)

    for j in range(CHUNKS):
        x_copy(j).start()

    spot = lax.broadcasted_iota(jnp.int32, (1, TOK), 1)
    valid = jnp.zeros((1, TOK), f32)
    first_spot = 0
    for i in range(lengths.shape[1]):
        real = lengths[0, i]
        valid += jnp.where((spot >= first_spot) & (spot < first_spot + real), 1.0, 0.0)
        first_spot += (real + CLUSTER - 1) // CLUSTER * CLUSTER
    cl_in[...] = jnp.concatenate([groups_in[...].astype(f32), valid, jnp.zeros((12, TOK), f32)], axis=0).astype(bf16)

    cl_z = 2 * k + zb
    cl_k = ((z - cl_z + 4) % 4) // 2
    cl_self = (cl_z == z) & (cl_k == k)
    cl_copy = remote(cl_in, cl, cl_sem.at[0], cl_sem.at[1], 2 * c + cl_k, cl_z)
    cl_local = pltpu.make_async_copy(cl_in, cl, cl_sem.at[1])
    start(cl_self, cl_local, cl_copy)

    for i, one in enumerate((key_in, query_in, value_in)):
        wt_ref[GROUP * i : GROUP * (i + 1), :] = one[...]
    bias_in[...] = jnp.broadcast_to(vectors[:, 7 * D :], bias_in.shape)
    ib_in[...] = jnp.broadcast_to(vectors[:, 6 * D : 7 * D], ib_in.shape)
    qrow = wt_ref.shape[0] // 4

    def wq_rows(part):
        return wg.at[rows_at(qrow * part, qrow, 16)]

    w_copy = remote(wt_ref.at[rows_at(qrow * c, qrow, 16)], wq_rows(c), q_send.at[0], q_recv.at[c], s, across)
    w_local = pltpu.make_async_copy(wt_ref, wg, q_send.at[0])
    b_copy = remote(bias_in, bias, b_sem.at[0], b_sem.at[1], s, across)
    b_local = pltpu.make_async_copy(bias_in, bias, b_sem.at[1])

    def wq_copy(turn):
        return remote(wq_rows(c), wq_rows(c), q_send.at[turn], q_recv.at[c], 2 * ((c + turn) % columns) + k, z)

    @pl.when((k == 1) & gathers)
    def _():
        w_copy.start()

    @pl.when(k == 1)
    def _():
        b_copy.start()

    @pl.when(k == 0)
    def _():
        w_local.start()
        b_local.start()

    bases, pieces = [0, 2 * D], [2 * D // 8, tail // 8]

    def w_rows(r, part, which):
        return g.at[planes[r], rows_at(bases[part] + pieces[part] * which, pieces[part], 16)]

    def w1(r, part):
        rows = w_rows(0, part, 4 * k + c)
        return remote(rows, rows, w1_send.at[part, r - 1], w1_recv.at[part, r - 1], s, planes[r])

    def w2(r, part, turn):
        rows = w_rows(r, part, 4 * k + c)
        dest = [across_x, across_y][turn - 1] if square else (c + turn) % columns
        return remote(rows, rows, w2_send.at[part, r - 1, turn - 1], w2_recv.at[part, r - 1, c], 2 * dest + k, z)

    def each_w2(r, part, action):
        if square:
            for turn in (1, 2):
                action(w2(r, part, turn))
        else:
            @pl.loop(1, columns)
            def _(turn):
                action(w2(r, part, turn))

    def w3(r, part, core):
        rows = g.at[planes[r], rows_at(bases[part] + 4 * pieces[part] * core, 4 * pieces[part], 16)]
        return remote(rows, rows, w3_send.at[part, r - 1], w3_recv.at[part, r - 1], mate, z)

    at_end = (z == 0) | (z == 3)

    def arrived_piece(r, part):
        rows = w_rows(r, part, 4 * k + c)
        return remote(rows, rows, w1_send.at[part, r - 1], w1_recv.at[part, r - 1], s, z)

    def relay_piece(r, part, index):
        rows = w_rows(r, part, 4 * k + c)
        return remote(rows, rows, w1_send.at[part, index - 1], w1_recv.at[part, index - 1], s, pair)

    def send_middle(part):
        @pl.when(gathers & at_end)
        def _():
            w1(1, part).start()
            w1(2, part).start()

        @pl.when(gathers & jnp.logical_not(at_end))
        def _():
            w1(3, part).start()

    def send_end(part):
        @pl.when(gathers & jnp.logical_not(at_end))
        def _():
            w1(1, part).start()

    def relay_ends(part):
        @pl.when(gathers & jnp.logical_not(at_end))
        def _():
            arrived_piece(3, part).wait_recv()
            w1(3, part).wait_send()
            relay_piece(3, part, 2).start()
            arrived_piece(2, part).wait_recv()
            relay_piece(2, part, 3).start()

    def spread(r, part):
        @pl.when(gathers)
        def _():
            if r == 1:
                arrived_piece(r, part).wait_recv()
            else:
                @pl.when(at_end)
                def _():
                    arrived_piece(r, part).wait_recv()

            each_w2(r, part, lambda copy: copy.start())

    def pass_piece(r, part, i):
        size = pieces[part] // 2
        dest, owner, sem = [(across_y, across_x, across_x), (across_x, across_y, 4)][i]
        rows = g.at[planes[r], rows_at(bases[part] + pieces[part] * (4 * k + owner) + size * i, size, 16)]
        return remote(rows, rows, w2_send.at[part, r - 1, 2 + i], w2_recv.at[part, r - 1, sem], 2 * dest + k, z)

    def relay_columns(r, part):
        if square:
            for i, peer in ((0, across_x), (1, across_y)):
                rows = w_rows(r, part, 4 * k + peer)
                remote(rows, rows, w1_send.at[part, 0], w2_recv.at[part, r - 1, peer], s, z).wait_recv()
                pass_piece(r, part, i).start()

    def share_core(r, part):
        if square:
            for i, sem in ((0, across_xy), (1, 4)):
                rows = g.at[planes[r], rows_at(bases[part] + pieces[part] * (4 * k + across_xy) + pieces[part] // 2 * i, pieces[part] // 2, 16)]
                remote(rows, rows, w1_send.at[part, 0], w2_recv.at[part, r - 1, sem], s, z).wait_recv()
        else:
            for peer in range(4):
                @pl.when(c != peer)
                def _():
                    rows = w_rows(r, part, 4 * k + peer)
                    remote(rows, rows, w1_send.at[part, 0], w2_recv.at[part, r - 1, peer], s, z).wait_recv()
        w3(r, part, k).start()

    def have(r, part):
        w3(r, part, 1 - k).wait_recv()

    for one in g_loads:
        one.wait()
    send_middle(1)
    send_middle(0)

    cot_k, cot_z = zb, 2 * k + half
    cot_self = (cot_k == k) & (cot_z == z)
    cot_copy = remote(cot_in, cot, cot_sem.at[0], cot_sem.at[1], 2 * c + cot_k, cot_z)
    cot_local = pltpu.make_async_copy(cot_in, cot, cot_sem.at[1])

    def ib_copy(r):
        return remote(ib_in, ib_ref.at[z], ib_send.at[r - 1], ib_recv.at[r - 1], s, planes[r])

    def bump(dst, src, rows, first=0):
        def body(t, carry):
            at = pl.ds(pl.multiple_of(first + 16 * t, 16), 16)
            from_ = pl.ds(pl.multiple_of(16 * t, 16), 16)
            dst[at, :] = (dst[at, :].astype(f32) + src[from_, :].astype(f32)).astype(bf16)
            return carry

        lax.fori_loop(0, rows // 16, body, 0)

    def core_copy(j):
        rows = rows_at(D * (1 - k), D, 16)
        return remote(g.at[j, rows], got1.at[j], c1_send.at[j], c1_recv.at[j], mate, z)

    def core_copy_small():
        rows = rows_at(2 * D + small * (1 - k), small, 16)
        return remote(g.at[:, rows], got1s, c1_send.at[4], c1_recv.at[4], mate, z)

    def column_copy(j, turn):
        dest = (c + turn) % columns
        if j < 4:
            rows = rows_at(D * k + piece * dest, piece, 16)
            return remote(g.at[j, rows], got2.at[j, turn - 1], c2_send.at[j, turn - 1], c2_recv.at[j, turn - 1], 2 * dest + k, z)
        rows = rows_at(2 * D + small * k + spiece * dest, spiece, 16)
        return remote(g.at[:, rows], got2s.at[turn - 1], c2_send.at[j, turn - 1], c2_recv.at[j, turn - 1], 2 * dest + k, z)

    def hop(j, i):
        dest, owner, part = [
            (across_x, across_x, 0), (across_x, across_xy, 0), (across_y, across_y, 1), (across_y, across_xy, 1),
            (across_y, across_y, 0), (across_x, across_x, 1),
        ][i]
        if j < 4:
            half_piece = piece // 2
            rows = rows_at(D * k + piece * owner + half_piece * part, half_piece, 16)
            return remote(g.at[j, rows], got2.at[j, i], c2_send.at[j, i], c2_recv.at[j, i], 2 * dest + k, z)
        half_piece = spiece // 2
        rows = rows_at(2 * D + small * k + spiece * owner + half_piece * part, half_piece, 16)
        return remote(g.at[:, rows], got2s.at[i], c2_send.at[j, i], c2_recv.at[j, i], 2 * dest + k, z)

    def take(j, i):
        owner, part = [(c, 0), (across_y, 0), (c, 1), (across_x, 1), (c, 0), (c, 1)][i]
        hop(j, i).wait_recv()
        if j < 4:
            bump(g.at[j], got2.at[j, i], piece // 2, D * k + piece * owner + piece // 2 * part)
        else:
            def one(q, carry):
                bump(g.at[q], got2s.at[i, q], spiece // 2, 2 * D + small * k + spiece * owner + spiece // 2 * part)
                return carry

            lax.fori_loop(0, 4, one, 0)

    def start_columns(j):
        if square:
            for i in range(4):
                hop(j, i).start()
            return

        @pl.loop(1, columns)
        def _(turn):
            @pl.when((c + turn) % columns < reducers)
            def _():
                column_copy(j, turn).start()

    def middle(j):
        if square:
            take(j, 1)
            hop(j, 4).start()
            take(j, 3)
            hop(j, 5).start()
            take(j, 0)
            take(j, 2)

    def core_add(j):
        core_copy(j).wait()
        bump(g.at[j], got1.at[j], D, D * k)
        start_columns(j)

    def core_add_small():
        core_copy_small().wait()

        def one(j, carry):
            bump(g.at[j], got1s.at[j], small, 2 * D + small * k)
            return carry

        lax.fori_loop(0, 4, one, 0)
        start_columns(4)

    mine = D * k + piece * c
    smine = 2 * D + small * k + spiece * c

    def column_add(j):
        if square:
            take(j, 4)
            take(j, 5)
            return

        @pl.when(reduces)
        def _():
            @pl.loop(1, columns)
            def _(turn):
                if j < 4:
                    column_copy(j, turn).wait_recv()
                    term = got2.at[j, turn - 1]
                    if far:
                        fetch = pltpu.make_async_copy(term, stage, load_sem.at[4])
                        fetch.start()
                        fetch.wait()
                        term = stage
                    bump(g.at[j], term, piece, mine)
                else:
                    column_copy(j, turn).wait_recv()

                    def one(i, carry):
                        term = got2s.at[turn - 1, i]
                        if far:
                            fetch = pltpu.make_async_copy(term, stages, load_sem.at[4])
                            fetch.start()
                            fetch.wait()
                            term = stages
                        bump(g.at[i], term, spiece, smine)
                        return carry

                    lax.fori_loop(0, 4, one, 0)

    def plane_rows(part):
        return rows_at(mine if part == 0 else smine, piece if part == 0 else spiece, 16)

    def plane_copy(part, r):
        got = got3 if part == 0 else got3s
        return remote(g.at[planes[r], plane_rows(part)], got.at[r - 1], c3_send.at[part, r - 1], c3_recv.at[part, r - 1], s, planes[r])

    def start_plane(part, j):
        got = got3 if part == 0 else got3s
        r = planes[j]

        @pl.when(reduces & (z != j))
        def _():
            remote(g.at[j, plane_rows(part)], got.at[r - 1], c3_send.at[part, r - 1], c3_recv.at[part, r - 1], s, j).start()

    def finish_columns(turn):
        column_add(SLICES[turn])
        start_plane(0, SLICES[turn])

    def by_core(action):
        for core, half_of in ((0, fin_inner), (1, fin_outer)):
            @pl.when(k == core)
            def _():
                action(half_of)

    def final_rows(part, column, core, half_of=fin_inner):
        if part == 0:
            return half_of.at[rows_at(piece * column, piece, 16)]
        return fin_tail.at[rows_at(small * core + spiece * column, spiece, 16)]

    def final_copy(part, turn, half_of=fin_inner):
        own = done if part == 0 else dones
        return remote(own, final_rows(part, c, k, half_of), c4_send.at[part, turn - 1], c4_recv.at[part, c], 2 * ((c + turn) % columns) + k, z)

    def final_local(part, half_of=fin_inner):
        return pltpu.make_async_copy(done if part == 0 else dones, final_rows(part, c, k, half_of), load_sem.at[6 + part])

    def finish_planes(part):
        first, size = (mine, piece) if part == 0 else (smine, spiece)
        got = got3 if part == 0 else got3s
        own = done if part == 0 else dones

        @pl.when(reduces)
        def _():
            for r in range(1, 4):
                plane_copy(part, r).wait_recv()

            def body(t, carry):
                at = pl.ds(pl.multiple_of(first + 16 * t, 16), 16)
                from_ = pl.ds(pl.multiple_of(16 * t, 16), 16)
                total = g[z, at, :].astype(f32)
                for step in range(3):
                    total += got[step, from_, :].astype(f32)
                own[from_, :] = total.astype(bf16)
                return carry

            lax.fori_loop(0, size // 16, body, 0)

            def send(half_of):
                final_local(part, half_of).start()

                @pl.loop(1, columns)
                def _(turn):
                    final_copy(part, turn, half_of).start()

            by_core(send)

    def mate_copy(part, core, half_of=fin_inner):
        rows = half_of if part == 0 else fin_tail.at[rows_at(small * core, small, 16)]
        return remote(rows, rows, c5_send.at[part], c5_recv.at[part], mate, z)

    def spread_final(part):
        for peer in range(reducers):
            @pl.when(c != peer)
            def _():
                rows = final_rows(part, peer, k)
                remote(rows, rows, c4_send.at[part, 0], c4_recv.at[part, peer], s, z).wait_recv()
        @pl.when(reduces)
        def _():
            final_local(part).wait()

        by_core(lambda half_of: mate_copy(part, k, half_of).start())

    lo_copy = remote(lo_src, lo_ref, lo_sem.at[0], lo_sem.at[1], owner_seq, owner_tp)
    lo_local = pltpu.make_async_copy(lo_src, lo_ref, lo_sem.at[1])

    def gm_copy(q, h):
        home_z = 2 * half + q % 2
        home_k = ((q - home_z + 4) % 4) // 2
        rows = slice(HEAD_DIM * h, HEAD_DIM * (h + 1))
        return remote(
            gsend.at[q, rows], gm.at[rows, rows_at(QUARTER * member, QUARTER, QUARTER)],
            gm_send.at[q, h], gm_recv.at[member, h], 2 * c + home_k, home_z,
        )

    dwb = got1.at[3, 0 : dw_ref.shape[0]]
    dxp = [got1.at[i, 0:QUARTER] for i in range(3)]
    wrow = dwb.shape[0] // reducers

    def dw_rows(ref, part):
        return ref.at[rows_at(wrow * part, wrow, 16)]

    def e1(turn):
        dest = (c + turn) % columns
        return remote(dw_rows(dwb, dest), e1_got.at[turn - 1], e1_send.at[turn - 1], e1_recv.at[turn - 1], 2 * dest + k, z)

    def attention(qt, table, onehot, rt, mx):
        finish(cl_self, cl_local, cl_copy)
        low_iota = lax.broadcasted_iota(jnp.int32, (CLUSTER, CLUSTER), 0)
        high_iota = lax.broadcasted_iota(jnp.int32, (CLUSTER, CLUSTER), 1)
        upper = jnp.concatenate([(low_iota < high_iota).astype(f32), jnp.ones((CLUSTER, CLUSTER), f32)], axis=1).astype(bf16)
        names = lax.broadcasted_iota(jnp.int32, (BLOCKS, CLUSTER), 0).astype(f32)
        base = jnp.zeros((3 * BLOCKS, CLUSTER), f32)
        slot_ref[...] = jnp.zeros_like(slot_ref)
        for b in range(BLOCKS):
            lanes = slice(CLUSTER * b, CLUSTER * (b + 1))
            block = cl[:, lanes].astype(f32)
            belongs = jnp.concatenate([(block[h : h + 1] == names).astype(f32) for h in range(3)], axis=0)
            counts = nn(belongs.astype(bf16), upper)
            seen = (counts[:, :CLUSTER] + base) * belongs
            base = base + counts[:, CLUSTER:]
            for h in range(3):
                rank = jnp.sum(seen[BLOCKS * h : BLOCKS * (h + 1)], axis=0, keepdims=True)
                slot_ref[h : h + 1, lanes] = rank
                slot_ref[h + 3 : h + 4, lanes] = block[h : h + 1]
        valid = cl[3:4, :].astype(f32)
        fill = lax.broadcasted_iota(jnp.int32, (16, TOK), 0) == 0
        mask_rows = jnp.where(fill, jnp.where(valid > 0.5, 0.0, -1e30), 0.0).astype(bf16)
        ones_rows = jnp.where(fill, 1.0, 0.0).astype(bf16)
        for h in range(3):
            qt[h, 64:80, :] = mask_rows
            qt[h, 144:160, :] = ones_rows

        def canon(q):
            return jnp.where(half == 1, 3 - q, q)

        first_half = canon(z)
        order = [z, canon(1 - first_half), canon(2), canon(3)]
        order[0] = jnp.where(primary, z, canon(0))
        order[1] = jnp.where(primary, order[1], canon(1))

        def arrived(q, j):
            return remote(x_rows(q, j), x_rows(q, j), x_send.at[0], x_recv.at[q, j], s, z)

        def pass_on():
            for j in range(CHUNKS):
                for i in (2, 3):
                    arrived(order[i], j).wait_recv()

                    @pl.when(is_inner)
                    def _():
                        x_forward(order[i], i - 2, j).start()

                    x_mate(order[i], i, j).start()

        def project(i):
            q = order[i]
            if i == 0:
                @pl.when(jnp.logical_not(primary))
                def _():
                    for j in range(CHUNKS):
                        arrived(q, j).wait_recv()
            elif i == 1:
                for j in range(CHUNKS):
                    arrived(q, j).wait_recv()

                    @pl.when(primary)
                    def _():
                        x_mate(q, 1, j).start()
            else:
                @pl.when(jnp.logical_not(primary))
                def _():
                    for j in range(CHUNKS):
                        arrived(q, j).wait_recv()
            lanes = rows_at(QUARTER * q, QUARTER, QUARTER)
            tokens = xg[lanes, :]
            found = (nt(wg[...], tokens) + bias_col).astype(bf16)
            for h in range(3):
                for place_at, i in ((K_ROWS, 0), (Q_ROWS, 1), (V_ROWS, 2)):
                    qt[h, place_at : place_at + 64, lanes] = found[GROUP * i + HEAD_DIM * h : GROUP * i + HEAD_DIM * (h + 1)]

        @pl.when(primary)
        def _():
            x_local.wait()
            for j in range(CHUNKS):
                x_mate(z, 0, j).start()

        @pl.when(is_inner)
        def _():
            pass_on()
            send_end(1)
            send_end(0)

        @pl.when(k == 0)
        def _():
            w_local.wait()
            b_local.wait()

        @pl.when((k == 1) & gathers)
        def _():
            w_copy.wait()

            @pl.loop(1, columns)
            def _(turn):
                wq_copy(turn).start()

        @pl.when(k == 1)
        def _():
            b_copy.wait()
            for peer in range(4):
                @pl.when(c != peer)
                def _():
                    remote(wq_rows(peer), wq_rows(peer), q_send.at[0], q_recv.at[peer], s, z).wait_recv()

        bias_col = jnp.transpose(bias[...], (1, 0))[0 : 3 * GROUP, 0:1]
        project(0)
        project(1)

        @pl.when(primary & jnp.logical_not(is_inner))
        def _():
            pass_on()

        project(2)
        project(3)

        @pl.when(jnp.logical_not(is_inner))
        def _():
            send_end(1)
            send_end(0)

        relay_ends(1)
        relay_ends(0)

        start(cot_self, cot_local, cot_copy)
        ib_ref[pl.ds(z, 1)] = ib_in[...][None]
        for r in range(1, 4):
            ib_copy(r).start()

        def mixed_at(h, grp):
            return mixed.at[rows_at(GROUP * grp + HEAD_DIM * h, HEAD_DIM, HEAD_DIM)]

        rank_iota = lax.broadcasted_iota(jnp.int32, (CLUSTER, TOK), 0).astype(f32)

        def head(h, carry):
            rank_row = slot_ref[pl.ds(h, 1), :]
            name_row = slot_ref[pl.ds(h + 3, 1), :]
            onehot[...] = (rank_row == rank_iota).astype(f32).astype(bf16)

            def build(b, carry):
                name = b.astype(f32)
                table[rows_at(CLUSTER * b, CLUSTER, CLUSTER), :] = onehot[...] * (name_row == name).astype(f32).astype(bf16)
                return carry

            lax.fori_loop(0, BLOCKS, build, 0)

            def sort(b, carry):
                rows = rows_at(TOK // 2 * b, TOK // 2, TOK // 2)
                srt[h, :, rows] = nt(qt[h], table[rows, :]).astype(bf16)
                return carry

            lax.fori_loop(0, 2, sort, 0)

            @pl.when(h == 0)
            def _():
                for r in range(1, 4):
                    spread(r, 1)
                spread(1, 0)

            @pl.when(h == 1)
            def _():
                spread(2, 0)

            @pl.when(h == 2)
            def _():
                spread(3, 0)
                share_core(1, 0)

            for b in range(BLOCKS):
                lanes = slice(CLUSTER * b, CLUSTER * (b + 1))
                scores = tn(srt[h, K_ROWS : K_ROWS + 80, lanes], srt[h, Q_ROWS : Q_ROWS + 80, lanes]) * scale
                top = jnp.maximum(jnp.max(scores, axis=0, keepdims=True), -1e20)
                weights = jnp.exp(scores - top)
                total = jnp.sum(weights, axis=0, keepdims=True)
                part = weights / jnp.where(total > 0.5, total, 1.0)
                share[h, b] = part
                rt[:, lanes] = nn(srt[h, V_ROWS : V_ROWS + 64, lanes], part.astype(bf16)).astype(bf16)

            def send_back(d):
                @pl.when(d == member)
                def _():
                    pltpu.make_async_copy(mx.at[h, d], mixed_at(h, group), m_recv.at[h, d]).start()

                @pl.when(d != member)
                def _():
                    remote(
                        mx.at[h, d], mixed_at(h, group), m_send.at[h, d], m_recv.at[h, member], 2 * c + d % 2, 2 * half + d // 2
                    ).start()

            def back(e, carry):
                found = nn(rt[...], table[:, rows_at(TOK // 2 * e, TOK // 2, TOK // 2)]).astype(bf16)
                for f in range(2):
                    mx[h, 2 * e + f] = found[:, QUARTER * f : QUARTER * (f + 1)]
                    send_back(2 * e + f)
                return carry

            lax.fori_loop(0, 2, back, 0)

            @pl.when(h == 1)
            def _():
                for r in range(1, 4):
                    relay_columns(r, 1)
                relay_columns(1, 0)

            @pl.when(h == 2)
            def _():
                relay_columns(2, 0)

            return carry

        lax.fori_loop(0, 3, head, 0)
        for r in range(1, 4):
            share_core(r, 1)

        def await_mixed(h, carry):
            def one(d, carry):
                grp = (2 * half + d // 2 + 2 * (d % 2)) % 4
                remote(mx.at[h, d], mixed_at(h, grp), m_send.at[h, d], m_recv.at[h, d], s, z).wait_recv()

                @pl.when(d != member)
                def _():
                    remote(mx.at[h, d], mixed_at(h, grp), m_send.at[h, d], m_recv.at[h, d], s, z).wait_send()

                return carry

            return lax.fori_loop(0, 4, one, carry)

        lax.fori_loop(0, 3, await_mixed, 0)
        relay_columns(3, 0)
        share_core(2, 0)

    pl.run_scoped(
        attention,
        pltpu.VMEM((3, AUG, TOK), bf16), pltpu.VMEM((TOK, TOK), bf16), pltpu.VMEM((CLUSTER, TOK), bf16),
        pltpu.VMEM((HEAD_DIM, TOK), bf16), pltpu.VMEM((3, 4, HEAD_DIM, QUARTER), bf16),
    )

    def feed_forward(gi, mixt, norm, rstd, low, turned, act, slope):
        for r in range(1, 4):
            have(r, 1)
        for q in range(4):
            mixt[q] = jnp.transpose(mixed[GROUP * q : GROUP * (q + 1), :], (1, 0))
        for n in wide:
            total = nn(mixt[0], g[0, 2 * D : 2 * D + GROUP, n])
            for q in range(1, 4):
                total += nn(mixt[q], g[q, 2 * D : 2 * D + GROUP, n])
            two[:, n] = total

        def mean_of(rows):
            return jnp.mean(rows, axis=-1, keepdims=True)

        def first_norm(t, carry):
            at = rows_at(ROWS * t, ROWS, ROWS)
            rows = two[at, :] + xg[rows_at(QUARTER * member + ROWS * t, ROWS, ROWS), :].astype(f32) + vec[0]
            centred = rows - mean_of(rows)
            scaled = lax.rsqrt(mean_of(centred * centred) + 1e-6)
            normed = centred * scaled
            norm[at, :] = normed
            rstd[at, :] = jnp.broadcast_to(scaled, (ROWS, 128))
            low[at, :] = (normed * vec[1] + vec[2]).astype(bf16)
            return carry

        lax.fori_loop(0, QUARTER // ROWS, first_norm, 0)

        for r in range(1, 4):
            ib_copy(r).wait_send()
            remote(ib_in, ib_ref.at[planes[r]], ib_send.at[r - 1], ib_recv.at[r - 1], s, z).wait_recv()

        def forward_slice(step, carry):
            j = jnp.where(step == 0, z, jnp.where(step == 1, pair, jnp.where(step == 2, across, 3 - z)))
            for r in range(1, 4):
                @pl.when(step == r)
                def _():
                    have(r, 0)

            for n in wide:
                slope[j, :, n] = nn(low[...], g[j, 0:D, n]) + ib_ref[j, 0:1, n]

            def bend(t, carry):
                at = rows_at(ROWS * t, ROWS, ROWS)
                v = slope[j, at, :]
                phi = 0.5 + 0.5 * lax.erf(v * (0.5 ** 0.5))
                act[j, at, :] = (v * phi).astype(bf16)
                slope[j, at, :] = phi + v * (jnp.exp(v * v * -0.5) * 0.3989422804014327)
                return carry

            lax.fori_loop(0, QUARTER // ROWS, bend, 0)

            @pl.when(step == 0)
            def _():
                share_core(3, 0)

            for n in wide:
                part = nn(act[j], g[j, D : 2 * D, n])

                @pl.when(step == 0)
                def _():
                    two[:, n] = part

                @pl.when(step > 0)
                def _():
                    two[:, n] += part

            return carry

        lax.fori_loop(0, 4, forward_slice, 0)

        for part in range(2):
            for r in range(1, 4):
                w3(r, part, k).wait_send()

                @pl.when(gathers)
                def _():
                    if r < 3:
                        w1(r, part).wait_send()
                    else:
                        @pl.when(jnp.logical_not(at_end))
                        def _():
                            w1(r, part).wait_send()

                    each_w2(r, part, lambda copy: copy.wait_send())

                if square:
                    for i in range(2):
                        pass_piece(r, part, i).wait_send()

        finish(cot_self, cot_local, cot_copy)

        zero_row = jnp.zeros((1, D), f32)

        def second_norm(t, carry):
            gain_sum, shift_sum, bias_sum = carry
            at = rows_at(ROWS * t, ROWS, ROWS)
            rows = norm[at, :] * vec[1] + vec[2] + two[at, :] + vec[3]
            centred = rows - mean_of(rows)
            scaled = lax.rsqrt(mean_of(centred * centred) + 1e-6)
            normed = centred * scaled
            lo_src[at, :] = (normed * vec[4] + vec[5]).astype(bf16)
            up = cot[at, :].astype(f32)
            e = up * vec[4]
            grad = (e - mean_of(e) - normed * mean_of(e * normed)) * scaled
            two[at, :] = grad
            grad_low = grad.astype(bf16)
            gb[at, :] = grad_low
            return (
                gain_sum + jnp.sum(up * normed, axis=0, keepdims=True),
                shift_sum + jnp.sum(up, axis=0, keepdims=True),
                bias_sum + jnp.sum(grad_low.astype(f32), axis=0, keepdims=True),
            )

        gain2, shift2, outer_bias = lax.fori_loop(0, QUARTER // ROWS, second_norm, (zero_row, zero_row, zero_row))

        start(own_home, lo_local, lo_copy)

        turned[...] = jnp.transpose(low[...], (1, 0))
        inner_bias = {}
        for turn, j in enumerate(SLICES):
            sums = []
            for n in wide:
                found = (nt(gb[...], g[j, D + n.start : D + n.stop, :]) * slope[j, :, n]).astype(bf16)
                gi[:, n] = found
                sums.append(jnp.sum(found.astype(f32), axis=0, keepdims=True))
            inner_bias[j] = jnp.concatenate(sums, axis=1)
            act_turned = jnp.transpose(act[j], (1, 0))
            for n in wide:
                g[j, D : 2 * D, n] = nn(act_turned, gb[:, n]).astype(bf16)
            for n in wide:
                part = nt(gi[...], g[j, n.start : n.stop, :])
                gf[:, n] = part if turn == 0 else gf[:, n] + part
            for n in wide:
                g[j, 0:D, n] = nn(turned[...], gi[:, n]).astype(bf16)
            core_copy(j).start()
            if turn > 0:
                core_add(SLICES[turn - 1])

        def first_back(t, carry):
            gain_sum, shift_sum, bias_sum = carry
            at = rows_at(ROWS * t, ROWS, ROWS)
            up = two[at, :] + gf[at, :]
            e = up * vec[1]
            normed = norm[at, :]
            grad = (e - mean_of(e) - normed * mean_of(e * normed)) * rstd[at, 0:1]
            two[at, :] = grad
            grad_low = grad.astype(bf16)
            gb[at, :] = grad_low
            return (
                gain_sum + jnp.sum(up * normed, axis=0, keepdims=True),
                shift_sum + jnp.sum(up, axis=0, keepdims=True),
                bias_sum + jnp.sum(grad_low.astype(f32), axis=0, keepdims=True),
            )

        gain1, shift1, output_bias = lax.fori_loop(0, QUARTER // ROWS, first_back, (zero_row, zero_row, zero_row))

        for q in range(4):
            gsend[q] = nt(g[q, 2 * D : 2 * D + GROUP, :], gb[...]).astype(bf16)

            @pl.when(group == q)
            def _():
                gm[:, rows_at(QUARTER * member, QUARTER, QUARTER)] = gsend[q]

        for h in range(3):
            for q in range(4):
                @pl.when(group != q)
                def _():
                    gm_copy(q, h).start()

        middle(SLICES[0])
        head_rows = jnp.concatenate([gain2, shift2, outer_bias, gain1, shift1, output_bias], axis=0)
        for q in range(4):
            g[q, 2 * D : 2 * D + GROUP, :] = nn(mixed[GROUP * q : GROUP * (q + 1), :], gb[...]).astype(bf16)
            g[q, 2 * D + GROUP : 2 * D + GROUP + 16, :] = jnp.concatenate(
                [head_rows, inner_bias[q], jnp.zeros((9, D), f32)], axis=0
            ).astype(bf16)
        core_copy_small().start()
        core_add(SLICES[3])

    pl.run_scoped(
        feed_forward,
        pltpu.VMEM((QUARTER, D), bf16), pltpu.VMEM((4, QUARTER, GROUP), bf16), pltpu.VMEM((QUARTER, D), f32), pltpu.VMEM((QUARTER, 128), f32),
        pltpu.VMEM((QUARTER, D), bf16), pltpu.VMEM((D, QUARTER), bf16), pltpu.VMEM((4, QUARTER, D), bf16), pltpu.VMEM((4, QUARTER, D), f32),
    )

    def attention_back(table, onehot, gs, ds, dt):
        rank_iota = lax.broadcasted_iota(jnp.int32, (CLUSTER, TOK), 0).astype(f32)

        def head(h, carry):
            rank_row = slot_ref[pl.ds(h, 1), :]
            for m in range(4):
                @pl.when(m != member)
                def _():
                    part = gm.at[rows_at(HEAD_DIM * h, HEAD_DIM, HEAD_DIM), QUARTER * m : QUARTER * (m + 1)]
                    remote(part, part, gm_send.at[0, 0], gm_recv.at[m, h], s, z).wait_recv()

            name_row = slot_ref[pl.ds(h + 3, 1), :]
            onehot[...] = (rank_row == rank_iota).astype(f32).astype(bf16)

            def build(b, carry):
                name = b.astype(f32)
                table[rows_at(CLUSTER * b, CLUSTER, CLUSTER), :] = onehot[...] * (name_row == name).astype(f32).astype(bf16)
                return carry

            lax.fori_loop(0, BLOCKS, build, 0)

            def sort(b, carry):
                rows = rows_at(TOK // 2 * b, TOK // 2, TOK // 2)
                gs[:, rows] = nt(gm[rows_at(HEAD_DIM * h, HEAD_DIM, HEAD_DIM), :], table[rows, :]).astype(bf16)
                return carry

            lax.fori_loop(0, 2, sort, 0)

            @pl.when(h == 1)
            def _():
                middle(SLICES[2])

            @pl.when(h == 2)
            def _():
                middle(SLICES[3])
                finish_columns(1)

            for b in range(BLOCKS // 2):
                lanes = slice(2 * CLUSTER * b, 2 * CLUSTER * (b + 1))
                grad = gs[:, lanes]
                grad_part = tn(srt[h, V_ROWS : V_ROWS + 64, lanes], grad)
                scores, probs = [], []
                for e in range(2):
                    at = slice(CLUSTER * e, CLUSTER * (e + 1))
                    part = share[h, 2 * b + e]
                    block = grad_part[at, at]
                    inside = jnp.sum(block * part, axis=0, keepdims=True)
                    scores.append((part * (block - inside)).astype(bf16))
                    probs.append(part.astype(bf16))
                scores, probs = diagonal(*scores), diagonal(*probs)
                ds[0:64, lanes] = (nt(srt[h, Q_ROWS : Q_ROWS + 64, lanes], scores) * scale).astype(bf16)
                ds[64:128, lanes] = (nn(srt[h, K_ROWS : K_ROWS + 64, lanes], scores) * scale).astype(bf16)
                ds[128:192, lanes] = nt(grad, probs).astype(bf16)

            def back(d, carry):
                rows = rows_at(TOK // 2 * d, TOK // 2, TOK // 2)
                found = nn(ds[...], table[:, rows]).astype(bf16)
                for i in range(3):
                    dt[rows_at(GROUP * i + HEAD_DIM * h, HEAD_DIM, HEAD_DIM), rows] = found[HEAD_DIM * i : HEAD_DIM * (i + 1)]
                return carry

            lax.fori_loop(0, 2, back, 0)

            @pl.when(h == 0)
            def _():
                core_add_small()
                middle(SLICES[1])
                finish_columns(0)

            @pl.when(h == 2)
            def _():
                middle(4)
                finish_columns(2)

            return carry

        lax.fori_loop(0, 3, head, 0)


        here = 2 * zb
        there = 2 * (1 - zb)

        def partial_rows(quarter, n):
            return tn(dt[:, rows_at(QUARTER * quarter, QUARTER, QUARTER)], wg[:, n])

        def d1(i):
            return remote(dxp[i], rd1.at[i], d1_send.at[i], d1_recv.at[i], mate, z)

        def d2(i):
            rows = slice(CHUNK * i, CHUNK * (i + 1))
            return remote(dxp[2].at[rows], rd2.at[rows], d2_send.at[i], d2_recv.at[i], s, pair)

        def d3(i):
            rows = slice(CHUNK * i, CHUNK * (i + 1))
            return remote(dx_src.at[rows], dx_ref.at[rows], d3_send.at[i], d3_recv.at[i], owner_seq, owner_tp)

        def d3_local(i):
            rows = slice(CHUNK * i, CHUNK * (i + 1))
            return pltpu.make_async_copy(dx_src.at[rows], dx_ref.at[rows], d3_recv.at[i])

        for n in wide:
            dxp[0][:, n] = partial_rows(there + 1 - k, n).astype(bf16)
        d1(0).start()
        for n in wide:
            gf[:, n] = partial_rows(there + k, n)
        d1(0).wait_recv()
        for i in range(CHUNKS):
            def add_there(t, carry):
                at = rows_at(CHUNK * i + 16 * t, 16, 16)
                dxp[2][at, :] = (gf[at, :] + rd1[0, at, :].astype(f32)).astype(bf16)
                return carry

            lax.fori_loop(0, CHUNK // 16, add_there, 0)
            d2(i).start()
        for n in wide:
            dxp[1][:, n] = partial_rows(here + 1 - k, n).astype(bf16)
        d1(1).start()
        for n in wide:
            two[:, n] += partial_rows(here + k, n)
        d1(1).wait_recv()

        for n in wide:
            dwb[0 : 3 * GROUP, n] = nn(dt[...], xg[:, n]).astype(bf16)
        ones = jnp.ones((16, TOK), bf16)
        dwb[3 * GROUP : 3 * GROUP + 16, 0 : 3 * GROUP] = nt(ones, dt[...]).astype(bf16)
        dwb[3 * GROUP : 3 * GROUP + 16, 3 * GROUP :] = jnp.zeros((16, D - 3 * GROUP), bf16)
        dwb[3 * GROUP + 16 :, :] = jnp.zeros((dwb.shape[0] - 3 * GROUP - 16, D), bf16)

        @pl.loop(1, columns)
        def _(turn):
            @pl.when((c + turn) % columns < reducers)
            def _():
                e1(turn).start()


        def finish_tokens(i):
            d2(i).wait_recv()

            def add_here(t, carry):
                at = rows_at(CHUNK * i + 16 * t, 16, 16)
                dx_src[at, :] = (two[at, :] + rd1[1, at, :].astype(f32) + rd2[at, :].astype(f32)).astype(bf16)
                return carry

            lax.fori_loop(0, CHUNK // 16, add_here, 0)
            start(own_home, d3_local(i), d3(i))

        finish_tokens(0)
        finish_columns(3)
        column_add(4)
        for j in range(4):
            start_plane(1, j)
        for i in range(1, CHUNKS):
            finish_tokens(i)

        @pl.when(reduces)
        def _():
            @pl.loop(1, columns)
            def _(turn):
                e1(turn).wait_recv()
                bump(dwb, e1_got.at[turn - 1], wrow, wrow * c)

        e2 = remote(dw_rows(dwb, c), e2_got, e2_send.at[0], e2_recv.at[0], s - 1, across)

        def e3(turn):
            return remote(dw_rows(dw_ref, c), dw_rows(dw_ref, c), e3_send.at[turn - 1], e3_recv.at[c], 2 * ((c + turn) % columns) + k, z)

        e4 = remote(dw_ref, dw_ref, e4_send.at[0], e4_recv.at[0], mate, z)

        @pl.when(reduces & (k == 1))
        def _():
            e2.start()

        finish_planes(0)
        finish_planes(1)

        @pl.when(reduces & (k == 0))
        def _():
            remote(e2_got, e2_got, e2_send.at[0], e2_recv.at[0], s, z).wait_recv()

            def add_dw(t, carry):
                at = rows_at(wrow * c + 16 * t, 16, 16)
                from_ = rows_at(16 * t, 16, 16)
                dw_ref[at, :] = (dwb[at, :].astype(f32) + e2_got[from_, :].astype(f32)).astype(bf16)
                return carry

            lax.fori_loop(0, wrow // 16, add_dw, 0)

            @pl.loop(1, columns)
            def _(turn):
                e3(turn).start()

        spread_final(0)
        spread_final(1)

        @pl.when(k == 0)
        def _():
            for peer in range(reducers):
                @pl.when(c != peer)
                def _():
                    remote(dw_rows(dw_ref, peer), dw_rows(dw_ref, peer), e3_send.at[0], e3_recv.at[peer], s, z).wait_recv()
            e4.start()
            e4.wait_send()

        @pl.when(k == 1)
        def _():
            e4.wait_recv()

        @pl.when(reduces & (k == 1))
        def _():
            e2.wait_send()

        @pl.when(reduces & (k == 0))
        def _():
            @pl.loop(1, columns)
            def _(turn):
                e3(turn).wait_send()

        @pl.loop(1, columns)
        def _(turn):
            @pl.when((c + turn) % columns < reducers)
            def _():
                e1(turn).wait_send()
                if not square:
                    for j in range(5):
                        column_copy(j, turn).wait_send()

        if square:
            for j in range(5):
                for i in range(6):
                    hop(j, i).wait_send()

        for part in range(2):
            @pl.when(reduces)
            def _():
                for r in range(1, 4):
                    plane_copy(part, r).wait_send()

                @pl.loop(1, columns)
                def _(turn):
                    final_copy(part, turn).wait_send()

            mate_copy(part, k).wait_send()
            mate_copy(part, 1 - k).wait_recv()

        finish(own_home, lo_local, lo_copy)
        for i in range(CHUNKS):
            finish(own_home, d3_local(i), d3(i))
        for q in range(4):
            @pl.when(group != q)
            def _():
                for h in range(3):
                    gm_copy(q, h).wait_send()
        for i in range(2):
            d1(i).wait_send()
        for i in range(CHUNKS):
            d2(i).wait_send()

        for j in range(CHUNKS):
            x_copy(j).wait_send()

            @pl.when(primary)
            def _():
                for i in range(4):
                    x_mate(0, i, j).wait_send()

            @pl.when(is_inner)
            def _():
                for i in range(2):
                    x_forward(0, i, j).wait_send()

        @pl.when((k == 1) & gathers)
        def _():
            @pl.loop(1, columns)
            def _(turn):
                wq_copy(turn).wait_send()

    pl.run_scoped(
        attention_back,
        pltpu.VMEM((TOK, TOK), bf16), pltpu.VMEM((CLUSTER, TOK), bf16), pltpu.VMEM((HEAD_DIM, TOK), bf16), pltpu.VMEM((GROUP, TOK), bf16),
        pltpu.VMEM((3 * GROUP, TOK), bf16),
    )


def layer_call(columns, reducers, tail, *arrays):
    vmem = pl.BlockSpec(memory_space=pltpu.VMEM)
    smem = pl.BlockSpec(memory_space=pltpu.SMEM)
    anyspec = pl.BlockSpec(memory_space=pl.ANY)
    dma = pltpu.SemaphoreType.DMA
    rows = 2 * D + tail
    piece, spiece = D // reducers, tail // 2 // reducers
    turns = columns - 1
    wide = 16 * reducers * -(-(3 * GROUP + 16) // (16 * reducers))
    far = columns > 4
    low = lambda *shape: pltpu.VMEM(shape, bf16)
    full = lambda *shape: pltpu.VMEM(shape, f32)
    out = lambda *shape: jax.ShapeDtypeStruct(shape, bf16)
    terms, sterms = (4, turns, piece, D), (turns, 4, spiece, D)
    if columns == 4:
        terms, sterms = (4, 6, piece // 2, D), (6, 4, spiece // 2, D)
    return pl.pallas_call(
        functools.partial(layer, columns, reducers, tail, far),
        out_shape=[out(QUARTER, D), out(QUARTER, D), out(D, D), out(D, D), out(tail, D), out(wide, D)]
        + ([out(*terms), out(*sterms)] if far else []),
        in_specs=[anyspec, vmem, smem] + [vmem] * 3 + [anyspec] * 4 + [vmem],
        out_specs=[anyspec] * 5 + [vmem] + ([anyspec] * 2 if far else []),
        scratch_shapes=([low(piece, D), low(spiece, D)] if far else [low(*terms), low(*sterms)])
        + [
            low(4, rows, D), low(TOK, D), low(3, AUG, TOK), full(3, BLOCKS, CLUSTER, CLUSTER), low(3 * GROUP, D), low(16, TOK),
            full(8, TOK), full(8, 640), low(D, QUARTER), low(QUARTER, D), full(4, 8, D),
            full(QUARTER, D), full(QUARTER, D), low(QUARTER, D), low(4, GROUP, QUARTER), low(GROUP, TOK), low(QUARTER, D), low(QUARTER, D),
            low(4, D, D), low(4, tail // 2, D), low(3, piece, D), low(3, spiece, D),
            low(2, QUARTER, D), low(QUARTER, D), low(turns, wide // reducers, D), low(wide // reducers, D), low(piece, D), low(spiece, D),
            low(16, TOK), low(3 * GROUP, D), full(8, 640), full(8, D),
            dma((8,)), dma((CHUNKS,)), dma((4, CHUNKS)), dma((2, CHUNKS)), dma((4, CHUNKS)), dma((2,)), dma((columns,)), dma((4,)),
            dma((2,)), dma((2,)), dma((3,)), dma((3,)),
            dma((2, 3)), dma((2, 3)), dma((2, 3, max(turns, 4))), dma((2, 3, 5)), dma((2, 3)), dma((2, 3)), dma((3, 4)), dma((3, 4)),
            dma((4, 3)), dma((4, 3)), dma((2,)),
            dma((5,)), dma((5,)), dma((5, max(turns, 6))), dma((5, max(turns, 6))), dma((2, 3)), dma((2, 3)), dma((2, turns)), dma((2, reducers)),
            dma((2,)), dma((2,)), dma((2,)), dma((2,)), dma((CHUNKS,)), dma((CHUNKS,)), dma((CHUNKS,)), dma((CHUNKS,)),
            dma((turns,)), dma((turns,)), dma((1,)), dma((1,)), dma((turns,)), dma((reducers,)), dma((1,)), dma((1,)),
        ],
        compiler_params=pltpu.CompilerParams(collective_id=0, has_side_effects=True, vmem_limit_bytes=63 * 2**20),
    )(*arrays)


def shards(
    layer_input, clusters, document_lengths, query_weight, key_weight, value_weight, query_bias, value_bias, output_weight,
    output_bias, first_gain, first_shift, inner_weight, inner_bias, outer_weight, outer_bias, second_gain, second_shift, cotangent,
):
    columns = lax.axis_size("seq") // 2
    reducers = min(columns, 16)
    tail = 32 * reducers * -(-(GROUP + 16) // (32 * reducers))
    vectors = jnp.concatenate(
        [output_bias, first_gain, first_shift, outer_bias, second_gain, second_shift, inner_bias]
        + [jnp.zeros((GROUP,), f32), query_bias, value_bias, jnp.zeros((64,), f32)]
    ).reshape(1, -1)
    lo, dx, fin_inner, fin_outer, fin_tail, dw, *_ = layer_call(
        columns, reducers, tail, layer_input, clusters.T, document_lengths, query_weight.T, key_weight.T, value_weight.T,
        inner_weight, outer_weight, output_weight, cotangent, vectors,
    )
    turned = lambda i: dw[GROUP * i : GROUP * (i + 1)].astype(f32).T
    bias_row = dw[3 * GROUP].astype(f32)
    sums = fin_tail[GROUP : GROUP + 16].astype(f32)
    return (
        lo,
        dx.astype(f32),
        turned(1),
        turned(0),
        turned(2),
        bias_row[GROUP : 2 * GROUP],
        bias_row[2 * GROUP : 3 * GROUP],
        fin_tail[:GROUP].astype(f32),
        sums[5],
        sums[3],
        sums[4],
        fin_inner.astype(f32),
        sums[6],
        fin_outer.astype(f32),
        sums[2],
        sums[0],
        sums[1],
    )


def solution(mesh):
    rows, cols = P(("seq", "tp"), None), P(None, "tp")
    return jax.shard_map(
        shards,
        mesh=mesh,
        in_specs=(
            rows, P("seq", "tp"), P("seq", None), cols, cols, cols, P("tp"), P("tp"), P("tp", None), P(), P(), P(),
            cols, P("tp"), P("tp", None), P(), P(), P(), rows,
        ),
        out_specs=(
            rows, rows, cols, cols, cols, P("tp"), P("tp"), P("tp", None), P(), P(), P(), cols, P("tp"), P("tp", None), P(), P(), P(),
        ),
        check_vma=False,
    )
```
